32 devices in a mesh: tm: 8 (over y, x, core), height: 4 (over z).
Axes of the slice: x: 2, y: 2, z: 4, core: 2. Of those that a mesh axis runs over, the one named last changes fastest.
Arguments:
- tokens: bfloat16 [16, 16, 80, 3072], P('tm', 'height'), may hold values from -6 to 6
- mod_scale: float32 [3072], replicated, may hold values from -3 to 3
- mod_shift: float32 [3072], replicated, may hold values from -3 to 3
- w_qkv: bfloat16 [3072, 4608], P(('tm', 'height')), may hold values from -0.109375 to 0.109375
- q_gain: float32 [128], replicated, may hold values from 0.25 to 1.75
- k_gain: float32 [128], replicated, may hold values from 0.25 to 1.75
- window: int32 [12, 3], replicated, may hold values from 0 to 2, as said below
- valid: int32 [16, 16, 80], replicated, may hold values from 0 to 1, as said below
Outputs:
- attended: bfloat16 [16, 16, 80, 1536], P('tm', 'height')
The draws below stay inside these ranges and needn't reach their ends.
Inputs may be any that keep to these rules, and one draw needn't show every extreme that they name: `window`: column 0 is at most 1, column 1 at most 1, column 2 at most 2; some head has all three at these most values. `valid`: the last frames, rows and columns of the grid may be padding with 0; scattered tokens elsewhere are 0 too.
All inputs are finite; a program needn't handle non-finite values.
Results may differ from the reference program's by a relative error of at most 0.0055.
Values may be sent and summed in bfloat16 or wider, within the bound.
No kernel may reach another device: no remote copies, remote signals or barrier semaphores. Data moves between devices by JAX's collectives and lax.ppermute only.
A program may use at most 128 MiB of HBM per device.

```python
import jax
import jax.numpy as jnp
from jax import lax

D = 3072
HDIM = 128
HEADS = 12
TT = 1
TH = 2
TW = 8
WT = 1
WH = 1
WW = 2
FH = 4
W = 80
NT = 16
NH = 16


def draw_window(key, part):
    keys = jax.random.split(jax.random.fold_in(key, 11), 4)
    frames = jax.random.randint(keys[0], (HEADS,), 0, WT + 1)
    rows = jax.random.randint(keys[1], (HEADS,), 0, WH + 1)
    columns = jax.random.randint(keys[2], (HEADS,), 0, WW + 1)
    widest = jax.random.randint(keys[3], (), 0, HEADS)
    chosen = jnp.arange(HEADS) == widest
    frames = jnp.where(chosen, WT, frames)
    rows = jnp.where(chosen, WH, rows)
    columns = jnp.where(chosen, WW, columns)
    return jnp.stack([frames, rows, columns], axis=1).astype(jnp.int32)


def draw_valid(key, part):
    keys = jax.random.split(jax.random.fold_in(key, 23), 4)
    pad_frames = jax.random.randint(keys[0], (), 0, TT + 1)
    pad_rows = jax.random.randint(keys[1], (), 0, TH + 1)
    pad_columns = jax.random.randint(keys[2], (), 0, TW)
    scattered = jax.random.randint(keys[3], (NT, NH, W), 0, 16) != 0
    frame_ok = (jnp.arange(NT) < NT - pad_frames)[:, None, None]
    row_ok = (jnp.arange(NH) < NH - pad_rows)[None, :, None]
    column_ok = (jnp.arange(W) < W - pad_columns)[None, None, :]
    return (scattered & frame_ok & row_ok & column_ok).astype(jnp.int32)


def block_scale(key, shape, cuts, low, high):
    loudness, own = 1.0, jax.random.fold_in(key, 6)
    for position, shards_of in cuts:
        steps = jnp.exp(jax.random.uniform(jax.random.fold_in(own, position), (shards_of,), jnp.float32, low / len(cuts), high / len(cuts)))
        loudness = loudness * jnp.repeat(steps, shape[position] // shards_of).reshape([-1 if axis == position else 1 for axis in range(len(shape))])
    return loudness


def normal_values(stream_key, dims, scale, most, shards=(), kind=jnp.bfloat16):
    drawn = scale * jax.random.normal(stream_key, dims, jnp.float32)
    if shards:
        drawn = drawn * block_scale(stream_key, dims, shards, -0.22, 0.18)
    return jnp.clip(drawn, -most, most).astype(kind)


def setup_inputs(seed: int = 0) -> dict:
    seeds = jax.random.split(jax.random.key(seed), 9)
    tokens = normal_values(seeds[0], (NT, NH, W, D), 1.0, 6.0, ((0, 8), (1, 4)))
    mod_scale = normal_values(seeds[1], (D,), 0.5, 3.0, (), jnp.float32)
    mod_shift = normal_values(seeds[2], (D,), 0.5, 3.0, (), jnp.float32)
    w_qkv = normal_values(seeds[3], (D, 3 * HEADS * HDIM), D ** -0.5, 0.109375, ((0, 32),))
    q_gain = jnp.clip(1.0 + 0.15 * jax.random.normal(seeds[4], (HDIM,), jnp.float32), 0.25, 1.75)
    k_gain = jnp.clip(1.0 + 0.15 * jax.random.normal(seeds[5], (HDIM,), jnp.float32), 0.25, 1.75)
    window = draw_window(jax.random.fold_in(seeds[8], 71), 0)
    valid = draw_valid(jax.random.fold_in(seeds[8], 71), 0)
    return dict(tokens=tokens, mod_scale=mod_scale, mod_shift=mod_shift, w_qkv=w_qkv, q_gain=q_gain, k_gain=k_gain, window=window, valid=valid)


EPS = 1e-06

def modulate(tokens, mod_scale, mod_shift):
    values = tokens.astype(jnp.float32)
    mean = lax.optimization_barrier(jnp.mean(values, axis=-1, keepdims=True))
    centred = values - mean
    variance = lax.optimization_barrier(jnp.mean(centred * centred, axis=-1, keepdims=True))
    normed = centred * lax.rsqrt(variance + EPS)
    return (normed * (1.0 + mod_scale) + mod_shift).astype(jnp.bfloat16)

def head_norm(values, gain):
    power = lax.optimization_barrier(jnp.mean(values * values, axis=-1, keepdims=True))
    return (values * lax.rsqrt(power + EPS) * gain).astype(jnp.bfloat16)

def project(flat, mod_scale, mod_shift, w_qkv, q_gain, k_gain):
    count = flat.shape[0]
    modulated = modulate(flat, mod_scale, mod_shift)
    qkv = jnp.dot(modulated, w_qkv, preferred_element_type=jnp.float32)
    inner = qkv.shape[1] // 3
    query = head_norm(qkv[:, :inner].reshape(count, HEADS, HDIM), q_gain)
    key = head_norm(qkv[:, inner:2 * inner].reshape(count, HEADS, HDIM), k_gain)
    value = qkv[:, 2 * inner:].reshape(count, HEADS, HDIM).astype(jnp.bfloat16)
    return (query, key, value)

def tile_coords(frames, rows, width):
    shape = (frames.shape[0], rows.shape[0], width)
    columns = jnp.arange(width, dtype=jnp.int32)
    frame_tiles = jnp.broadcast_to((frames // TT)[:, None, None], shape).reshape(-1)
    row_tiles = jnp.broadcast_to((rows // TH)[None, :, None], shape).reshape(-1)
    column_tiles = jnp.broadcast_to((columns // TW)[None, None, :], shape).reshape(-1)
    return (frame_tiles, row_tiles, column_tiles)

def distances(query_coords, key_coords):
    return tuple((jnp.abs(qa[:, None] - ka[None, :]) for qa, ka in zip(query_coords, key_coords)))

def reference(tokens, mod_scale, mod_shift, w_qkv, q_gain, k_gain, window, valid):

    def per_frame(frame_tokens):
        query, key, value = project(frame_tokens.reshape(NH * W, D), mod_scale, mod_shift, w_qkv, q_gain, k_gain)
        shape = (NH, W, HEADS, HDIM)
        return (query.reshape(shape), key.reshape(shape), value.reshape(shape))
    query_grid, key_grid, value_grid = lax.map(per_frame, tokens)
    padding = ((TT, TT), (TH, TH), (0, 0), (0, 0), (0, 0))
    key_pad = jnp.pad(key_grid, padding)
    value_pad = jnp.pad(value_grid, padding)
    valid_pad = jnp.pad(valid, ((TT, TT), (TH, TH), (0, 0)))
    bands = NH // FH
    zero = jnp.int32(0)

    def block(index):
        frame = (index // bands).astype(jnp.int32)
        first_row = (index % bands * FH).astype(jnp.int32)
        query = lax.dynamic_slice(query_grid, (frame, first_row, zero, zero, zero), (1, FH, W, HEADS, HDIM)).reshape(-1, HEADS, HDIM)
        key_size = (1 + 2 * TT, FH + 2 * TH, W, HEADS, HDIM)
        key = lax.dynamic_slice(key_pad, (frame, first_row, zero, zero, zero), key_size).reshape(-1, HEADS, HDIM)
        value = lax.dynamic_slice(value_pad, (frame, first_row, zero, zero, zero), key_size).reshape(-1, HEADS, HDIM)
        key_valid = lax.dynamic_slice(valid_pad, (frame, first_row, zero), (1 + 2 * TT, FH + 2 * TH, W)).reshape(-1) > 0
        query_valid = lax.dynamic_slice(valid, (frame, first_row, zero), (1, FH, W)).reshape(-1) > 0
        query_coords = tile_coords(frame + jnp.arange(1, dtype=jnp.int32), first_row + jnp.arange(FH, dtype=jnp.int32), W)
        key_coords = tile_coords(frame - TT + jnp.arange(1 + 2 * TT, dtype=jnp.int32), first_row - TH + jnp.arange(FH + 2 * TH, dtype=jnp.int32), W)
        apart_t, apart_h, apart_w = distances(query_coords, key_coords)
        allowed = (apart_t[None] <= window[:, 0, None, None]) & (apart_h[None] <= window[:, 1, None, None])
        allowed = allowed & (apart_w[None] <= window[:, 2, None, None]) & key_valid[None, None, :]
        scores = jnp.einsum('qhd,khd->hqk', query.astype(jnp.float32), key.astype(jnp.float32)) / jnp.sqrt(jnp.float32(HDIM))
        terms = jnp.where(allowed, jnp.exp(scores), jnp.float32(0.0))
        total = lax.optimization_barrier(jnp.sum(terms, axis=-1, keepdims=True))
        total = jnp.where(query_valid[None, :, None], total, jnp.float32(1.0))
        weights = (terms / total).astype(jnp.bfloat16)
        result = jnp.einsum('hqk,khd->qhd', weights.astype(jnp.float32), value.astype(jnp.float32))
        result = jnp.where(query_valid[:, None, None], result, jnp.float32(0.0)).astype(jnp.bfloat16)
        return result.reshape(FH, W, HEADS * HDIM)
    blocks = lax.map(block, jnp.arange(NT * bands, dtype=jnp.int32))
    return blocks.reshape(NT, NH, W, HEADS * HDIM)
```

```python
import functools

import jax
import jax.numpy as jnp
import numpy as np
from jax import lax
from jax.experimental import pallas as pl
from jax.experimental.pallas import tpu as pltpu
from jax.sharding import Mesh
from jax.sharding import PartitionSpec as P

HDIM = 128
HEADS = 12
TT = 1
TH = 2
TW = 8
CORES = 2
GROUP = 6
EPS = 1e-06
VMEM = 56 * 1024 * 1024


def modulate(tokens, mod_scale, mod_shift):
    values = tokens.astype(jnp.float32)
    mean = jnp.mean(values, axis=-1, keepdims=True)
    centred = values - mean
    variance = jnp.mean(centred * centred, axis=-1, keepdims=True)
    normed = centred * lax.rsqrt(variance + EPS)
    return (normed * (1.0 + mod_scale) + mod_shift).astype(jnp.bfloat16)


def gather_columns(w_qkv, spans):
    part = jnp.concatenate([w_qkv[:, start:stop] for start, stop in spans], axis=1)
    own = lax.all_gather(part, ("chip", "height"), axis=0, tiled=True)
    other = lax.ppermute(own, "core", [(i, CORES - 1 - i) for i in range(CORES)])
    return own, other


def project_body(x_own, x_other, w_own, w_other, gain, out, *, normed):
    total = jnp.dot(x_own[...], w_own[...], preferred_element_type=jnp.float32)
    total += jnp.dot(x_other[...], w_other[...], preferred_element_type=jnp.float32)

    def plain():
        out[0] = total.astype(out.dtype)

    def norm():
        for start in range(0, total.shape[1], HDIM):
            head = total[:, start : start + HDIM]
            power = jnp.mean(head * head, axis=-1, keepdims=True)
            out[0, :, start : start + HDIM] = (head * lax.rsqrt(power + EPS) * gain[...]).astype(out.dtype)

    step = pl.program_id(0)
    if normed is None:
        norm()
    else:
        pl.when(step < normed)(norm)
        pl.when(step >= normed)(plain)


def project(x_own, x_other, w_own, w_other, gain, parts, normed_parts):
    rows, depth = x_own.shape
    columns = w_own.shape[1]
    block = 2 * HDIM
    per_part = columns // parts // block
    steps = columns // block
    normed = None if normed_parts == parts else normed_parts * per_part
    whole = lambda j: (0, 0)
    slab = lambda j: (0, j)
    return pl.pallas_call(
        functools.partial(project_body, normed=normed),
        grid=(steps,),
        in_specs=[
            pl.BlockSpec((rows, depth), whole),
            pl.BlockSpec((rows, depth), whole),
            pl.BlockSpec((depth, block), slab),
            pl.BlockSpec((depth, block), slab),
            pl.BlockSpec((1, HDIM), whole),
        ],
        out_specs=pl.BlockSpec((1, rows, block), lambda j: (j // per_part, 0, j % per_part)),
        out_shape=jax.ShapeDtypeStruct((parts, rows, columns // parts), jnp.bfloat16),
        compiler_params=pltpu.CompilerParams(vmem_limit_bytes=VMEM),
        cost_estimate=pl.CostEstimate(
            flops=4 * rows * depth * columns,
            bytes_accessed=4 * depth * columns + 4 * rows * depth + 2 * rows * columns,
            transcendentals=0,
        ),
    )(x_own, x_other, w_own, w_other, gain.reshape(1, HDIM))


def attend_body(window, query, own, above, below, before, after, valid, *rest, frames, tiles, cell, first):
    out, keys, values, band = rest[-4:]
    group = pl.program_id(0)
    head = first + group
    width = cell // TH
    inner = tiles * cell

    @pl.when(group == 0)
    def _():
        values[:, :, HDIM:] = valid[...]
        q_tile = lax.broadcasted_iota(jnp.int32, (cell, 3 * cell), 0)
        k_tile = lax.broadcasted_iota(jnp.int32, (cell, 3 * cell), 1)
        apart = jnp.abs(lax.rem(q_tile, width) // TW - lax.rem(k_tile, width) // TW)
        for reach in range(3):
            band[reach] = jnp.where(apart <= reach, 1.0, 0.0).astype(band.dtype)

    for which, store in ((0, keys), (1, values)):
        def put(frame, rows, block):
            if which:
                block = block * valid[frame, rows, :]
            store[frame, rows, :HDIM] = block

        for frame in range(frames):
            put(frame + 1, pl.ds(0, cell), above[which, frame])
            put(frame + 1, pl.ds(cell, inner), own[which, frame])
            put(frame + 1, pl.ds(cell + inner, cell), below[which, frame])
        put(0, pl.ds(0, inner + 2 * cell), before[which])
        put(frames + 1, pl.ds(0, inner + 2 * cell), after[which])

    scale = np.float32(np.log2(np.e) / np.sqrt(HDIM))
    reach_t, reach_h, reach_w = window[head, 0], window[head, 1], window[head, 2]

    def attend(over_t, over_h):
        seen = (3 if over_h else 1) * cell
        mask = band[reach_w, :, :seen]
        for frame in range(frames):
            for tile in range(tiles):
                start = (frame * tiles + tile) * cell
                rows = pl.ds((tile + (0 if over_h else 1)) * cell, seen)
                mine = query[pl.ds(start, cell), :]
                total = None
                for step in (-1, 0, 1) if over_t else (0,):
                    source = frame + 1 + step
                    scores = lax.dot_general(
                        mine,
                        keys[source, rows, :],
                        (((1,), (1,)), ((), ())),
                        preferred_element_type=jnp.float32,
                    )
                    terms = jnp.exp2(scores * scale).astype(jnp.bfloat16) * mask
                    part = jnp.dot(terms, values[source, rows, :], preferred_element_type=jnp.float32)
                    total = part if total is None else total + part
                here = valid[frame + 1, pl.ds((tile + 1) * cell, cell), :] > 0
                weight = jnp.where(here, total[:, HDIM:], 1.0)
                result = jnp.where(here, total[:, :HDIM] / weight, 0.0)
                out[pl.ds(start, cell), :] = result.astype(out.dtype)

    for over_t in (False, True):
        for over_h in (False, True):
            pl.when(((reach_t > 0) == over_t) & ((reach_h > 0) == over_h))(
                functools.partial(attend, over_t, over_h)
            )


def attend(window, query, own, above, below, before, after, valid, first, total_heads, onto=None):
    _, frames, inner, columns = own.shape
    heads = columns // HDIM
    cell = above.shape[2]
    tiles = inner // cell
    rows = query.shape[0]
    span = inner + 2 * cell
    specs = [
        pl.BlockSpec((rows, HDIM), lambda h, w: (0, h)),
        pl.BlockSpec((2, frames, inner, HDIM), lambda h, w: (0, 0, 0, h)),
        pl.BlockSpec((2, frames, cell, HDIM), lambda h, w: (0, 0, 0, h)),
        pl.BlockSpec((2, frames, cell, HDIM), lambda h, w: (0, 0, 0, h)),
        pl.BlockSpec((2, span, HDIM), lambda h, w: (0, 0, h)),
        pl.BlockSpec((2, span, HDIM), lambda h, w: (0, 0, h)),
        pl.BlockSpec((frames + 2, span, HDIM), lambda h, w: (0, 0, 0)),
    ]
    operands = [window, query, own, above, below, before, after, valid]
    aliases = {}
    if onto is not None:
        specs.append(pl.BlockSpec(memory_space=pl.ANY))
        operands.append(onto)
        aliases = {len(operands) - 1: 0}
    return pl.pallas_call(
        functools.partial(attend_body, frames=frames, tiles=tiles, cell=cell, first=first),
        grid_spec=pltpu.PrefetchScalarGridSpec(
            num_scalar_prefetch=1,
            grid=(heads,),
            in_specs=specs,
            out_specs=pl.BlockSpec((rows, HDIM), lambda h, w: (0, first + h)),
            scratch_shapes=[
                pltpu.VMEM((frames + 2, span, HDIM), jnp.bfloat16),
                pltpu.VMEM((frames + 2, span, 2 * HDIM), jnp.bfloat16),
                pltpu.VMEM((3, cell, 3 * cell), jnp.bfloat16),
            ],
        ),
        out_shape=jax.ShapeDtypeStruct((rows, total_heads * HDIM), jnp.bfloat16),
        input_output_aliases=aliases,
        compiler_params=pltpu.CompilerParams(vmem_limit_bytes=VMEM),
        cost_estimate=pl.CostEstimate(
            flops=heads * rows * 9 * cell * HDIM * 6,
            bytes_accessed=2 * columns * (2 * rows + 2 * (frames + 2) * span),
            transcendentals=heads * rows * 9 * cell,
        ),
    )(*operands)


def halo(kv, frames, rows, width):
    parts, _, columns = kv.shape
    cell = TH * width
    grid = kv.reshape(parts, frames, rows * width, columns)
    up = lax.axis_size("height")
    above = lax.ppermute(grid[:, :, rows * width - cell :], "height", [(i, i + 1) for i in range(up - 1)])
    below = lax.ppermute(grid[:, :, :cell], "height", [(i + 1, i) for i in range(up - 1)])
    along = ("chip", "core")
    count = lax.axis_size("chip") * lax.axis_size("core")
    last = jnp.concatenate([above[:, -1], grid[:, -1], below[:, -1]], axis=1)
    head = jnp.concatenate([above[:, 0], grid[:, 0], below[:, 0]], axis=1)
    before = lax.ppermute(last, along, [(i, i + 1) for i in range(count - 1)])
    after = lax.ppermute(head, along, [(i + 1, i) for i in range(count - 1)])
    return grid, above, below, before, after


def per_device(tokens, mod_scale, mod_shift, w_qkv, q_gain, k_gain, window, valid):
    frames, rows, width, features = tokens.shape
    count = frames * rows * width
    inner = w_qkv.shape[1] // 3
    chips = lax.axis_size("chip")
    core = lax.axis_index("core")

    step = GROUP * HDIM
    starts = range(0, inner, step)
    kv_weights = [
        gather_columns(w_qkv, [(inner + s, inner + s + step), (2 * inner + s, 2 * inner + s + step)])
        for s in starts
    ]
    q_weights = [gather_columns(w_qkv, [(s, s + step)]) for s in starts]

    modulated = modulate(tokens.reshape(count, features), mod_scale, mod_shift)
    slabs = modulated.reshape(count, chips, CORES, features // chips // CORES)
    x_own = lax.dynamic_index_in_dim(slabs, core, 2, False).reshape(count, features // CORES)
    x_other = lax.dynamic_index_in_dim(slabs, CORES - 1 - core, 2, False).reshape(count, features // CORES)

    valid_pad = jnp.pad(valid, ((TT, TT), (TH, TH), (0, 0)))
    first_frame = (lax.axis_index("chip") * CORES + core) * frames
    first_row = lax.axis_index("height") * rows
    near = lax.dynamic_slice(
        valid_pad, (first_frame, first_row, jnp.int32(0)), (frames + 2 * TT, rows + 2 * TH, width)
    )
    near = jnp.broadcast_to(
        (near > 0).astype(jnp.bfloat16).reshape(frames + 2 * TT, -1, 1),
        (frames + 2 * TT, (rows + 2 * TH) * width, HDIM),
    )

    cells = [
        halo(project(x_own, x_other, own, other, k_gain, 2, 1), frames, rows, width)
        for own, other in kv_weights
    ]
    queries = [project(x_own, x_other, own, other, q_gain, 1, 1)[0] for own, other in q_weights]
    out = None
    for index, (query, parts) in enumerate(zip(queries, cells)):
        out = attend(window, query, *parts, near, index * GROUP, HEADS, out)
    return out.reshape(frames, rows, width, inner)


def solution(mesh):
    split = Mesh(
        mesh.devices.reshape(mesh.shape["tm"] // CORES, CORES, mesh.shape["height"]),
        ("chip", "core", "height"),
    )
    in_specs = (
        P(("chip", "core"), "height", None, None),
        P(),
        P(),
        P(("chip", "core", "height"), None),
        P(),
        P(),
        P(),
        P(),
    )
    out_specs = P(("chip", "core"), "height", None, None)
    return jax.shard_map(
        per_device, mesh=split, in_specs=in_specs, out_specs=out_specs, check_vma=False
    )
```

```python
import functools

import jax
import jax.numpy as jnp
import numpy as np
from jax import lax
from jax.experimental import pallas as pl
from jax.experimental.pallas import tpu as pltpu
from jax.sharding import Mesh
from jax.sharding import PartitionSpec as P

HDIM = 128
HEADS = 12
TT = 1
TH = 2
TW = 8
CORES = 2
MATES = 4
OWN_HEADS = HEADS // MATES
SPAN = OWN_HEADS * HDIM
EPS = 1e-06
VMEM = 56 * 1024 * 1024
TEAM = ("pair", "core")


def swap(x, axis, flip):
    names = axis if isinstance(axis, tuple) else (axis,)
    count = int(np.prod([lax.axis_size(name) for name in names]))
    return lax.ppermute(x, axis, [(i, i ^ flip) for i in range(count)])


def swap_neighbours(x, axis, odd):
    count = lax.axis_size(axis)
    pairs = [(i, i + 1) for i in range(odd, count - 1, 2)]
    return lax.ppermute(x, axis, pairs + [(j, i) for i, j in pairs])


def modulate_body(tokens, scale, shift, out):
    values = tokens[...].astype(jnp.float32)
    centred = values - jnp.mean(values, axis=-1, keepdims=True)
    variance = jnp.mean(centred * centred, axis=-1, keepdims=True)
    normed = centred * lax.rsqrt(variance + EPS)
    out[...] = (normed * (1.0 + scale[...]) + shift[...]).astype(out.dtype)


def modulate(tokens, scale, shift):
    count, features = tokens.shape
    block = 128
    row = pl.BlockSpec((block, features), lambda i: (i, 0))
    whole = pl.BlockSpec((1, features), lambda i: (0, 0))
    return pl.pallas_call(
        modulate_body,
        grid=(count // block,),
        in_specs=[row, whole, whole],
        out_specs=row,
        out_shape=jax.ShapeDtypeStruct(tokens.shape, jnp.bfloat16),
        compiler_params=pltpu.CompilerParams(vmem_limit_bytes=VMEM),
        cost_estimate=pl.CostEstimate(
            flops=12 * count * features, bytes_accessed=4 * count * features, transcendentals=0
        ),
    )(tokens, scale.reshape(1, features), shift.reshape(1, features))


def project_body(places, order, *rest, arrays, steps, parts, normed):
    first, second = rest[:2]
    blocks = rest[2 : 2 + arrays]
    gain = rest[2 + arrays]
    out, weights, sems = rest[-3:]
    step = pl.program_id(0)
    pieces, depth, columns = blocks[0].shape

    @pl.when(step == 0)
    def _():
        copies = []
        for a in range(arrays):
            for p in range(pieces):
                row = pl.multiple_of(places[a * pieces + p] * depth, depth)
                copy = pltpu.make_async_copy(
                    blocks[a].at[p], weights.at[pl.ds(row, depth), :], sems.at[a * pieces + p]
                )
                copy.start()
                copies.append(copy)
        for copy in copies:
            copy.wait()

    def run(rows):
        wide = 2 * HDIM
        for start in range(0, columns, wide):
            stop = min(start + wide, columns)
            total = jnp.dot(rows[...], weights[:, start:stop], preferred_element_type=jnp.float32)
            for column in range(start, stop, HDIM):
                head = total[:, column - start : column - start + HDIM]
                part, offset = divmod(column, SPAN)
                if part < normed:
                    power = jnp.mean(head * head, axis=-1, keepdims=True)
                    head = head * lax.rsqrt(power + EPS) * gain[...]
                out[part, 0, :, offset : offset + HDIM] = head.astype(out.dtype)

    pl.when(step < steps)(lambda: run(first))
    pl.when(step >= steps)(lambda: run(second))


def project(first, second, order, blocks, places, gain, parts, normed, members, onto=None):
    rows, depth = first.shape
    pieces, shard, columns = blocks[0].shape
    arrays = len(blocks)
    block = rows // 2
    steps = rows // block
    specs = [
        pl.BlockSpec((block, depth), lambda i, p, o: (jnp.minimum(i, steps - 1), 0)),
        pl.BlockSpec((block, depth), lambda i, p, o: (jnp.maximum(i - steps, 0), 0)),
    ]
    specs += [pl.BlockSpec(memory_space=pl.ANY)] * arrays
    specs += [pl.BlockSpec((1, HDIM), lambda i, p, o: (0, 0))]
    operands = [places, order, first, second, *blocks, gain.reshape(1, HDIM)]
    aliases = {}
    if onto is not None:
        specs.append(pl.BlockSpec(memory_space=pl.ANY))
        operands.append(onto)
        aliases = {len(operands) - 1: 0}
    return pl.pallas_call(
        functools.partial(project_body, arrays=arrays, steps=steps, parts=parts, normed=normed),
        grid_spec=pltpu.PrefetchScalarGridSpec(
            num_scalar_prefetch=2,
            grid=(2 * steps,),
            in_specs=specs,
            out_specs=pl.BlockSpec(
                (parts, 1, block, SPAN), lambda i, p, o: (0, o[i // steps], i % steps, 0)
            ),
            scratch_shapes=[
                pltpu.VMEM((depth, columns), jnp.bfloat16),
                pltpu.SemaphoreType.DMA((arrays * pieces,)),
            ],
        ),
        out_shape=jax.ShapeDtypeStruct((parts, members, rows, SPAN), jnp.bfloat16),
        input_output_aliases=aliases,
        compiler_params=pltpu.CompilerParams(vmem_limit_bytes=VMEM),
        cost_estimate=pl.CostEstimate(
            flops=4 * rows * depth * columns,
            bytes_accessed=2 * depth * columns + 4 * rows * depth + 4 * rows * columns,
            transcendentals=0,
        ),
    )(*operands)


def attend_body(meta, *rest, near, chip_frames, frames, cell, inner, sides):
    query = rest[0]
    chips = (rest[1:4], rest[4:7])
    borders = [rest[7 + 2 * s : 9 + 2 * s] for s in range(sides)]
    valid = rest[7 + 2 * sides]
    out, keys, values, band = rest[-4:]
    head_step, frame = pl.program_id(0), pl.program_id(1)
    member, pair, z_odd, r_odd = (meta[3 * HEADS + i] for i in range(4))
    head = member * OWN_HEADS + head_step
    width = cell // TH

    @pl.when((head_step == 0) & (frame == 0))
    def _():
        values[:, :, HDIM:] = valid[...]
        q_tile = lax.broadcasted_iota(jnp.int32, (cell, 3 * cell), 0)
        k_tile = lax.broadcasted_iota(jnp.int32, (cell, 3 * cell), 1)
        apart = jnp.abs(lax.rem(q_tile, width) // TW - lax.rem(k_tile, width) // TW)
        for reach in range(3):
            band[reach] = jnp.where(apart <= reach, 1.0, 0.0).astype(band.dtype)
        if sides < 2:
            empty = jnp.where(r_odd == 1, frames + 1, 0)
            keys[empty] = jnp.zeros(keys.shape[1:], keys.dtype)
            values[empty, :, :HDIM] = jnp.zeros((keys.shape[1], HDIM), values.dtype)

    @pl.when(frame == 0)
    def _():
        even_rows = pl.multiple_of(jnp.where(z_odd == 1, 0, cell + inner), cell)
        odd_rows = pl.multiple_of(jnp.where(z_odd == 1, cell + inner, 0), cell)

        def put(place, start, length, key, value):
            rows = pl.ds(start, length)
            keys[place, rows, :] = key
            values[place, rows, :HDIM] = value * valid[place, rows, :]

        for which, (own, even, odd) in enumerate(chips):
            base = 1 + chip_frames * (pair if which == 0 else 1 - pair)
            for index in range(chip_frames):
                put(base + index, cell, inner, own[0, index], own[1, index])
                put(base + index, even_rows, cell, even[0, index], even[1, index])
                put(base + index, odd_rows, cell, odd[0, index], odd[1, index])
        for side, (own, ends) in enumerate(borders):
            place = jnp.where(r_odd == 1 - side, 0, frames + 1) if side == 0 else jnp.where(r_odd == 1, frames + 1, 0)
            put(place, cell, inner, own[0], own[1])
            put(place, even_rows, cell, ends[0, 0], ends[0, 1])
            put(place, odd_rows, cell, ends[1, 0], ends[1, 1])

    scale = np.float32(np.log2(np.e) / np.sqrt(HDIM))
    reach_t, reach_h, reach_w = (meta[3 * head + i] for i in range(3))

    def attend(over_t, over_h):
        seen = (3 if over_h else 1) * cell
        mask = band[reach_w, :, :seen]
        for tile in range(inner // cell):
            rows = pl.ds((tile + (0 if over_h else 1)) * cell, seen)
            mine = query[0, 0, 0, pl.ds(tile * cell, cell), :]
            total = None
            for step in (0, 1, 2) if over_t else (1,):
                scores = lax.dot_general(
                    mine,
                    keys[frame + step, rows, :],
                    (((1,), (1,)), ((), ())),
                    preferred_element_type=jnp.float32,
                )
                terms = jnp.exp2(scores * scale).astype(jnp.bfloat16) * mask
                part = jnp.dot(terms, values[frame + step, rows, :], preferred_element_type=jnp.float32)
                total = part if total is None else total + part
            here = valid[frame + 1, pl.ds((tile + 1) * cell, cell), :] > 0
            weight = jnp.where(here, total[:, HDIM:], 1.0)
            result = jnp.where(here, total[:, :HDIM] / weight, 0.0)
            out[0, 0, pl.ds(tile * cell, cell), :] = result.astype(out.dtype)

    for over_t in (False, True):
        for over_h in (False, True):
            pl.when(((reach_t > 0) == over_t) & ((reach_h > 0) == over_h))(
                functools.partial(attend, over_t, over_h)
            )


def attend(meta, query, chips, borders, valid, near):
    _, chip_frames, inner, _ = chips[0][0].shape
    frames = 2 * chip_frames
    cell = chips[0][1].shape[2]
    span = inner + 2 * cell
    head = lambda h, f, m: (0, 0, 0, h)
    specs = [
        pl.BlockSpec((1, 1, 1, inner, HDIM), lambda h, f, m: (0, f // near, f % near, 0, h)),
    ]
    operands = [query]
    for own, even, odd in chips:
        for part in (own, even, odd):
            specs.append(pl.BlockSpec((*part.shape[:-1], HDIM), head))
            operands.append(part)
    for own, ends in borders:
        specs.append(pl.BlockSpec((*own.shape[:-1], HDIM), lambda h, f, m: (0, 0, h)))
        specs.append(pl.BlockSpec((*ends.shape[:-1], HDIM), head))
        operands += [own, ends]
    specs.append(pl.BlockSpec(valid.shape, lambda h, f, m: (0, 0, 0)))
    operands.append(valid)
    flips = lambda f, m: (f // near) ^ m[3 * HEADS]
    return pl.pallas_call(
        functools.partial(
            attend_body,
            near=near,
            chip_frames=chip_frames,
            frames=frames,
            cell=cell,
            inner=inner,
            sides=len(borders),
        ),
        grid_spec=pltpu.PrefetchScalarGridSpec(
            num_scalar_prefetch=1,
            grid=(OWN_HEADS, frames),
            in_specs=specs,
            out_specs=pl.BlockSpec((1, 1, inner, HDIM), lambda h, f, m: (flips(f, m), f % near, 0, h)),
            scratch_shapes=[
                pltpu.VMEM((frames + 2, span, HDIM), jnp.bfloat16),
                pltpu.VMEM((frames + 2, span, 2 * HDIM), jnp.bfloat16),
                pltpu.VMEM((3, cell, 3 * cell), jnp.bfloat16),
            ],
        ),
        out_shape=jax.ShapeDtypeStruct((MATES, near, inner, SPAN), jnp.bfloat16),
        compiler_params=pltpu.CompilerParams(vmem_limit_bytes=VMEM),
        cost_estimate=pl.CostEstimate(
            flops=OWN_HEADS * frames * inner * 9 * cell * HDIM * 6,
            bytes_accessed=2 * OWN_HEADS * HDIM * frames * (2 * inner + 2 * span),
            transcendentals=OWN_HEADS * frames * inner * 9 * cell,
        ),
    )(meta, *operands)


def collect_body(member, *rest):
    out = rest[-1]
    for flip, piece in enumerate(rest[:-1]):
        column = pl.multiple_of((member[0] ^ flip) * SPAN, SPAN)
        out[:, pl.ds(column, SPAN)] = piece[...]


def collect(member, pieces):
    rows = pieces[0].shape[0]
    whole = pl.BlockSpec((rows, SPAN), lambda i, m: (0, 0))
    return pl.pallas_call(
        collect_body,
        grid_spec=pltpu.PrefetchScalarGridSpec(
            num_scalar_prefetch=1,
            grid=(1,),
            in_specs=[whole] * MATES,
            out_specs=pl.BlockSpec((rows, HEADS * HDIM), lambda i, m: (0, 0)),
        ),
        out_shape=jax.ShapeDtypeStruct((rows, HEADS * HDIM), jnp.bfloat16),
        compiler_params=pltpu.CompilerParams(vmem_limit_bytes=VMEM),
    )(member.reshape(1), *pieces)


def gather_blocks(pieces):
    lines = [pieces] + [swap(pieces, "height", d) for d in range(1, lax.axis_size("height"))]
    found = list(lines)
    for e in range(1, lax.axis_size("rest")):
        found += [swap(line, "rest", e) for line in lines]
    return found


def aligned(blocks, places):
    shard = blocks[0].shape[1]
    if shard % 16 == 0:
        return blocks, places
    rows = jnp.concatenate(blocks, axis=0)
    ordered = jnp.zeros_like(rows).at[places].set(rows)
    return [ordered.reshape(1, -1, rows.shape[-1])], jnp.zeros((1,), jnp.int32)


def per_device(tokens, mod_scale, mod_shift, w_qkv, q_gain, k_gain, window, valid):
    frames, rows, width, features = tokens.shape
    count = frames * rows * width
    inner = rows * width
    cell = TH * width
    model = w_qkv.shape[1] // 3
    rest, pair, core, height = (lax.axis_index(a) for a in ("rest", "pair", "core", "height"))
    member = pair * CORES + core
    high = lax.axis_size("height")
    many = lax.axis_size("rest")

    def columns_of(mate):
        return jnp.concatenate(
            [lax.dynamic_slice_in_dim(w_qkv, s * model + mate * SPAN, SPAN, axis=1) for s in range(3)], axis=1
        )

    shares = [columns_of(member)] + [swap(columns_of(member ^ flip), TEAM, flip) for flip in range(1, MATES)]
    stacked = jnp.stack(shares)
    kv_blocks = gather_blocks(stacked[:, :, SPAN:])
    q_blocks = gather_blocks(stacked[:, :, :SPAN])
    places = jnp.stack(
        [
            ((rest ^ e) * MATES + (member ^ j)) * high + (height ^ d)
            for e in range(many)
            for d in range(high)
            for j in range(MATES)
        ]
    ).astype(jnp.int32)
    kv_blocks, kv_places = aligned(kv_blocks, places)
    q_blocks, q_places = aligned(q_blocks, places)

    mine = modulate(tokens.reshape(count, features), mod_scale, mod_shift)
    across = swap(mine, "pair", 1)
    beside = swap(mine, "core", 1)
    beyond = swap(across, "core", 1)

    z_odd = height % 2
    r_odd = rest % 2
    orders = jnp.stack([core, 1 - core]).astype(jnp.int32)

    def chip_cells(first, second):
        kv = project(first, second, orders, kv_blocks, kv_places, k_gain, 2, 1, CORES)
        grid = kv.reshape(2, CORES * frames, inner, SPAN)
        low, top = jnp.int32(0), jnp.int32(inner - cell)
        even = swap_neighbours(
            lax.dynamic_slice_in_dim(grid, jnp.where(z_odd == 1, low, top), cell, axis=2), "height", 0
        )
        odd = swap_neighbours(
            lax.dynamic_slice_in_dim(grid, jnp.where(z_odd == 1, top, low), cell, axis=2), "height", 1
        )
        return grid, even, odd

    near_chip = chip_cells(mine, beside)
    far_chip = chip_cells(across, beyond)
    mates = jnp.stack([member ^ j for j in range(MATES)]).astype(jnp.int32)
    query = project(mine, beside, mates[:2], q_blocks, q_places, q_gain, 1, 1, MATES)
    query = project(across, beyond, mates[2:], q_blocks, q_places, q_gain, 1, 1, MATES, query)

    def border(odd):
        last = r_odd == odd
        chosen = jnp.where(last, 1, 0) == pair
        frame = jnp.where(last, CORES * frames - 1, 0)
        own, even, other = (
            jnp.where(
                chosen,
                lax.dynamic_index_in_dim(a, frame, 1, False),
                lax.dynamic_index_in_dim(b, frame, 1, False),
            )
            for a, b in zip(near_chip, far_chip)
        )
        return (
            swap_neighbours(own, "rest", odd),
            swap_neighbours(jnp.stack([even, other]), "rest", odd),
        )

    borders = [border(odd) for odd in range(min(2, many - 1))]

    total_frames = MATES * frames
    valid_pad = jnp.pad(valid, ((TT, TT), (TH, TH), (0, 0)))
    around = lax.dynamic_slice(
        valid_pad,
        (rest * total_frames, height * rows, jnp.int32(0)),
        (total_frames + 2 * TT, rows + 2 * TH, width),
    )
    seen = jnp.broadcast_to(
        (around > 0).astype(jnp.bfloat16).reshape(total_frames + 2 * TT, -1, 1),
        (total_frames + 2 * TT, (rows + 2 * TH) * width, HDIM),
    )
    meta = jnp.concatenate(
        [window.reshape(-1), jnp.stack([member, pair, z_odd, r_odd]).astype(jnp.int32)]
    )
    queries = query.reshape(1, MATES, frames, inner, SPAN)
    attended = attend(meta, queries, (near_chip, far_chip), borders, seen, frames)
    attended = attended.reshape(MATES, count, SPAN)
    pieces = [attended[0]] + [swap(attended[flip], TEAM, flip) for flip in range(1, MATES)]
    return collect(member.astype(jnp.int32), pieces).reshape(frames, rows, width, model)


def solution(mesh):
    split = Mesh(
        mesh.devices.reshape(mesh.shape["tm"] // MATES, MATES // CORES, CORES, mesh.shape["height"]),
        ("rest", "pair", "core", "height"),
    )
    along = ("rest", "pair", "core")
    in_specs = (
        P(along, "height", None, None),
        P(),
        P(),
        P((*along, "height"), None),
        P(),
        P(),
        P(),
        P(),
    )
    out_specs = P(along, "height", None, None)
    return jax.shard_map(
        per_device, mesh=split, in_specs=in_specs, out_specs=out_specs, check_vma=False
    )
```

```python
import functools

import jax
import jax.numpy as jnp
import numpy as np
from jax import lax
from jax.experimental import pallas as pl
from jax.experimental.pallas import tpu as pltpu
from jax.sharding import Mesh
from jax.sharding import PartitionSpec as P

HDIM = 128
HEADS = 12
TT = 1
TH = 2
TW = 8
CORES = 2
MATES = 4
OWN_HEADS = HEADS // MATES
SPAN = OWN_HEADS * HDIM
EPS = 1e-06
VMEM = 56 * 1024 * 1024
TEAM = ("pair", "core")


def swap(x, axis, flip):
    names = axis if isinstance(axis, tuple) else (axis,)
    count = int(np.prod([lax.axis_size(name) for name in names]))
    return lax.ppermute(x, axis, [(i, i ^ flip) for i in range(count)])


def swap_neighbours(x, axis, odd):
    count = lax.axis_size(axis)
    pairs = [(i, i + 1) for i in range(odd, count - 1, 2)]
    return lax.ppermute(x, axis, pairs + [(j, i) for i, j in pairs])


def modulate_body(tokens, scale, shift, out):
    values = tokens[...].astype(jnp.float32)
    centred = values - jnp.mean(values, axis=-1, keepdims=True)
    variance = jnp.mean(centred * centred, axis=-1, keepdims=True)
    normed = centred * lax.rsqrt(variance + EPS)
    out[...] = (normed * (1.0 + scale[...]) + shift[...]).astype(out.dtype)


def modulate(tokens, scale, shift):
    count, features = tokens.shape
    block = count // 2
    row = pl.BlockSpec((block, features), lambda i: (i, 0))
    whole = pl.BlockSpec((1, features), lambda i: (0, 0))
    return pl.pallas_call(
        modulate_body,
        grid=(count // block,),
        in_specs=[row, whole, whole],
        out_specs=row,
        out_shape=jax.ShapeDtypeStruct(tokens.shape, jnp.bfloat16),
        compiler_params=pltpu.CompilerParams(vmem_limit_bytes=VMEM),
        cost_estimate=pl.CostEstimate(
            flops=12 * count * features, bytes_accessed=4 * count * features, transcendentals=0
        ),
    )(tokens, scale.reshape(1, features), shift.reshape(1, features))


def project_body(places, order, grid_frames, *rest, sources, normed):
    xs = rest[:sources]
    blocks, gain, seen, out, rows, weights, row_sems, weight_sems = rest[sources:]
    pieces, depth, columns = blocks.shape
    inner = out.shape[2]
    cell = (seen.shape[1] - inner) // 2

    loads = [pltpu.make_async_copy(x, rows.at[i], row_sems.at[i]) for i, x in enumerate(xs)]
    copies = []
    for p in range(pieces):
        row = pl.multiple_of(places[p] * depth, depth)
        copies.append(pltpu.make_async_copy(blocks.at[p], weights.at[pl.ds(row, depth), :], weight_sems.at[p]))
    loads[0].start()
    for copy in copies:
        copy.start()
    for load in loads[1:]:
        load.start()
    for copy in copies:
        copy.wait()
    wide = 2 * HDIM
    for i in range(sources):
        loads[i].wait()
        for start in range(0, columns, wide):
            stop = min(start + wide, columns)
            total = jnp.dot(rows[i], weights[:, start:stop], preferred_element_type=jnp.float32)
            for column in range(start, stop, HDIM):
                head = total[:, column - start : column - start + HDIM]
                part, offset = divmod(column, SPAN)
                if part < normed:
                    power = jnp.mean(head * head, axis=-1, keepdims=True)
                    head = head * lax.rsqrt(power + EPS) * gain[...]
                else:
                    head = head * seen[grid_frames[i] + 1, cell : cell + inner, :].astype(jnp.float32)
                out[part, order[i], :, offset : offset + HDIM] = head.astype(out.dtype)


def project(sources, order, grid_frames, blocks, places, gain, seen, parts, normed):
    inner, depth = sources[0].shape
    pieces, shard, columns = blocks.shape
    count = len(sources)
    any_space = pl.BlockSpec(memory_space=pl.ANY)
    vmem = pl.BlockSpec(memory_space=pltpu.VMEM)
    return pl.pallas_call(
        functools.partial(project_body, sources=count, normed=normed),
        grid_spec=pltpu.PrefetchScalarGridSpec(
            num_scalar_prefetch=3,
            grid=(),
            in_specs=[any_space] * (count + 1) + [vmem, vmem],
            out_specs=vmem,
            scratch_shapes=[
                pltpu.VMEM((count, inner, depth), jnp.bfloat16),
                pltpu.VMEM((depth, columns), jnp.bfloat16),
                pltpu.SemaphoreType.DMA((count,)),
                pltpu.SemaphoreType.DMA((pieces,)),
            ],
        ),
        out_shape=jax.ShapeDtypeStruct((parts, count, inner, SPAN), jnp.bfloat16),
        compiler_params=pltpu.CompilerParams(vmem_limit_bytes=VMEM),
        cost_estimate=pl.CostEstimate(
            flops=2 * count * inner * depth * columns,
            bytes_accessed=2 * depth * columns + 2 * count * inner * (depth + columns),
            transcendentals=0,
        ),
    )(places, order, grid_frames, *sources, blocks, gain.reshape(1, HDIM), seen)


def attend_body(meta, *rest, near, far, sides, cell, inner):
    query, main = rest[0], rest[1:-6]
    valid, out, cells, band, sems, full = rest[-6:]
    step = pl.program_id(0)
    member, pair, z_odd, r_odd = (meta[3 * HEADS + i] for i in range(4))
    chip = 1 - pair if far else pair
    width = cell // TH
    frames = cells.shape[0] - 2
    even_rows = pl.multiple_of(jnp.where(z_odd == 1, 0, cell + inner), cell)
    odd_rows = pl.multiple_of(jnp.where(z_odd == 1, cell + inner, 0), cell)

    near_set, far_a, far_b, borders = main[0:3], main[3:6], main[6:9], main[9:]
    near_frame = lambda i: tuple(part.at[:, i] for part in near_set)
    far_frame = lambda i: tuple(part.at[:, i // 2] for part in (far_b if i % 2 else far_a))
    own_frame, other_frame = (far_frame, near_frame) if far else (near_frame, far_frame)

    def load(slot, parts):
        own, even, odd = parts
        for part, start, length in ((own, cell, inner), (even, even_rows, cell), (odd, odd_rows, cell)):
            pltpu.make_async_copy(part, cells.at[slot, :, pl.ds(start, length), :], sems.at[slot]).start()

    def await_slot(slot):
        pltpu.make_async_copy(cells.at[slot], cells.at[slot], sems.at[slot]).wait()

    def border(side):
        own, ends = borders[2 * side : 2 * side + 2]
        return own, ends.at[0], ends.at[1]

    @pl.when(step == 0)
    def _():
        for end, slot in ((0, 0), (1, frames + 1)):

            @pl.when(chip != end)
            def _():
                load(slot, other_frame(0 if end else frames - 1))

            @pl.when(chip == end)
            def _():
                for side in range(sides):
                    pl.when((r_odd == 1) == (end == side))(functools.partial(load, slot, border(side)))

                if sides < 2:

                    @pl.when((r_odd == 1) == (end == 1))
                    def _():
                        cells[slot] = jnp.zeros(cells.shape[1:], cells.dtype)

        for index in range(frames):
            load(index + 1, own_frame(index))
        q_tile = lax.broadcasted_iota(jnp.int32, (cell, 3 * cell), 0)
        k_tile = lax.broadcasted_iota(jnp.int32, (cell, 3 * cell), 1)
        apart = jnp.abs(lax.rem(q_tile, width) // TW - lax.rem(k_tile, width) // TW)
        for reach in range(3):
            band[reach] = jnp.where(apart <= reach, 1.0, 0.0).astype(band.dtype)

    def await_end(slot, end):
        empty = (chip == end) & ((r_odd == 1) == (end == 1)) if sides < 2 else False
        pl.when(jnp.logical_not(empty))(functools.partial(await_slot, slot))

    @pl.when(step == 0)
    def _():
        await_end(0, 0)
        await_slot(1)

    pl.when(step < frames - 1)(lambda: await_slot(step + 2))
    pl.when(step == frames - 1)(lambda: await_end(frames + 1, 1))

    scale = np.float32(np.log2(np.e) / np.sqrt(HDIM))
    first = chip * frames + step

    def attend(head, over_t, over_h):
        lanes = slice(head * HDIM, (head + 1) * HDIM)
        seen = (3 if over_h else 1) * cell
        mask = band[meta[3 * (member * OWN_HEADS + head) + 2], :, :seen]
        for tile in range(inner // cell):
            rows = pl.ds((tile + (0 if over_h else 1)) * cell, seen)
            mine = query[0, 0, pl.ds(tile * cell, cell), lanes]
            total = None
            for near_step in (0, 1, 2) if over_t else (1,):
                scores = lax.dot_general(
                    mine,
                    cells[step + near_step, 0, rows, lanes],
                    (((1,), (1,)), ((), ())),
                    preferred_element_type=jnp.float32,
                )
                terms = jnp.exp2(scores * scale).astype(jnp.bfloat16) * mask
                both = jnp.concatenate(
                    [cells[step + near_step, 1, rows, lanes], valid[first + near_step, rows, :]], axis=1
                )
                part = jnp.dot(terms, both, preferred_element_type=jnp.float32)
                total = part if total is None else total + part
            here = valid[first + 1, pl.ds((tile + 1) * cell, cell), :] > 0
            weight = jnp.where(here, total[:, HDIM:], 1.0)
            result = jnp.where(here, total[:, :HDIM] / weight, 0.0)
            out[0, 0, pl.ds(tile * cell, cell), lanes] = result.astype(out.dtype)

    for head in range(OWN_HEADS):
        reach_t, reach_h = (meta[3 * (member * OWN_HEADS + head) + i] for i in range(2))
        for over_t in (False, True):
            for over_h in (False, True):
                pl.when(((reach_t > 0) == over_t) & ((reach_h > 0) == over_h))(
                    functools.partial(attend, head, over_t, over_h)
                )


def attend(meta, query, near_set, far_a, far_b, borders, valid, far):
    _, chip_frames, inner, _ = near_set[0].shape
    cell = near_set[1].shape[2]
    span = inner + 2 * cell
    near = chip_frames // CORES
    parts = [*near_set, *far_a, *far_b, *(p for pair in borders for p in pair)]
    chip = lambda m: 1 - m[3 * HEADS + 1] if far else m[3 * HEADS + 1]
    core = lambda m: m[3 * HEADS] % CORES
    return pl.pallas_call(
        functools.partial(
            attend_body, near=near, far=far, sides=len(borders), cell=cell, inner=inner
        ),
        grid_spec=pltpu.PrefetchScalarGridSpec(
            num_scalar_prefetch=1,
            grid=(chip_frames,),
            in_specs=[
                pl.BlockSpec((1, 1, inner, SPAN), lambda f, m: (0, chip(m) * chip_frames + f, 0, 0)),
                *[pl.BlockSpec(memory_space=pl.ANY)] * len(parts),
                pl.BlockSpec(memory_space=pltpu.VMEM),
            ],
            out_specs=pl.BlockSpec(
                (1, 1, inner, SPAN), lambda f, m: ((f // near) ^ core(m), f % near, 0, 0)
            ),
            scratch_shapes=[
                pltpu.VMEM((chip_frames + 2, 2, span, SPAN), jnp.bfloat16),
                pltpu.VMEM((3, cell, 3 * cell), jnp.bfloat16),
                pltpu.SemaphoreType.DMA((chip_frames + 2,)),
                pltpu.SMEM((1,), jnp.int32),
            ],
        ),
        out_shape=jax.ShapeDtypeStruct((CORES, near, inner, SPAN), jnp.bfloat16),
        compiler_params=pltpu.CompilerParams(vmem_limit_bytes=VMEM),
        cost_estimate=pl.CostEstimate(
            flops=OWN_HEADS * chip_frames * inner * 9 * cell * HDIM * 6,
            bytes_accessed=4 * SPAN * (chip_frames + 2) * span + 4 * SPAN * chip_frames * inner,
            transcendentals=OWN_HEADS * chip_frames * inner * 9 * cell,
        ),
    )(meta, query, *parts, valid)


def collect_body(member, *rest):
    out = rest[-1]
    for flip, piece in enumerate(rest[:-1]):
        column = pl.multiple_of((member[0] ^ flip) * SPAN, SPAN)
        out[:, pl.ds(column, SPAN)] = piece[...]


def collect(member, pieces):
    rows = pieces[0].shape[0]
    whole = pl.BlockSpec((rows, SPAN), lambda i, m: (0, 0))
    return pl.pallas_call(
        collect_body,
        grid_spec=pltpu.PrefetchScalarGridSpec(
            num_scalar_prefetch=1,
            grid=(1,),
            in_specs=[whole] * MATES,
            out_specs=pl.BlockSpec((rows, HEADS * HDIM), lambda i, m: (0, 0)),
        ),
        out_shape=jax.ShapeDtypeStruct((rows, HEADS * HDIM), jnp.bfloat16),
        compiler_params=pltpu.CompilerParams(vmem_limit_bytes=VMEM),
    )(member.reshape(1), *pieces)


def gather_blocks(pieces, places):
    blocks = lax.all_gather(pieces, ("rest", "height"))
    blocks = blocks.reshape(-1, *blocks.shape[2:])
    if blocks.shape[1] % 16:
        ordered = jnp.zeros_like(blocks).at[places].set(blocks)
        return ordered.reshape(1, -1, blocks.shape[2]), jnp.zeros((1,), jnp.int32)
    return blocks, places


def per_device(tokens, mod_scale, mod_shift, w_qkv, q_gain, k_gain, window, valid):
    frames, rows, width, features = tokens.shape
    count = frames * rows * width
    inner = rows * width
    cell = TH * width
    model = w_qkv.shape[1] // 3
    rest, pair, core, height = (lax.axis_index(a) for a in ("rest", "pair", "core", "height"))
    member = pair * CORES + core
    high = lax.axis_size("height")
    many = lax.axis_size("rest")
    z_odd = height % 2
    r_odd = rest % 2
    ints = lambda *values: jnp.stack(values).astype(jnp.int32)

    def columns_of(mate):
        return jnp.concatenate(
            [lax.dynamic_slice_in_dim(w_qkv, s * model + mate * SPAN, SPAN, axis=1) for s in range(3)], axis=1
        )

    shares = [columns_of(member)] + [swap(columns_of(member ^ flip), TEAM, flip) for flip in range(1, MATES)]
    stacked = jnp.stack(shares)
    kv_share, q_share = stacked[:, :, SPAN:], stacked[:, :, :SPAN]
    mine = [modulate(tokens[f].reshape(inner, features), mod_scale, mod_shift) for f in range(frames)]
    kv_share, q_share, *mine = lax.optimization_barrier((kv_share, q_share, *mine))
    places = ints(
        *[
            (r * MATES + (member ^ j)) * high + h
            for r in range(many)
            for h in range(high)
            for j in range(MATES)
        ]
    )
    kv_blocks, kv_places = gather_blocks(kv_share, places)
    q_blocks, q_places = gather_blocks(q_share, places)

    across = [swap(x, "pair", 1) for x in mine]
    beside = [swap(x, "core", 1) for x in mine]
    beyond = [swap(x, "core", 1) for x in across]

    total_frames = MATES * frames
    valid_pad = jnp.pad(valid, ((TT, TT), (TH, TH), (0, 0)))
    around = lax.dynamic_slice(
        valid_pad,
        (rest * total_frames, height * rows, jnp.int32(0)),
        (total_frames + 2 * TT, rows + 2 * TH, width),
    )
    seen = jnp.broadcast_to(
        (around > 0).astype(jnp.bfloat16).reshape(total_frames + 2 * TT, -1, 1),
        (total_frames + 2 * TT, (rows + 2 * TH) * width, HDIM),
    )

    def cells_of(sources, order, grid_frames):
        grid = project(sources, order, grid_frames, kv_blocks, kv_places, k_gain, seen, 2, 1)
        low, top = jnp.int32(0), jnp.int32(inner - cell)
        even = swap_neighbours(
            lax.dynamic_slice_in_dim(grid, jnp.where(z_odd == 1, low, top), cell, axis=2), "height", 0
        )
        odd = swap_neighbours(
            lax.dynamic_slice_in_dim(grid, jnp.where(z_odd == 1, top, low), cell, axis=2), "height", 1
        )
        return grid, even, odd

    places_of = lambda flip: [(member ^ flip) * frames + f for f in range(frames)]
    by_core = [core * frames + f for f in range(frames)] + [(1 - core) * frames + f for f in range(frames)]
    near_set = cells_of([*mine, *beside], ints(*by_core), ints(*places_of(0), *places_of(1)))
    far_sets = [
        cells_of(
            [across[f], beyond[f]], ints(core, 1 - core), ints(places_of(2)[f], places_of(3)[f])
        )
        for f in range(frames)
    ]
    everyone = ints(*(p for flip in range(MATES) for p in places_of(flip)))
    query = project(
        [*mine, *beside, *across, *beyond], everyone, everyone, q_blocks, q_places, q_gain, seen, 1, 1
    )

    def border(odd):
        last = r_odd == odd
        chosen = jnp.where(last, 1, 0) == pair
        own, even, other = (
            jnp.where(
                chosen,
                jnp.where(last, a[:, -1], a[:, 0]),
                jnp.where(last, c[:, -1], b[:, 0]),
            )
            for a, b, c in zip(near_set, far_sets[0], far_sets[-1])
        )
        return (
            swap_neighbours(own, "rest", odd),
            swap_neighbours(jnp.stack([even, other]), "rest", odd),
        )

    borders = [border(odd) for odd in range(min(2, many - 1))]
    meta = jnp.concatenate([window.reshape(-1), ints(member, pair, z_odd, r_odd)])
    far_out = attend(meta, query, near_set, *far_sets, borders, seen, True).reshape(CORES, count, SPAN)
    travelled = [swap(far_out[flip], TEAM, CORES + flip) for flip in range(CORES)]
    near_out = attend(meta, query, near_set, *far_sets, borders, seen, False).reshape(CORES, count, SPAN)
    pieces = [near_out[0], swap(near_out[1], TEAM, 1), *travelled]
    return collect(member.astype(jnp.int32), pieces).reshape(frames, rows, width, model)


def solution(mesh):
    split = Mesh(
        mesh.devices.reshape(mesh.shape["tm"] // MATES, MATES // CORES, CORES, mesh.shape["height"]),
        ("rest", "pair", "core", "height"),
    )
    along = ("rest", "pair", "core")
    in_specs = (
        P(along, "height", None, None),
        P(),
        P(),
        P((*along, "height"), None),
        P(),
        P(),
        P(),
        P(),
    )
    out_specs = P(along, "height", None, None)
    return jax.shard_map(
        per_device, mesh=split, in_specs=in_specs, out_specs=out_specs, check_vma=False
    )
```

```python
import functools

import jax
import jax.numpy as jnp
import numpy as np
from jax import lax
from jax.experimental import pallas as pl
from jax.experimental.pallas import tpu as pltpu
from jax.sharding import Mesh
from jax.sharding import PartitionSpec as P

HDIM = 128
HEADS = 12
TT = 1
TH = 2
TW = 8
CORES = 2
MATES = 4
OWN_HEADS = HEADS // MATES
SPAN = OWN_HEADS * HDIM
EPS = 1e-06
VMEM = 56 * 1024 * 1024
TEAM = ("pair", "core")


def swap(x, axis, flip):
    names = axis if isinstance(axis, tuple) else (axis,)
    count = int(np.prod([lax.axis_size(name) for name in names]))
    return lax.ppermute(x, axis, [(i, i ^ flip) for i in range(count)])


def swap_neighbours(x, axis, odd):
    count = lax.axis_size(axis)
    pairs = [(i, i + 1) for i in range(odd, count - 1, 2)]
    return lax.ppermute(x, axis, pairs + [(j, i) for i, j in pairs])


def modulate_body(tokens, scale, shift, out):
    values = tokens[...].astype(jnp.float32)
    centred = values - jnp.mean(values, axis=-1, keepdims=True)
    variance = jnp.mean(centred * centred, axis=-1, keepdims=True)
    normed = centred * lax.rsqrt(variance + EPS)
    out[...] = (normed * (1.0 + scale[...]) + shift[...]).astype(out.dtype)


def modulate(tokens, scale, shift, first, count):
    features = tokens.shape[1]
    block = count // 2
    row = lambda start: pl.BlockSpec((block, features), lambda i: (start // block + i, 0))
    whole = pl.BlockSpec((1, features), lambda i: (0, 0))
    return pl.pallas_call(
        modulate_body,
        grid=(count // block,),
        in_specs=[row(first), whole, whole],
        out_specs=row(0),
        out_shape=jax.ShapeDtypeStruct((count, features), jnp.bfloat16),
        compiler_params=pltpu.CompilerParams(vmem_limit_bytes=VMEM),
        cost_estimate=pl.CostEstimate(
            flops=12 * count * features, bytes_accessed=4 * count * features, transcendentals=0
        ),
    )(tokens, scale.reshape(1, features), shift.reshape(1, features))


def project_body(places, order, grid_frames, *rest, sources, normed, halves):
    xs = rest[:sources]
    blocks, gain, seen = rest[sources : sources + 3]
    outs, (rows, weights, row_sems, weight_sems) = rest[sources + 3 : -4], rest[-4:]
    pieces, depth, columns = blocks.shape
    inner = rows.shape[1]
    cell = (seen.shape[1] - inner) // 2

    loads = [pltpu.make_async_copy(x, rows.at[i], row_sems.at[i]) for i, x in enumerate(xs)]
    copies = []
    for p in range(pieces):
        row = pl.multiple_of(places[p] * depth, depth)
        copies.append(pltpu.make_async_copy(blocks.at[p], weights.at[pl.ds(row, depth), :], weight_sems.at[p]))
    loads[0].start()
    for copy in copies:
        copy.start()
    for load in loads[1:]:
        load.start()
    for copy in copies:
        copy.wait()
    for i in range(sources):
        loads[i].wait()
        total = jnp.dot(rows[i], weights[...], preferred_element_type=jnp.float32)
        for column in range(0, columns, HDIM):
            head = total[:, column : column + HDIM]
            part, offset = divmod(column, SPAN)
            if part < normed:
                power = jnp.mean(head * head, axis=-1, keepdims=True)
                head = head * lax.rsqrt(power + EPS) * gain[...]
            else:
                head = head * seen[grid_frames[i] + 1, cell : cell + inner, :].astype(jnp.float32)
            head = head.astype(jnp.bfloat16)
            lanes = slice(offset, offset + HDIM)
            if halves:
                top, bottom = head[:cell], head[cell:]
                odd = order[sources] == 1
                outs[0][part, order[i], :, lanes] = jnp.where(odd, top, bottom)
                outs[1][part, order[i], :, lanes] = jnp.where(odd, bottom, top)
            else:
                outs[0][part, order[i], :, lanes] = head


def project(sources, order, grid_frames, blocks, places, gain, seen, parts, normed, halves):
    inner, depth = sources[0].shape
    pieces, shard, columns = blocks.shape
    count = len(sources)
    any_space = pl.BlockSpec(memory_space=pl.ANY)
    vmem = pl.BlockSpec(memory_space=pltpu.VMEM)
    outs = 2 if halves else 1
    return pl.pallas_call(
        functools.partial(project_body, sources=count, normed=normed, halves=halves),
        grid_spec=pltpu.PrefetchScalarGridSpec(
            num_scalar_prefetch=3,
            grid=(),
            in_specs=[any_space] * (count + 1) + [vmem, vmem],
            out_specs=[vmem] * outs,
            scratch_shapes=[
                pltpu.VMEM((count, inner, depth), jnp.bfloat16),
                pltpu.VMEM((depth, columns), jnp.bfloat16),
                pltpu.SemaphoreType.DMA((count,)),
                pltpu.SemaphoreType.DMA((pieces,)),
            ],
        ),
        out_shape=[jax.ShapeDtypeStruct((parts, count, inner // outs, SPAN), jnp.bfloat16)] * outs,
        compiler_params=pltpu.CompilerParams(vmem_limit_bytes=VMEM),
        cost_estimate=pl.CostEstimate(
            flops=2 * count * inner * depth * columns,
            bytes_accessed=2 * depth * columns + 2 * count * inner * (depth + columns),
            transcendentals=0,
        ),
    )(places, order, grid_frames, *sources, blocks, gain.reshape(1, HDIM), seen)


def attend_body(meta, *rest, near, far, sides, cell, inner):
    query, main = rest[0], rest[1:-7]
    valid, out_first, out_second, cells, band, sems, result_cells = rest[-7:]
    step = pl.program_id(0)
    member, pair, z_odd, r_odd = (meta[3 * HEADS + i] for i in range(4))
    chip = 1 - pair if far else pair
    core = member % CORES
    width = cell // TH
    frames = cells.shape[0] - 2

    row_of = [jnp.where(z_odd == 1, a, b) * cell for a, b in ((1, 2), (2, 1), (0, 3), (3, 0))]
    near_set, far_a, far_b, borders = main[0:4], main[4:8], main[8:12], main[12:]
    near_frame = lambda i: tuple(part.at[:, i] for part in near_set)
    far_frame = lambda i: tuple(part.at[:, i // 2] for part in (far_b if i % 2 else far_a))
    own_frame, other_frame = (far_frame, near_frame) if far else (near_frame, far_frame)

    def load(slot, parts):
        for part, row in zip(parts, row_of):
            rows = pl.ds(pl.multiple_of(row, cell), cell)
            pltpu.make_async_copy(part, cells.at[slot, :, rows, :], sems.at[slot]).start()

    def await_slot(slot):
        pltpu.make_async_copy(cells.at[slot], cells.at[slot], sems.at[slot]).wait()

    def border(side):
        sent, received = borders[2 * side : 2 * side + 2]
        return sent.at[0], sent.at[1], received.at[0], received.at[1]

    @pl.when(step == 0)
    def _():
        for end, slot in ((0, 0), (1, frames + 1)):

            @pl.when(chip != end)
            def _():
                load(slot, other_frame(0 if end else frames - 1))

            @pl.when(chip == end)
            def _():
                for side in range(sides):
                    pl.when((r_odd == 1) == (end == side))(functools.partial(load, slot, border(side)))

                if sides < 2:

                    @pl.when((r_odd == 1) == (end == 1))
                    def _():
                        cells[slot] = jnp.zeros(cells.shape[1:], cells.dtype)

        for index in range(frames):
            load(index + 1, own_frame(index))
        q_tile = lax.broadcasted_iota(jnp.int32, (cell, 3 * cell), 0)
        k_tile = lax.broadcasted_iota(jnp.int32, (cell, 3 * cell), 1)
        apart = jnp.abs(lax.rem(q_tile, width) // TW - lax.rem(k_tile, width) // TW)
        for reach in range(3):
            band[reach] = jnp.where(apart <= reach, 1.0, 0.0).astype(band.dtype)

    def await_end(slot, end):
        empty = (chip == end) & ((r_odd == 1) == (end == 1)) if sides < 2 else False
        pl.when(jnp.logical_not(empty))(functools.partial(await_slot, slot))

    low, top = (lambda: await_end(0, 0)), (lambda: await_end(frames + 1, 1))

    @pl.when(step == 0)
    def _():
        for slot in range(near, near + 2):
            await_slot(slot)

    def await_side(lower):
        if lower:
            low()
            for slot in range(1, near):
                await_slot(slot)
        else:
            for slot in range(near + 2, frames + 1):
                await_slot(slot)
            top()

    for at, first_core in ((0, 0), (near, 1)):
        pl.when((step == at) & (core == first_core))(functools.partial(await_side, True))
        pl.when((step == at) & (core != first_core))(functools.partial(await_side, False))

    slot = step ^ (near * core)
    scale = np.float32(np.log2(np.e) / np.sqrt(HDIM))
    first = chip * frames + slot

    def attend(out, head, over_t, over_h):
        lanes = slice(head * HDIM, (head + 1) * HDIM)
        seen = (3 if over_h else 1) * cell
        mask = band[meta[3 * (member * OWN_HEADS + head) + 2], :, :seen]
        for tile in range(inner // cell):
            rows = pl.ds((tile + (0 if over_h else 1)) * cell, seen)
            mine = query[0, 0, pl.ds(tile * cell, cell), lanes]
            total = None
            for near_step in (0, 1, 2) if over_t else (1,):
                scores = lax.dot_general(
                    mine,
                    cells[slot + near_step, 0, rows, lanes],
                    (((1,), (1,)), ((), ())),
                    preferred_element_type=jnp.float32,
                )
                terms = jnp.exp2(scores * scale).astype(jnp.bfloat16) * mask
                both = jnp.concatenate(
                    [cells[slot + near_step, 1, rows, lanes], valid[first + near_step, rows, :]], axis=1
                )
                part = jnp.dot(terms, both, preferred_element_type=jnp.float32)
                total = part if total is None else total + part
            here = valid[first + 1, pl.ds((tile + 1) * cell, cell), :] > 0
            weight = jnp.where(here, total[:, HDIM:], 1.0)
            result = jnp.where(here, total[:, :HDIM] / weight, 0.0)
            out[0, pl.ds(tile * cell, cell), lanes] = result.astype(out.dtype)

    for head in range(OWN_HEADS):
        reach_t, reach_h = (meta[3 * (member * OWN_HEADS + head) + i] for i in range(2))
        for over_t in (False, True):
            for over_h in (False, True):
                pl.when(((reach_t > 0) == over_t) & ((reach_h > 0) == over_h))(
                    functools.partial(attend, result_cells, head, over_t, over_h)
                )

    pl.when(step < near)(lambda: out_first.__setitem__(0, result_cells[0]))
    pl.when(step >= near)(lambda: out_second.__setitem__(0, result_cells[0]))


def attend(meta, query, near_set, far_a, far_b, borders, valid, far):
    _, chip_frames, cell, _ = near_set[0].shape
    inner = 2 * cell
    span = 4 * cell
    near = chip_frames // CORES
    parts = [*near_set, *far_a, *far_b, *(p for pair in borders for p in pair)]
    chip = lambda m: 1 - m[3 * HEADS + 1] if far else m[3 * HEADS + 1]
    frame = lambda f, m: chip(m) * chip_frames + (f ^ (near * (m[3 * HEADS] % CORES)))
    piece = jax.ShapeDtypeStruct((near, inner, SPAN), jnp.bfloat16)
    return pl.pallas_call(
        functools.partial(
            attend_body, near=near, far=far, sides=len(borders), cell=cell, inner=inner
        ),
        grid_spec=pltpu.PrefetchScalarGridSpec(
            num_scalar_prefetch=1,
            grid=(chip_frames,),
            in_specs=[
                pl.BlockSpec((1, 1, inner, SPAN), lambda f, m: (0, frame(f, m), 0, 0)),
                *[pl.BlockSpec(memory_space=pl.ANY)] * len(parts),
                pl.BlockSpec(memory_space=pltpu.VMEM),
            ],
            out_specs=[
                pl.BlockSpec((1, inner, SPAN), lambda f, m: (jnp.minimum(f, near - 1), 0, 0)),
                pl.BlockSpec((1, inner, SPAN), lambda f, m: (jnp.maximum(f - near, 0), 0, 0)),
            ],
            scratch_shapes=[
                pltpu.VMEM((chip_frames + 2, 2, span, SPAN), jnp.bfloat16),
                pltpu.VMEM((3, cell, 3 * cell), jnp.bfloat16),
                pltpu.SemaphoreType.DMA((chip_frames + 2,)),
                pltpu.VMEM((1, inner, SPAN), jnp.bfloat16),
            ],
        ),
        out_shape=[piece, piece],
        compiler_params=pltpu.CompilerParams(vmem_limit_bytes=VMEM),
        cost_estimate=pl.CostEstimate(
            flops=OWN_HEADS * chip_frames * inner * 9 * cell * HDIM * 6,
            bytes_accessed=4 * SPAN * (chip_frames + 2) * span + 4 * SPAN * chip_frames * inner,
            transcendentals=OWN_HEADS * chip_frames * inner * 9 * cell,
        ),
    )(meta, query, *parts, valid)


def collect_body(member, *rest):
    out = rest[-1]
    for flip, piece in enumerate(rest[:-1]):
        column = pl.multiple_of((member[0] ^ flip) * SPAN, SPAN)
        out[:, pl.ds(column, SPAN)] = piece[...]


def collect(member, pieces):
    rows = pieces[0].shape[0]
    whole = pl.BlockSpec((rows, SPAN), lambda i, m: (0, 0))
    return pl.pallas_call(
        collect_body,
        grid_spec=pltpu.PrefetchScalarGridSpec(
            num_scalar_prefetch=1,
            grid=(1,),
            in_specs=[whole] * MATES,
            out_specs=pl.BlockSpec((rows, HEADS * HDIM), lambda i, m: (0, 0)),
        ),
        out_shape=jax.ShapeDtypeStruct((rows, HEADS * HDIM), jnp.bfloat16),
        compiler_params=pltpu.CompilerParams(vmem_limit_bytes=VMEM),
    )(member.reshape(1), *pieces)


def gather_blocks(pieces, places):
    blocks = lax.all_gather(pieces, ("rest", "height"))
    blocks = blocks.reshape(-1, *blocks.shape[2:])
    if blocks.shape[1] % 16:
        ordered = jnp.zeros_like(blocks).at[places].set(blocks)
        return ordered.reshape(1, -1, blocks.shape[2]), jnp.zeros((1,), jnp.int32)
    return blocks, places


def per_device(tokens, mod_scale, mod_shift, w_qkv, q_gain, k_gain, window, valid):
    frames, rows, width, features = tokens.shape
    count = frames * rows * width
    inner = rows * width
    cell = TH * width
    model = w_qkv.shape[1] // 3
    rest, pair, core, height = (lax.axis_index(a) for a in ("rest", "pair", "core", "height"))
    member = pair * CORES + core
    high = lax.axis_size("height")
    many = lax.axis_size("rest")
    z_odd = height % 2
    r_odd = rest % 2
    ints = lambda *values: jnp.stack(values).astype(jnp.int32)

    def columns_of(mate):
        return jnp.concatenate(
            [lax.dynamic_slice_in_dim(w_qkv, s * model + mate * SPAN, SPAN, axis=1) for s in range(3)], axis=1
        )

    shares = [columns_of(member)] + [swap(columns_of(member ^ flip), TEAM, flip) for flip in range(1, MATES)]
    stacked = jnp.stack(shares)
    kv_share, q_share = stacked[:, :, SPAN:], stacked[:, :, :SPAN]
    flat = tokens.reshape(count, features)
    mine = [modulate(flat, mod_scale, mod_shift, 0, inner)]
    kv_share, q_share, scale_after = lax.optimization_barrier((kv_share, q_share, mod_scale))
    mine += [modulate(flat, scale_after, mod_shift, f * inner, inner) for f in range(1, frames)]
    places = ints(
        *[
            (r * MATES + (member ^ j)) * high + h
            for r in range(many)
            for h in range(high)
            for j in range(MATES)
        ]
    )
    kv_blocks, kv_places = gather_blocks(kv_share, places)
    q_blocks, q_places = gather_blocks(q_share, places)

    across = [swap(x, "pair", 1) for x in mine]
    beside = [swap(x, "core", 1) for x in mine]
    beyond = [swap(x, "core", 1) for x in across]

    total_frames = MATES * frames
    valid_pad = jnp.pad(valid, ((TT, TT), (TH, TH), (0, 0)))
    around = lax.dynamic_slice(
        valid_pad,
        (rest * total_frames, height * rows, jnp.int32(0)),
        (total_frames + 2 * TT, rows + 2 * TH, width),
    )
    seen = jnp.broadcast_to(
        (around > 0).astype(jnp.bfloat16).reshape(total_frames + 2 * TT, -1, 1),
        (total_frames + 2 * TT, (rows + 2 * TH) * width, HDIM),
    )

    def cells_of(sources, order, grid_frames, after=()):
        even, odd = project(
            sources, order, grid_frames, kv_blocks, kv_places, k_gain, seen, 2, 1, True
        )
        even, odd, *after = lax.optimization_barrier((even, odd, *after))
        from_even, from_odd = swap_neighbours(even, "height", 0), swap_neighbours(odd, "height", 1)
        return (even, odd, from_even, from_odd), after

    places_of = lambda flip: [(member ^ flip) * frames + f for f in range(frames)]
    by_core = [core * frames + f for f in range(frames)] + [(1 - core) * frames + f for f in range(frames)]
    near_set, _ = cells_of([*mine, *beside], ints(*by_core, z_odd), ints(*places_of(0), *places_of(1)))
    far_sets = []
    for f in range(frames):
        last = f == frames - 1
        found, after = cells_of(
            [across[f], beyond[f]],
            ints(core, 1 - core, z_odd),
            ints(places_of(2)[f], places_of(3)[f]),
            near_set[2:] if last else (),
        )
        far_sets.append(found)
        if last:
            near_set = (*near_set[:2], *after)
    everyone = ints(*(p for flip in range(MATES) for p in places_of(flip)))
    (query,) = project(
        [*mine, *beside, *across, *beyond], everyone, everyone, q_blocks, q_places, q_gain, seen, 1, 1, False
    )
    query, *received = lax.optimization_barrier((query, *far_sets[0][2:], *far_sets[-1][2:]))
    far_sets = [(*found[:2], *received[2 * f : 2 * f + 2]) for f, found in enumerate(far_sets)]

    def border(odd):
        last = r_odd == odd
        chosen = jnp.where(last, 1, 0) == pair
        cells = [
            jnp.where(
                chosen,
                jnp.where(last, a[:, -1], a[:, 0]),
                jnp.where(last, c[:, -1], b[:, 0]),
            )
            for a, b, c in zip(near_set, far_sets[0], far_sets[-1])
        ]
        return (
            swap_neighbours(jnp.stack(cells[:2]), "rest", odd),
            swap_neighbours(jnp.stack(cells[2:]), "rest", odd),
        )

    borders = [border(odd) for odd in range(min(2, many - 1))]
    meta = jnp.concatenate([window.reshape(-1), ints(member, pair, z_odd, r_odd)])
    far_out = attend(meta, query, near_set, *far_sets, borders, seen, True)
    meta, *far_out = lax.optimization_barrier((meta, *far_out))
    travelled = [swap(out.reshape(count, SPAN), TEAM, CORES + flip) for flip, out in enumerate(far_out)]
    near_out = attend(meta, query, near_set, *far_sets, borders, seen, False)
    pieces = [near_out[0].reshape(count, SPAN), swap(near_out[1].reshape(count, SPAN), TEAM, 1), *travelled]
    return collect(member.astype(jnp.int32), pieces).reshape(frames, rows, width, model)


def solution(mesh):
    split = Mesh(
        mesh.devices.reshape(mesh.shape["tm"] // MATES, MATES // CORES, CORES, mesh.shape["height"]),
        ("rest", "pair", "core", "height"),
    )
    along = ("rest", "pair", "core")
    in_specs = (
        P(along, "height", None, None),
        P(),
        P(),
        P((*along, "height"), None),
        P(),
        P(),
        P(),
        P(),
    )
    out_specs = P(along, "height", None, None)
    return jax.shard_map(
        per_device, mesh=split, in_specs=in_specs, out_specs=out_specs, check_vma=False
    )
```

```python
import functools

import jax
import jax.numpy as jnp
import numpy as np
from jax import lax
from jax.experimental import pallas as pl
from jax.experimental.pallas import tpu as pltpu
from jax.sharding import Mesh
from jax.sharding import PartitionSpec as P

HDIM = 128
HEADS = 12
TT = 1
TH = 2
TW = 8
CORES = 2
MATES = 4
OWN_HEADS = HEADS // MATES
SPAN = OWN_HEADS * HDIM
EPS = 1e-06
MIB = 1024 * 1024
TEAM = ("pair", "core")

MEMBER, PAIR, CORE, Z_ODD, R_ODD = (3 * HEADS + i for i in range(5))


def swap(x, axis, flip):
    names = axis if isinstance(axis, tuple) else (axis,)
    count = int(np.prod([lax.axis_size(name) for name in names]))
    return lax.ppermute(x, axis, [(i, i ^ flip) for i in range(count)])


def swap_neighbours(x, axis, odd):
    count = lax.axis_size(axis)
    pairs = [(i, i + 1) for i in range(odd, count - 1, 2)]
    flat = x.reshape(-1, x.shape[-1])
    return lax.ppermute(flat, axis, pairs + [(j, i) for i, j in pairs]).reshape(x.shape)


def modulate_body(tokens, scale, shift, out):
    values = tokens[...].astype(jnp.float32)
    centred = values - jnp.mean(values, axis=-1, keepdims=True)
    variance = jnp.mean(centred * centred, axis=-1, keepdims=True)
    normed = centred * lax.rsqrt(variance + EPS)
    out[...] = (normed * (1.0 + scale[...]) + shift[...]).astype(out.dtype)


def modulate(tokens, scale, shift, first, count):
    features = tokens.shape[1]
    block = count // 2
    row = lambda start: pl.BlockSpec((block, features), lambda i: (start // block + i, 0))
    whole = pl.BlockSpec((1, features), lambda i: (0, 0))
    return pl.pallas_call(
        modulate_body,
        grid=(count // block,),
        in_specs=[row(first), whole, whole],
        out_specs=row(0),
        out_shape=jax.ShapeDtypeStruct((count, features), jnp.bfloat16),
        compiler_params=pltpu.CompilerParams(vmem_limit_bytes=24 * MIB),
        cost_estimate=pl.CostEstimate(
            flops=12 * count * features, bytes_accessed=4 * count * features, transcendentals=0
        ),
    )(tokens, scale.reshape(1, features), shift.reshape(1, features))


def project_body(meta, *rest, sources, normed, halves, spots):
    xs = rest[:sources]
    blocks, gain = rest[sources : sources + 2]
    outs, (rows, weights, row_sems, weight_sems) = rest[sources + 2 : -4], rest[-4:]
    pieces, depth, columns = blocks.shape
    cell = rows.shape[1] // 2
    frames = sources // (CORES if halves else MATES)

    loads = [pltpu.make_async_copy(x, rows.at[i], row_sems.at[i]) for i, x in enumerate(xs)]
    copies = []
    for p, (base, flip, step) in enumerate(spots):
        row = pl.multiple_of((base + (meta[MEMBER] ^ flip) * step) * depth, depth)
        copies.append(pltpu.make_async_copy(blocks.at[p], weights.at[pl.ds(row, depth), :], weight_sems.at[p]))
    loads[0].start()
    for copy in copies:
        copy.start()
    for load in loads[1:]:
        load.start()
    for copy in copies:
        copy.wait()
    for i in range(sources):
        loads[i].wait()
        place = (meta[CORE if halves else MEMBER] ^ (i // frames)) * frames + i % frames
        total = jnp.dot(rows[i], weights[...], preferred_element_type=jnp.float32)
        for column in range(0, columns, HDIM):
            head = total[:, column : column + HDIM]
            part, offset = divmod(column, SPAN)
            if part < normed:
                power = jnp.mean(head * head, axis=-1, keepdims=True)
                head = head * lax.rsqrt(power + EPS) * gain[...]
            head = head.astype(jnp.bfloat16)
            lanes = slice(offset, offset + HDIM)
            if halves:
                top, bottom = head[:cell], head[cell:]
                odd = meta[Z_ODD] == 1
                outs[0][part, place, :, lanes] = jnp.where(odd, top, bottom)
                outs[1][part, place, :, lanes] = jnp.where(odd, bottom, top)
            else:
                outs[0][part, place, :, lanes] = head


def project(meta, sources, blocks, spots, gain, parts, normed, halves):
    inner, depth = sources[0].shape
    pieces, shard, columns = blocks.shape
    count = len(sources)
    any_space = pl.BlockSpec(memory_space=pl.ANY)
    vmem = pl.BlockSpec(memory_space=pltpu.VMEM)
    outs = 2 if halves else 1
    return pl.pallas_call(
        functools.partial(project_body, sources=count, normed=normed, halves=halves, spots=spots),
        grid_spec=pltpu.PrefetchScalarGridSpec(
            num_scalar_prefetch=1,
            grid=(),
            in_specs=[any_space] * (count + 1) + [vmem],
            out_specs=[vmem] * outs,
            scratch_shapes=[
                pltpu.VMEM((count, inner, depth), jnp.bfloat16),
                pltpu.VMEM((depth, columns), jnp.bfloat16),
                pltpu.SemaphoreType.DMA((count,)),
                pltpu.SemaphoreType.DMA((pieces,)),
            ],
        ),
        out_shape=[jax.ShapeDtypeStruct((parts, count, inner // outs, SPAN), jnp.bfloat16)] * outs,
        compiler_params=pltpu.CompilerParams(vmem_limit_bytes=32 * MIB),
        cost_estimate=pl.CostEstimate(
            flops=2 * count * inner * depth * columns,
            bytes_accessed=2 * depth * columns + 2 * count * inner * (depth + columns),
            transcendentals=0,
        ),
    )(meta, *sources, blocks, gain.reshape(1, HDIM))


def attend_body(meta, *rest, near, far, sides, cell, inner):
    query, main = rest[0], rest[1:-7]
    valid, out_first, out_second, cells, band, sems, result_cells = rest[-7:]
    step = pl.program_id(0)
    member, pair, core, z_odd, r_odd = (meta[i] for i in (MEMBER, PAIR, CORE, Z_ODD, R_ODD))
    chip = 1 - pair if far else pair
    width = cell // TH
    frames = cells.shape[0] - 2

    row_of = [jnp.where(z_odd == 1, a, b) * cell for a, b in ((1, 2), (2, 1), (0, 3), (3, 0))]
    own_set, other_set, borders = main[0:4], main[4:8], main[8:]
    own_frame = lambda i: tuple(part.at[:, i] for part in own_set)
    other_frame = lambda i: tuple(part.at[:, i] for part in other_set)

    def load(slot, parts):
        for part, row in zip(parts, row_of):
            rows = pl.ds(pl.multiple_of(row, cell), cell)
            pltpu.make_async_copy(part, cells.at[slot, :, rows, :], sems.at[slot]).start()

    def await_slot(slot):
        pltpu.make_async_copy(cells.at[slot], cells.at[slot], sems.at[slot]).wait()

    def border(side):
        sent, received = borders[2 * side : 2 * side + 2]
        return sent.at[0], sent.at[1], received.at[0], received.at[1]

    @pl.when(step == 0)
    def _():
        for end, slot in ((0, 0), (1, frames + 1)):

            @pl.when(chip != end)
            def _():
                load(slot, other_frame(0 if end else frames - 1))

            @pl.when(chip == end)
            def _():
                for side in range(sides):
                    pl.when((r_odd == 1) == (end == side))(functools.partial(load, slot, border(side)))

                if sides < 2:

                    @pl.when((r_odd == 1) == (end == 1))
                    def _():
                        cells[slot] = jnp.zeros(cells.shape[1:], cells.dtype)

        for index in range(frames):
            load(index + 1, own_frame(index))
        q_tile = lax.broadcasted_iota(jnp.int32, (cell, 3 * cell), 0)
        k_tile = lax.broadcasted_iota(jnp.int32, (cell, 3 * cell), 1)
        apart = jnp.abs(lax.rem(q_tile, width) // TW - lax.rem(k_tile, width) // TW)
        for reach in range(3):
            band[reach] = jnp.where(apart <= reach, 1.0, 0.0).astype(band.dtype)

    def await_end(slot, end):
        empty = (chip == end) & ((r_odd == 1) == (end == 1)) if sides < 2 else False
        pl.when(jnp.logical_not(empty))(functools.partial(await_slot, slot))

    low, top = (lambda: await_end(0, 0)), (lambda: await_end(frames + 1, 1))

    @pl.when(step == 0)
    def _():
        for slot in range(near, near + 2):
            await_slot(slot)

    def await_side(lower):
        if lower:
            low()
            for slot in range(1, near):
                await_slot(slot)
        else:
            for slot in range(near + 2, frames + 1):
                await_slot(slot)
            top()

    for at, first_core in ((0, 0), (near, 1)):
        pl.when((step == at) & (core == first_core))(functools.partial(await_side, True))
        pl.when((step == at) & (core != first_core))(functools.partial(await_side, False))

    slot = step ^ (near * core)
    scale = np.float32(np.log2(np.e) / np.sqrt(HDIM))
    first = chip * frames + slot
    mine_valid = valid[first + 1, :, cell : cell + inner].astype(jnp.float32)
    real = jnp.transpose(jnp.broadcast_to(mine_valid, (HDIM, inner)))

    def attend(out, head, over_t, over_h):
        lanes = slice(head * HDIM, (head + 1) * HDIM)
        seen = (3 if over_h else 1) * cell
        mask = band[meta[3 * (member * OWN_HEADS + head) + 2], :, :seen]
        ones = jnp.ones((seen, HDIM), jnp.bfloat16)
        for tile in range(inner // cell):
            rows = pl.ds((tile + (0 if over_h else 1)) * cell, seen)
            mine = query[0, 0, pl.ds(tile * cell, cell), lanes]
            total = None
            for near_step in (0, 1, 2) if over_t else (1,):
                scores = lax.dot_general(
                    mine,
                    cells[slot + near_step, 0, rows, lanes],
                    (((1,), (1,)), ((), ())),
                    preferred_element_type=jnp.float32,
                )
                start = (tile + (0 if over_h else 1)) * cell
                allowed = mask * valid[first + near_step, :, start : start + seen]
                terms = jnp.exp2(scores * scale).astype(jnp.bfloat16) * allowed
                both = jnp.concatenate([cells[slot + near_step, 1, rows, lanes], ones], axis=1)
                part = jnp.dot(terms, both, preferred_element_type=jnp.float32)
                total = part if total is None else total + part
            here = real[tile * cell : (tile + 1) * cell] > 0
            weight = jnp.where(here, total[:, HDIM:], 1.0)
            result = jnp.where(here, total[:, :HDIM] / weight, 0.0)
            out[0, pl.ds(tile * cell, cell), lanes] = result.astype(out.dtype)

    for head in range(OWN_HEADS):
        reach_t, reach_h = (meta[3 * (member * OWN_HEADS + head) + i] for i in range(2))
        for over_t in (False, True):
            for over_h in (False, True):
                pl.when(((reach_t > 0) == over_t) & ((reach_h > 0) == over_h))(
                    functools.partial(attend, result_cells, head, over_t, over_h)
                )

    pl.when(step < near)(lambda: out_first.__setitem__(0, result_cells[0]))
    pl.when(step >= near)(lambda: out_second.__setitem__(0, result_cells[0]))


def attend(meta, query, near_set, far_set, borders, valid, far):
    _, chip_frames, cell, _ = near_set[0].shape
    inner = 2 * cell
    span = 4 * cell
    near = chip_frames // CORES
    sets = (*far_set, *near_set) if far else (*near_set, *far_set)
    parts = [*sets, *(p for pair in borders for p in pair)]
    chip = lambda m: 1 - m[PAIR] if far else m[PAIR]
    frame = lambda f, m: chip(m) * chip_frames + (f ^ (near * m[CORE]))
    piece = jax.ShapeDtypeStruct((near, inner, SPAN), jnp.bfloat16)
    return pl.pallas_call(
        functools.partial(
            attend_body, near=near, far=far, sides=len(borders), cell=cell, inner=inner
        ),
        grid_spec=pltpu.PrefetchScalarGridSpec(
            num_scalar_prefetch=1,
            grid=(chip_frames,),
            in_specs=[
                pl.BlockSpec((1, 1, inner, SPAN), lambda f, m: (0, frame(f, m), 0, 0)),
                *[pl.BlockSpec(memory_space=pl.ANY)] * len(parts),
                pl.BlockSpec(memory_space=pltpu.VMEM),
            ],
            out_specs=[
                pl.BlockSpec((1, inner, SPAN), lambda f, m: (jnp.minimum(f, near - 1), 0, 0)),
                pl.BlockSpec((1, inner, SPAN), lambda f, m: (jnp.maximum(f - near, 0), 0, 0)),
            ],
            scratch_shapes=[
                pltpu.VMEM((chip_frames + 2, 2, span, SPAN), jnp.bfloat16),
                pltpu.VMEM((3, cell, 3 * cell), jnp.bfloat16),
                pltpu.SemaphoreType.DMA((chip_frames + 2,)),
                pltpu.VMEM((1, inner, SPAN), jnp.bfloat16),
            ],
        ),
        out_shape=[piece, piece],
        compiler_params=pltpu.CompilerParams(vmem_limit_bytes=24 * MIB),
        cost_estimate=pl.CostEstimate(
            flops=OWN_HEADS * chip_frames * inner * 9 * cell * HDIM * 6,
            bytes_accessed=4 * SPAN * (chip_frames + 2) * span + 4 * SPAN * chip_frames * inner,
            transcendentals=OWN_HEADS * chip_frames * inner * 9 * cell,
        ),
    )(meta, query, *parts, valid)


def collect_body(member, *rest):
    out = rest[-1]
    for flip, piece in enumerate(rest[:-1]):
        column = pl.multiple_of((member[0] ^ flip) * SPAN, SPAN)
        out[:, pl.ds(column, SPAN)] = piece[...]


def collect(member, pieces):
    rows = pieces[0].shape[0]
    whole = pl.BlockSpec((rows, SPAN), lambda i, m: (0, 0))
    return pl.pallas_call(
        collect_body,
        grid_spec=pltpu.PrefetchScalarGridSpec(
            num_scalar_prefetch=1,
            grid=(1,),
            in_specs=[whole] * MATES,
            out_specs=pl.BlockSpec((rows, HEADS * HDIM), lambda i, m: (0, 0)),
        ),
        out_shape=jax.ShapeDtypeStruct((rows, HEADS * HDIM), jnp.bfloat16),
        compiler_params=pltpu.CompilerParams(vmem_limit_bytes=24 * MIB),
    )(member.reshape(1), *pieces)


def gather_blocks(pieces, spots, member):
    blocks = lax.all_gather(pieces, ("rest", "height"))
    blocks = blocks.reshape(-1, *blocks.shape[2:])
    if blocks.shape[1] % 16:
        places = jnp.stack([base + (member ^ flip) * step for base, flip, step in spots])
        ordered = jnp.zeros_like(blocks).at[places].set(blocks)
        return ordered.reshape(1, -1, blocks.shape[2]), ((0, 0, 0),)
    return blocks, spots


def per_device(tokens, mod_scale, mod_shift, w_qkv, q_gain, k_gain, window, valid):
    frames, rows, width, features = tokens.shape
    count = frames * rows * width
    inner = rows * width
    model = w_qkv.shape[1] // 3
    rest, pair, core, height = (lax.axis_index(a) for a in ("rest", "pair", "core", "height"))
    member = pair * CORES + core
    high = lax.axis_size("height")
    many = lax.axis_size("rest")
    r_odd = rest % 2

    def columns_of(mate):
        return jnp.concatenate(
            [lax.dynamic_slice_in_dim(w_qkv, s * model + mate * SPAN, SPAN, axis=1) for s in range(3)], axis=1
        )

    shares = [columns_of(member)] + [swap(columns_of(member ^ flip), TEAM, flip) for flip in range(1, MATES)]
    stacked = jnp.stack(shares)
    kv_share, q_share = stacked[:, :, SPAN:], stacked[:, :, :SPAN]
    flat = tokens.reshape(count, features)
    mine = [modulate(flat, mod_scale, mod_shift, 0, inner)]
    kv_share, q_share, scale_after, mine[0] = lax.optimization_barrier((kv_share, q_share, mod_scale, mine[0]))
    mine += [modulate(flat, scale_after, mod_shift, f * inner, inner) for f in range(1, frames)]

    meta = jnp.concatenate(
        [window.reshape(-1), jnp.stack([member, pair, core, height % 2, r_odd]).astype(jnp.int32)]
    )
    total_frames = MATES * frames
    valid_pad = jnp.pad(valid, ((TT, TT), (TH, TH), (0, 0)))
    around = lax.dynamic_slice(
        valid_pad,
        (rest * total_frames, height * rows, jnp.int32(0)),
        (total_frames + 2 * TT, rows + 2 * TH, width),
    )
    seen = (around > 0).astype(jnp.bfloat16).reshape(total_frames + 2 * TT, 1, -1)
    mine[-1], meta, seen = lax.optimization_barrier((mine[-1], meta, seen))

    spots = tuple(
        (r * MATES * high + h, j, high) for r in range(many) for h in range(high) for j in range(MATES)
    )
    kv_blocks, kv_spots = gather_blocks(kv_share, spots, member)
    q_blocks, q_spots = gather_blocks(q_share, spots, member)

    across = [swap(x, "pair", 1) for x in mine]
    beside = [swap(x, "core", 1) for x in mine]

    def cells_of(sources):
        return project(meta, sources, kv_blocks, kv_spots, k_gain, 2, 1, True)

    def exchanged(even, odd):
        return (even, odd, swap_neighbours(even, "height", 0), swap_neighbours(odd, "height", 1))

    even, odd = cells_of([*mine, *beside])
    even, odd, across[-1] = lax.optimization_barrier((even, odd, across[-1]))
    near_set = exchanged(even, odd)
    beyond = [swap(x, "core", 1) for x in across]
    even, odd = cells_of([*across, *beyond])
    even, odd, q_blocks, *near_back = lax.optimization_barrier((even, odd, q_blocks, *near_set[2:]))
    near_set = (*near_set[:2], *near_back)
    far_set = exchanged(even, odd)
    (query,) = project(meta, [*mine, *beside, *across, *beyond], q_blocks, q_spots, q_gain, 1, 1, False)
    query, *far_back = lax.optimization_barrier((query, *far_set[2:]))
    far_set = (*far_set[:2], *far_back)

    def border(odd):
        last = r_odd == odd
        chosen = jnp.where(last, 1, 0) == pair
        cells = [
            jnp.where(
                chosen,
                jnp.where(last, a[:, -1], a[:, 0]),
                jnp.where(last, b[:, -1], b[:, 0]),
            )
            for a, b in zip(near_set, far_set)
        ]
        return (
            swap_neighbours(jnp.stack(cells[:2]), "rest", odd),
            swap_neighbours(jnp.stack(cells[2:]), "rest", odd),
        )

    borders = [border(odd) for odd in range(min(2, many - 1))]
    far_out = attend(meta, query, near_set, far_set, borders, seen, True)
    meta, *far_out = lax.optimization_barrier((meta, *far_out))
    travelled = [swap(out.reshape(count, SPAN), TEAM, CORES + flip) for flip, out in enumerate(far_out)]
    near_out = attend(meta, query, near_set, far_set, borders, seen, False)
    other, *travelled = lax.optimization_barrier((near_out[1], *travelled))
    pieces = [near_out[0].reshape(count, SPAN), swap(other.reshape(count, SPAN), TEAM, 1), *travelled]
    return collect(member.astype(jnp.int32), pieces).reshape(frames, rows, width, model)


def solution(mesh):
    split = Mesh(
        mesh.devices.reshape(mesh.shape["tm"] // MATES, MATES // CORES, CORES, mesh.shape["height"]),
        ("rest", "pair", "core", "height"),
    )
    along = ("rest", "pair", "core")
    in_specs = (
        P(along, "height", None, None),
        P(),
        P(),
        P((*along, "height"), None),
        P(),
        P(),
        P(),
        P(),
    )
    out_specs = P(along, "height", None, None)
    return jax.shard_map(
        per_device, mesh=split, in_specs=in_specs, out_specs=out_specs, check_vma=False
    )
```

```python
import functools

import jax
import jax.numpy as jnp
import numpy as np
from jax import lax
from jax.experimental import pallas as pl
from jax.experimental.pallas import tpu as pltpu
from jax.sharding import Mesh
from jax.sharding import PartitionSpec as P

HDIM = 128
HEADS = 12
TT = 1
TH = 2
TW = 8
CORES = 2
MATES = 4
OWN_HEADS = HEADS // MATES
SPAN = OWN_HEADS * HDIM
EPS = 1e-06
MIB = 1024 * 1024
TEAM = ("pair", "core")

MEMBER, PAIR, CORE, Z_ODD, R_ODD, REST, HEIGHT = (3 * HEADS + i for i in range(7))


def swap(x, axis, flip):
    names = axis if isinstance(axis, tuple) else (axis,)
    count = int(np.prod([lax.axis_size(name) for name in names]))
    return lax.ppermute(x, axis, [(i, i ^ flip) for i in range(count)])


def swap_neighbours(x, axis, odd):
    count = lax.axis_size(axis)
    pairs = [(i, i + 1) for i in range(odd, count - 1, 2)]
    flat = x.reshape(-1, x.shape[-1])
    return lax.ppermute(flat, axis, pairs + [(j, i) for i, j in pairs]).reshape(x.shape)


def modulate_body(tokens, scale, shift, out):
    values = tokens[...].astype(jnp.float32)
    centred = values - jnp.mean(values, axis=-1, keepdims=True)
    variance = jnp.mean(centred * centred, axis=-1, keepdims=True)
    normed = centred * lax.rsqrt(variance + EPS)
    out[...] = (normed * (1.0 + scale[...]) + shift[...]).astype(out.dtype)


def modulate(tokens, scale, shift, first, count, block):
    features = tokens.shape[1]
    row = lambda start: pl.BlockSpec((block, features), lambda i: (start // block + i, 0))
    whole = pl.BlockSpec((1, features), lambda i: (0, 0))
    return pl.pallas_call(
        modulate_body,
        grid=(count // block,),
        in_specs=[row(first), whole, whole],
        out_specs=row(0),
        out_shape=jax.ShapeDtypeStruct((count, features), jnp.bfloat16),
        compiler_params=pltpu.CompilerParams(vmem_limit_bytes=24 * MIB),
        cost_estimate=pl.CostEstimate(
            flops=12 * count * features, bytes_accessed=4 * count * features, transcendentals=0
        ),
    )(tokens, scale.reshape(1, features), shift.reshape(1, features))


def project_body(meta, *rest, sources, members, frames, arrays, depth, spots, normed, halves):
    xs, blocks, gain = rest[:sources], rest[sources : sources + arrays], rest[sources + arrays]
    outs, (rows, weights, row_sems, weight_sems) = rest[sources + arrays + 1 : -4], rest[-4:]
    columns = weights.shape[1]
    count = rows.shape[0] // members
    inner = count // frames
    cell = inner // 2
    each = sources // members

    loads, first = [], 0
    for i, x in enumerate(xs):
        loads.append(pltpu.make_async_copy(x, rows.at[pl.ds(first, x.shape[0]), :], row_sems.at[i]))
        first += x.shape[0]
    copies = []
    for p, spot in enumerate(spots):
        place = 0
        if spot is not None:
            e, j, d, high = spot
            place = ((meta[REST] ^ e) * MATES + (meta[MEMBER] ^ j)) * high + (meta[HEIGHT] ^ d)
        held = len(spots) // arrays
        source = blocks[p // held].at[pl.ds(p % held * depth, depth), :]
        row = pl.multiple_of(place * depth, depth)
        copies.append(pltpu.make_async_copy(source, weights.at[pl.ds(row, depth), :], weight_sems.at[p]))
    for load in loads[:each]:
        load.start()
    for copy in copies:
        copy.start()
    for load in loads[each:]:
        load.start()
    for copy in copies:
        copy.wait()
    wide = 2 * HDIM
    for i in range(members):
        for load in loads[i * each : (i + 1) * each]:
            load.wait()
        for start in range(0, columns, wide):
            stop = min(start + wide, columns)
            total = jnp.dot(
                rows[i * count : (i + 1) * count, :], weights[:, start:stop], preferred_element_type=jnp.float32
            )
            for column in range(start, stop, HDIM):
                head = total[:, column - start : column - start + HDIM]
                part, offset = divmod(column, SPAN)
                if part < normed:
                    power = jnp.mean(head * head, axis=-1, keepdims=True)
                    head = head * lax.rsqrt(power + EPS) * gain[...]
                head = head.astype(jnp.bfloat16)
                lanes = slice(offset, offset + HDIM)
                for frame in range(frames):
                    place = (meta[CORE if halves else MEMBER] ^ i) * frames + frame
                    one = head[frame * inner : (frame + 1) * inner]
                    if halves:
                        top, bottom = one[:cell], one[cell:]
                        odd = meta[Z_ODD] == 1
                        outs[0][part, place, :, lanes] = jnp.where(odd, top, bottom)
                        outs[1][part, place, :, lanes] = jnp.where(odd, bottom, top)
                    else:
                        outs[0][part, place, :, lanes] = one


def project(meta, sources, members, frames, blocks, spots, gain, parts, normed, halves):
    features = sources[0].shape[1]
    total = sum(x.shape[0] for x in sources)
    inner = total // members // frames
    columns = blocks[0].shape[1]
    count = len(sources)
    any_space = pl.BlockSpec(memory_space=pl.ANY)
    vmem = pl.BlockSpec(memory_space=pltpu.VMEM)
    outs = 2 if halves else 1
    return pl.pallas_call(
        functools.partial(
            project_body,
            sources=count,
            members=members,
            frames=frames,
            arrays=len(blocks),
            depth=features // len(spots),
            spots=spots,
            normed=normed,
            halves=halves,
        ),
        grid_spec=pltpu.PrefetchScalarGridSpec(
            num_scalar_prefetch=1,
            grid=(),
            in_specs=[any_space] * (count + len(blocks)) + [vmem],
            out_specs=[vmem] * outs,
            scratch_shapes=[
                pltpu.VMEM((total, features), jnp.bfloat16),
                pltpu.VMEM((features, columns), jnp.bfloat16),
                pltpu.SemaphoreType.DMA((count,)),
                pltpu.SemaphoreType.DMA((len(spots),)),
            ],
        ),
        out_shape=[jax.ShapeDtypeStruct((parts, members * frames, inner // outs, SPAN), jnp.bfloat16)] * outs,
        compiler_params=pltpu.CompilerParams(vmem_limit_bytes=32 * MIB),
        cost_estimate=pl.CostEstimate(
            flops=2 * total * features * columns,
            bytes_accessed=2 * features * columns + 2 * total * (features + columns),
            transcendentals=0,
        ),
    )(meta, *sources, *blocks, gain.reshape(1, HDIM))


def attend_body(meta, *rest, near, far, sides, cell, inner):
    query, main = rest[0], rest[1:-7]
    valid, out_first, out_second, cells, band, sems, result_cells = rest[-7:]
    step = pl.program_id(0)
    member, pair, core, z_odd, r_odd = (meta[i] for i in (MEMBER, PAIR, CORE, Z_ODD, R_ODD))
    chip = 1 - pair if far else pair
    width = cell // TH
    frames = cells.shape[0] - 2

    row_of = [jnp.where(z_odd == 1, a, b) * cell for a, b in ((1, 2), (2, 1), (0, 3), (3, 0))]
    own_set, other_set, borders = main[0:4], main[4:8], main[8:]
    own_frame = lambda i: tuple(part.at[:, i] for part in own_set)
    other_frame = lambda i: tuple(part.at[:, i] for part in other_set)

    def load(slot, parts):
        for part, row in zip(parts, row_of):
            rows = pl.ds(pl.multiple_of(row, cell), cell)
            pltpu.make_async_copy(part, cells.at[slot, :, rows, :], sems.at[slot]).start()

    def await_slot(slot):
        pltpu.make_async_copy(cells.at[slot], cells.at[slot], sems.at[slot]).wait()

    def border(side):
        sent, received = borders[2 * side : 2 * side + 2]
        return sent.at[0], sent.at[1], received.at[0], received.at[1]

    @pl.when(step == 0)
    def _():
        for end, slot in ((0, 0), (1, frames + 1)):

            @pl.when(chip != end)
            def _():
                load(slot, other_frame(0 if end else frames - 1))

            @pl.when(chip == end)
            def _():
                for side in range(sides):
                    pl.when((r_odd == 1) == (end == side))(functools.partial(load, slot, border(side)))

                if sides < 2:

                    @pl.when((r_odd == 1) == (end == 1))
                    def _():
                        cells[slot] = jnp.zeros(cells.shape[1:], cells.dtype)

        for index in range(frames):
            load(index + 1, own_frame(index))
        q_tile = lax.broadcasted_iota(jnp.int32, (cell, 3 * cell), 0)
        k_tile = lax.broadcasted_iota(jnp.int32, (cell, 3 * cell), 1)
        apart = jnp.abs(lax.rem(q_tile, width) // TW - lax.rem(k_tile, width) // TW)
        for reach in range(3):
            band[reach] = jnp.where(apart <= reach, 1.0, 0.0).astype(band.dtype)

    def await_end(slot, end):
        empty = (chip == end) & ((r_odd == 1) == (end == 1)) if sides < 2 else False
        pl.when(jnp.logical_not(empty))(functools.partial(await_slot, slot))

    low, top = (lambda: await_end(0, 0)), (lambda: await_end(frames + 1, 1))

    @pl.when(step == 0)
    def _():
        for slot in range(near, near + 2):
            await_slot(slot)

    def await_side(lower):
        if lower:
            low()
            for slot in range(1, near):
                await_slot(slot)
        else:
            for slot in range(near + 2, frames + 1):
                await_slot(slot)
            top()

    for at, first_core in ((0, 0), (near, 1)):
        pl.when((step == at) & (core == first_core))(functools.partial(await_side, True))
        pl.when((step == at) & (core != first_core))(functools.partial(await_side, False))

    slot = step ^ (near * core)
    scale = np.float32(np.log2(np.e) / np.sqrt(HDIM))
    first = chip * frames + slot
    mine_valid = valid[first + 1, :, cell : cell + inner].astype(jnp.float32)
    real = jnp.transpose(jnp.broadcast_to(mine_valid, (HDIM, inner)))

    def attend(out, head, over_t, over_h):
        lanes = slice(head * HDIM, (head + 1) * HDIM)
        seen = (3 if over_h else 1) * cell
        mask = band[meta[3 * (member * OWN_HEADS + head) + 2], :, :seen]
        ones = jnp.ones((seen, HDIM), jnp.bfloat16)
        for tile in range(inner // cell):
            rows = pl.ds((tile + (0 if over_h else 1)) * cell, seen)
            mine = query[0, 0, pl.ds(tile * cell, cell), lanes]
            total = None
            for near_step in (0, 1, 2) if over_t else (1,):
                scores = lax.dot_general(
                    mine,
                    cells[slot + near_step, 0, rows, lanes],
                    (((1,), (1,)), ((), ())),
                    preferred_element_type=jnp.float32,
                )
                start = (tile + (0 if over_h else 1)) * cell
                allowed = mask * valid[first + near_step, :, start : start + seen]
                terms = jnp.exp2(scores * scale).astype(jnp.bfloat16) * allowed
                both = jnp.concatenate([cells[slot + near_step, 1, rows, lanes], ones], axis=1)
                part = jnp.dot(terms, both, preferred_element_type=jnp.float32)
                total = part if total is None else total + part
            here = real[tile * cell : (tile + 1) * cell] > 0
            weight = jnp.where(here, total[:, HDIM:], 1.0)
            result = jnp.where(here, total[:, :HDIM] / weight, 0.0)
            out[0, pl.ds(tile * cell, cell), lanes] = result.astype(out.dtype)

    for head in range(OWN_HEADS):
        reach_t, reach_h = (meta[3 * (member * OWN_HEADS + head) + i] for i in range(2))
        for over_t in (False, True):
            for over_h in (False, True):
                pl.when(((reach_t > 0) == over_t) & ((reach_h > 0) == over_h))(
                    functools.partial(attend, result_cells, head, over_t, over_h)
                )

    pl.when(step < near)(lambda: out_first.__setitem__(0, result_cells[0]))
    pl.when(step >= near)(lambda: out_second.__setitem__(0, result_cells[0]))


def attend(meta, query, near_set, far_set, borders, valid, far):
    _, chip_frames, cell, _ = near_set[0].shape
    inner = 2 * cell
    span = 4 * cell
    near = chip_frames // CORES
    sets = (*far_set, *near_set) if far else (*near_set, *far_set)
    parts = [*sets, *(p for pair in borders for p in pair)]
    chip = lambda m: 1 - m[PAIR] if far else m[PAIR]
    frame = lambda f, m: chip(m) * chip_frames + (f ^ (near * m[CORE]))
    piece = jax.ShapeDtypeStruct((near, inner, SPAN), jnp.bfloat16)
    return pl.pallas_call(
        functools.partial(
            attend_body, near=near, far=far, sides=len(borders), cell=cell, inner=inner
        ),
        grid_spec=pltpu.PrefetchScalarGridSpec(
            num_scalar_prefetch=1,
            grid=(chip_frames,),
            in_specs=[
                pl.BlockSpec((1, 1, inner, SPAN), lambda f, m: (0, frame(f, m), 0, 0)),
                *[pl.BlockSpec(memory_space=pl.ANY)] * len(parts),
                pl.BlockSpec(memory_space=pltpu.VMEM),
            ],
            out_specs=[
                pl.BlockSpec((1, inner, SPAN), lambda f, m: (jnp.minimum(f, near - 1), 0, 0)),
                pl.BlockSpec((1, inner, SPAN), lambda f, m: (jnp.maximum(f - near, 0), 0, 0)),
            ],
            scratch_shapes=[
                pltpu.VMEM((chip_frames + 2, 2, span, SPAN), jnp.bfloat16),
                pltpu.VMEM((3, cell, 3 * cell), jnp.bfloat16),
                pltpu.SemaphoreType.DMA((chip_frames + 2,)),
                pltpu.VMEM((1, inner, SPAN), jnp.bfloat16),
            ],
        ),
        out_shape=[piece, piece],
        compiler_params=pltpu.CompilerParams(vmem_limit_bytes=24 * MIB),
        cost_estimate=pl.CostEstimate(
            flops=OWN_HEADS * chip_frames * inner * 9 * cell * HDIM * 6,
            bytes_accessed=4 * SPAN * (chip_frames + 2) * span + 4 * SPAN * chip_frames * inner,
            transcendentals=OWN_HEADS * chip_frames * inner * 9 * cell,
        ),
    )(meta, query, *parts, valid)


def collect_body(member, *rest):
    out = rest[-1]
    for flip, piece in enumerate(rest[:-1]):
        column = pl.multiple_of((member[0] ^ flip) * SPAN, SPAN)
        out[:, pl.ds(column, SPAN)] = piece[...]


def collect(member, pieces):
    rows = pieces[0].shape[0]
    whole = pl.BlockSpec((rows, SPAN), lambda i, m: (0, 0))
    return pl.pallas_call(
        collect_body,
        grid_spec=pltpu.PrefetchScalarGridSpec(
            num_scalar_prefetch=1,
            grid=(1,),
            in_specs=[whole] * MATES,
            out_specs=pl.BlockSpec((rows, HEADS * HDIM), lambda i, m: (0, 0)),
        ),
        out_shape=jax.ShapeDtypeStruct((rows, HEADS * HDIM), jnp.bfloat16),
        compiler_params=pltpu.CompilerParams(vmem_limit_bytes=24 * MIB),
    )(member.reshape(1), *pieces)


def gather_lines(share):
    return [share] + [swap(share, "height", d) for d in range(1, lax.axis_size("height"))]


def gather_blocks(lines, spots, places):
    blocks = list(lines)
    for e in range(1, lax.axis_size("rest")):
        blocks += [swap(line, "rest", e) for line in lines]
    depth = lines[0].shape[0] // MATES
    if depth % 16:
        pieces = jnp.concatenate(blocks, axis=0).reshape(-1, depth, lines[0].shape[1])
        ordered = jnp.zeros_like(pieces).at[jnp.stack(places)].set(pieces)
        return [ordered.reshape(-1, pieces.shape[2])], (None,)
    return blocks, spots


def per_device(tokens, mod_scale, mod_shift, w_qkv, q_gain, k_gain, window, valid):
    frames, rows, width, features = tokens.shape
    count = frames * rows * width
    inner = rows * width
    model = w_qkv.shape[1] // 3
    rest, pair, core, height = (lax.axis_index(a) for a in ("rest", "pair", "core", "height"))
    member = pair * CORES + core
    high = lax.axis_size("height")
    many = lax.axis_size("rest")
    r_odd = rest % 2

    def columns_of(mate):
        return jnp.concatenate(
            [lax.dynamic_slice_in_dim(w_qkv, s * model + mate * SPAN, SPAN, axis=1) for s in range(3)], axis=1
        )

    shares = [columns_of(member)] + [swap(columns_of(member ^ flip), TEAM, flip) for flip in range(1, MATES)]
    stacked = jnp.concatenate(shares, axis=0)
    kv_share, q_share = stacked[:, SPAN:], stacked[:, :SPAN]
    flat = tokens.reshape(count, features)
    cut = count * 5 // 8 // width * width
    mine = [
        modulate(flat, mod_scale, mod_shift, 0, cut, width),
        modulate(flat, mod_scale, mod_shift, cut, count - cut, width),
    ]
    mine[0], kv_share, q_share = lax.optimization_barrier((mine[0], kv_share, q_share))

    meta = jnp.concatenate(
        [
            window.reshape(-1),
            jnp.stack([member, pair, core, height % 2, r_odd, rest, height]).astype(jnp.int32),
        ]
    )
    total_frames = MATES * frames
    valid_pad = jnp.pad(valid, ((TT, TT), (TH, TH), (0, 0)))
    around = lax.dynamic_slice(
        valid_pad,
        (rest * total_frames, height * rows, jnp.int32(0)),
        (total_frames + 2 * TT, rows + 2 * TH, width),
    )
    seen = (around > 0).astype(jnp.bfloat16).reshape(total_frames + 2 * TT, 1, -1)

    spots, places = [], []
    for e in range(many):
        for d in range(high):
            for j in range(MATES):
                spots.append((e, j, d, high))
                places.append(((rest ^ e) * MATES + (member ^ j)) * high + (height ^ d))
    kv_lines = gather_lines(kv_share)
    q_share, kv_lines[-1] = lax.optimization_barrier((q_share, kv_lines[-1]))
    kv_blocks, kv_spots = gather_blocks(kv_lines, tuple(spots), places)

    across = [swap(mine[0], "pair", 1)]
    held = kv_blocks[: 2 * high - 1]
    across[0], meta, seen, mates, held = lax.optimization_barrier((across[0], meta, seen, mine, held))
    kv_blocks[: 2 * high - 1] = held
    across.append(swap(mates[1], "pair", 1))
    beside = [swap(x, "core", 1) for x in mates]
    q_lines = gather_lines(q_share)
    kv_blocks[0], q_lines = lax.optimization_barrier((kv_blocks[0], q_lines))
    q_blocks, q_spots = gather_blocks(q_lines, tuple(spots), places)

    def cells_of(sources):
        return project(meta, sources, CORES, frames, kv_blocks, kv_spots, k_gain, 2, 1, True)

    def exchanged(even, odd):
        return (even, odd, swap_neighbours(even, "height", 0), swap_neighbours(odd, "height", 1))

    even, odd = cells_of([*mine, *beside])
    even, odd, across[-1] = lax.optimization_barrier((even, odd, across[-1]))
    near_set = exchanged(even, odd)
    beyond = [swap(x, "core", 1) for x in across]
    even, odd = cells_of([*across, *beyond])
    even, odd, *near_back = lax.optimization_barrier((even, odd, *near_set[2:]))
    near_set = (*near_set[:2], *near_back)
    far_set = exchanged(even, odd)
    q_blocks[0], even = lax.optimization_barrier((q_blocks[0], even))
    far_set = (even, *far_set[1:])
    everyone = [*mine, *beside, *across, *beyond]
    (query,) = project(meta, everyone, MATES, frames, q_blocks, q_spots, q_gain, 1, 1, False)
    query, *far_back = lax.optimization_barrier((query, *far_set[2:]))
    far_set = (*far_set[:2], *far_back)

    def border(odd):
        last = r_odd == odd
        chosen = jnp.where(last, 1, 0) == pair
        cells = [
            jnp.where(
                chosen,
                jnp.where(last, a[:, -1], a[:, 0]),
                jnp.where(last, b[:, -1], b[:, 0]),
            )
            for a, b in zip(near_set, far_set)
        ]
        return (
            swap_neighbours(jnp.stack(cells[:2]), "rest", odd),
            swap_neighbours(jnp.stack(cells[2:]), "rest", odd),
        )

    borders = [border(odd) for odd in range(min(2, many - 1))]
    far_out = attend(meta, query, near_set, far_set, borders, seen, True)
    meta, *far_out = lax.optimization_barrier((meta, *far_out))
    travelled = [swap(out.reshape(count, SPAN), TEAM, CORES + flip) for flip, out in enumerate(far_out)]
    near_out = attend(meta, query, near_set, far_set, borders, seen, False)
    other, *travelled = lax.optimization_barrier((near_out[1], *travelled))
    pieces = [near_out[0].reshape(count, SPAN), swap(other.reshape(count, SPAN), TEAM, 1), *travelled]
    return collect(member.astype(jnp.int32), pieces).reshape(frames, rows, width, model)


def solution(mesh):
    split = Mesh(
        mesh.devices.reshape(mesh.shape["tm"] // MATES, MATES // CORES, CORES, mesh.shape["height"]),
        ("rest", "pair", "core", "height"),
    )
    along = ("rest", "pair", "core")
    in_specs = (
        P(along, "height", None, None),
        P(),
        P(),
        P((*along, "height"), None),
        P(),
        P(),
        P(),
        P(),
    )
    out_specs = P(along, "height", None, None)
    return jax.shard_map(
        per_device, mesh=split, in_specs=in_specs, out_specs=out_specs, check_vma=False
    )
```

```python
import functools

import jax
import jax.numpy as jnp
import numpy as np
from jax import lax
from jax.experimental import pallas as pl
from jax.experimental.pallas import tpu as pltpu
from jax.sharding import Mesh
from jax.sharding import PartitionSpec as P

HDIM = 128
HEADS = 12
TT = 1
TH = 2
TW = 8
CORES = 2
MATES = 4
OWN_HEADS = HEADS // MATES
SPAN = OWN_HEADS * HDIM
EPS = 1e-06
MIB = 1024 * 1024
TEAM = ("pair", "core")

MEMBER, PAIR, CORE, Z_ODD, R_ODD, REST, HEIGHT = (3 * HEADS + i for i in range(7))


def swap(x, axis, flip):
    names = axis if isinstance(axis, tuple) else (axis,)
    count = int(np.prod([lax.axis_size(name) for name in names]))
    return lax.ppermute(x, axis, [(i, i ^ flip) for i in range(count)])


def swap_neighbours(x, axis, odd):
    count = lax.axis_size(axis)
    pairs = [(i, i + 1) for i in range(odd, count - 1, 2)]
    flat = x.reshape(-1, x.shape[-1])
    return lax.ppermute(flat, axis, pairs + [(j, i) for i, j in pairs]).reshape(x.shape)


def modulate_body(tokens, scale, shift, out):
    values = tokens[...].astype(jnp.float32)
    centred = values - jnp.mean(values, axis=-1, keepdims=True)
    variance = jnp.mean(centred * centred, axis=-1, keepdims=True)
    normed = centred * lax.rsqrt(variance + EPS)
    out[...] = (normed * (1.0 + scale[...]) + shift[...]).astype(out.dtype)


def modulate(tokens, scale, shift, first, count, block):
    features = tokens.shape[1]
    row = lambda start: pl.BlockSpec((block, features), lambda i: (start // block + i, 0))
    whole = pl.BlockSpec((1, features), lambda i: (0, 0))
    return pl.pallas_call(
        modulate_body,
        grid=(count // block,),
        in_specs=[row(first), whole, whole],
        out_specs=row(0),
        out_shape=jax.ShapeDtypeStruct((count, features), jnp.bfloat16),
        compiler_params=pltpu.CompilerParams(vmem_limit_bytes=12 * MIB),
        cost_estimate=pl.CostEstimate(
            flops=12 * count * features, bytes_accessed=4 * count * features, transcendentals=0
        ),
    )(tokens, scale.reshape(1, features), shift.reshape(1, features))


def project_body(meta, *rest, sources, members, frames, arrays, depth, spots, normed, halves):
    xs, blocks, gain = rest[:sources], rest[sources : sources + arrays], rest[sources + arrays]
    outs, (rows, weights, row_sems, weight_sems) = rest[sources + arrays + 1 : -4], rest[-4:]
    columns = weights.shape[1]
    count = rows.shape[0] // members
    inner = count // frames
    cell = inner // 2
    each = sources // members

    loads, first = [], 0
    for i, x in enumerate(xs):
        loads.append(pltpu.make_async_copy(x, rows.at[pl.ds(first, x.shape[0]), :], row_sems.at[i]))
        first += x.shape[0]
    copies = []
    for p, spot in enumerate(spots):
        place = 0
        if spot is not None:
            e, j, d, high = spot
            place = ((meta[REST] ^ e) * MATES + (meta[MEMBER] ^ j)) * high + (meta[HEIGHT] ^ d)
        held = len(spots) // arrays
        source = blocks[p // held].at[pl.ds(p % held * depth, depth), :]
        row = pl.multiple_of(place * depth, depth)
        copies.append(pltpu.make_async_copy(source, weights.at[pl.ds(row, depth), :], weight_sems.at[p]))
    for load in loads[:each]:
        load.start()
    for copy in copies:
        copy.start()
    for load in loads[each:]:
        load.start()
    for copy in copies:
        copy.wait()
    wide = 2 * HDIM
    for i in range(members):
        for load in loads[i * each : (i + 1) * each]:
            load.wait()
        for start in range(0, columns, wide):
            stop = min(start + wide, columns)
            total = jnp.dot(
                rows[i * count : (i + 1) * count, :], weights[:, start:stop], preferred_element_type=jnp.float32
            )
            for column in range(start, stop, HDIM):
                head = total[:, column - start : column - start + HDIM]
                part, offset = divmod(column, SPAN)
                if part < normed:
                    power = jnp.mean(head * head, axis=-1, keepdims=True)
                    head = head * lax.rsqrt(power + EPS) * gain[...]
                head = head.astype(jnp.bfloat16)
                lanes = slice(offset, offset + HDIM)
                for frame in range(frames):
                    place = (meta[CORE if halves else MEMBER] ^ i) * frames + frame
                    one = head[frame * inner : (frame + 1) * inner]
                    if halves:
                        top, bottom = one[:cell], one[cell:]
                        odd = meta[Z_ODD] == 1
                        outs[0][part, place, :, lanes] = jnp.where(odd, top, bottom)
                        outs[1][part, place, :, lanes] = jnp.where(odd, bottom, top)
                    else:
                        outs[0][part, place, :, lanes] = one


def project(meta, sources, members, frames, blocks, spots, gain, parts, normed, halves):
    features = sources[0].shape[1]
    total = sum(x.shape[0] for x in sources)
    inner = total // members // frames
    columns = blocks[0].shape[1]
    count = len(sources)
    any_space = pl.BlockSpec(memory_space=pl.ANY)
    vmem = pl.BlockSpec(memory_space=pltpu.VMEM)
    outs = 2 if halves else 1
    return pl.pallas_call(
        functools.partial(
            project_body,
            sources=count,
            members=members,
            frames=frames,
            arrays=len(blocks),
            depth=features // len(spots),
            spots=spots,
            normed=normed,
            halves=halves,
        ),
        grid_spec=pltpu.PrefetchScalarGridSpec(
            num_scalar_prefetch=1,
            grid=(),
            in_specs=[any_space] * (count + len(blocks)) + [vmem],
            out_specs=[vmem] * outs,
            scratch_shapes=[
                pltpu.VMEM((total, features), jnp.bfloat16),
                pltpu.VMEM((features, columns), jnp.bfloat16),
                pltpu.SemaphoreType.DMA((count,)),
                pltpu.SemaphoreType.DMA((len(spots),)),
            ],
        ),
        out_shape=[jax.ShapeDtypeStruct((parts, members * frames, inner // outs, SPAN), jnp.bfloat16)] * outs,
        compiler_params=pltpu.CompilerParams(vmem_limit_bytes=24 * MIB),
        cost_estimate=pl.CostEstimate(
            flops=2 * total * features * columns,
            bytes_accessed=2 * features * columns + 2 * total * (features + columns),
            transcendentals=0,
        ),
    )(meta, *sources, *blocks, gain.reshape(1, HDIM))


def attend_body(meta, *rest, near, far, sides, cell, inner, pieces):
    count = len(pieces)
    query, main = rest[0], rest[1 : -5 - count]
    valid, outs = rest[-5 - count], rest[-4 - count : -4]
    cells, band, sems, result_cells = rest[-4:]
    step = pl.program_id(0)
    member, pair, core, z_odd, r_odd = (meta[i] for i in (MEMBER, PAIR, CORE, Z_ODD, R_ODD))
    chip = 1 - pair if far else pair
    width = cell // TH
    frames = cells.shape[0] - 2

    row_of = [jnp.where(z_odd == 1, a, b) * cell for a, b in ((1, 2), (2, 1), (0, 3), (3, 0))]
    own_set, other_set, borders = main[0:4], main[4:8], main[8:]
    own_frame = lambda i: tuple(part.at[:, i] for part in own_set)
    other_frame = lambda i: tuple(part.at[:, i] for part in other_set)

    def load(slot, parts):
        for part, row in zip(parts, row_of):
            rows = pl.ds(pl.multiple_of(row, cell), cell)
            pltpu.make_async_copy(part, cells.at[slot, :, rows, :], sems.at[slot]).start()

    def await_slot(slot):
        pltpu.make_async_copy(cells.at[slot], cells.at[slot], sems.at[slot]).wait()

    def border(side):
        frame, even, odd = borders[3 * side : 3 * side + 3]
        return frame.at[0], frame.at[1], even, odd

    first_core = core ^ pieces[0]
    low = True if count > 1 else first_core == 0
    high = True if count > 1 else first_core == 1

    @pl.when(step == 0)
    def _():
        for end, slot, used in ((0, 0, low), (1, frames + 1, high)):

            @pl.when(used & (chip != end))
            def _():
                load(slot, other_frame(0 if end else frames - 1))

            @pl.when(used & (chip == end))
            def _():
                for side in range(sides):
                    pl.when((r_odd == 1) == (end == side))(functools.partial(load, slot, border(side)))

                if sides < 2:

                    @pl.when((r_odd == 1) == (end == 1))
                    def _():
                        cells[slot] = jnp.zeros(cells.shape[1:], cells.dtype)

        for index in range(frames):
            slot = index + 1
            used = low if slot < near else high if slot > near + 1 else True
            pl.when(used)(functools.partial(load, slot, own_frame(index)))
        q_tile = lax.broadcasted_iota(jnp.int32, (cell, 3 * cell), 0)
        k_tile = lax.broadcasted_iota(jnp.int32, (cell, 3 * cell), 1)
        apart = jnp.abs(lax.rem(q_tile, width) // TW - lax.rem(k_tile, width) // TW)
        for reach in range(3):
            band[reach] = jnp.where(apart <= reach, 1.0, 0.0).astype(band.dtype)
        for slot in range(near, near + 2):
            await_slot(slot)

    def await_end(slot, end):
        empty = (chip == end) & ((r_odd == 1) == (end == 1)) if sides < 2 else False
        pl.when(jnp.logical_not(empty))(functools.partial(await_slot, slot))

    def await_side(lower):
        if lower:
            await_end(0, 0)
            for slot in range(1, near):
                await_slot(slot)
        else:
            for slot in range(near + 2, frames + 1):
                await_slot(slot)
            await_end(frames + 1, 1)

    for index in range(count):
        at = step == index * near
        pl.when(at & (first_core == index))(functools.partial(await_side, True))
        pl.when(at & (first_core != index))(functools.partial(await_side, False))

    slot = step + near * first_core if count == 1 else step ^ (near * first_core)
    scale = np.float32(np.log2(np.e) / np.sqrt(HDIM))
    first = chip * frames + slot
    mine_valid = valid[first + 1, :, cell : cell + inner].astype(jnp.float32)
    real = jnp.transpose(jnp.broadcast_to(mine_valid, (HDIM, inner)))

    def attend(out, head, over_t, over_h):
        lanes = slice(head * HDIM, (head + 1) * HDIM)
        seen = (3 if over_h else 1) * cell
        mask = band[meta[3 * (member * OWN_HEADS + head) + 2], :, :seen]
        ones = jnp.ones((seen, HDIM), jnp.bfloat16)
        for tile in range(inner // cell):
            rows = pl.ds((tile + (0 if over_h else 1)) * cell, seen)
            mine = query[0, 0, pl.ds(tile * cell, cell), lanes]
            total = None
            for near_step in (0, 1, 2) if over_t else (1,):
                scores = lax.dot_general(
                    mine,
                    cells[slot + near_step, 0, rows, lanes],
                    (((1,), (1,)), ((), ())),
                    preferred_element_type=jnp.float32,
                )
                start = (tile + (0 if over_h else 1)) * cell
                allowed = mask * valid[first + near_step, :, start : start + seen]
                terms = jnp.exp2(scores * scale).astype(jnp.bfloat16) * allowed
                both = jnp.concatenate([cells[slot + near_step, 1, rows, lanes], ones], axis=1)
                part = jnp.dot(terms, both, preferred_element_type=jnp.float32)
                total = part if total is None else total + part
            here = real[tile * cell : (tile + 1) * cell] > 0
            weight = jnp.where(here, total[:, HDIM:], 1.0)
            result = jnp.where(here, total[:, :HDIM] / weight, 0.0)
            out[0, pl.ds(tile * cell, cell), lanes] = result.astype(out.dtype)

    for head in range(OWN_HEADS):
        reach_t, reach_h = (meta[3 * (member * OWN_HEADS + head) + i] for i in range(2))
        for over_t in (False, True):
            for over_h in (False, True):
                pl.when(((reach_t > 0) == over_t) & ((reach_h > 0) == over_h))(
                    functools.partial(attend, result_cells, head, over_t, over_h)
                )

    for index, out in enumerate(outs):
        pl.when(step // near == index)(functools.partial(out.__setitem__, 0, result_cells[0]))


def attend(meta, query, near_set, far_set, borders, valid, far, pieces):
    _, chip_frames, cell, _ = near_set[0].shape
    inner = 2 * cell
    span = 4 * cell
    near = chip_frames // CORES
    sets = (*far_set, *near_set) if far else (*near_set, *far_set)
    parts = [*sets, *(p for pair in borders for p in pair)]
    chip = lambda m: 1 - m[PAIR] if far else m[PAIR]
    count = len(pieces)
    frame = lambda f, m: chip(m) * chip_frames + (m[CORE] ^ pieces[0] ^ (f // near)) * near + f % near
    piece = jax.ShapeDtypeStruct((near, inner, SPAN), jnp.bfloat16)
    return pl.pallas_call(
        functools.partial(
            attend_body, near=near, far=far, sides=len(borders), cell=cell, inner=inner, pieces=pieces
        ),
        grid_spec=pltpu.PrefetchScalarGridSpec(
            num_scalar_prefetch=1,
            grid=(near * count,),
            in_specs=[
                pl.BlockSpec((1, 1, inner, SPAN), lambda f, m: (0, frame(f, m), 0, 0)),
                *[pl.BlockSpec(memory_space=pl.ANY)] * len(parts),
                pl.BlockSpec(memory_space=pltpu.VMEM),
            ],
            out_specs=[
                pl.BlockSpec((1, inner, SPAN), lambda f, m: (jnp.minimum(f, near - 1), 0, 0)),
                pl.BlockSpec((1, inner, SPAN), lambda f, m: (jnp.maximum(f - near, 0), 0, 0)),
            ][:count],
            scratch_shapes=[
                pltpu.VMEM((chip_frames + 2, 2, span, SPAN), jnp.bfloat16),
                pltpu.VMEM((3, cell, 3 * cell), jnp.bfloat16),
                pltpu.SemaphoreType.DMA((chip_frames + 2,)),
                pltpu.VMEM((1, inner, SPAN), jnp.bfloat16),
            ],
        ),
        out_shape=[piece] * count,
        compiler_params=pltpu.CompilerParams(vmem_limit_bytes=16 * MIB),
        cost_estimate=pl.CostEstimate(
            flops=OWN_HEADS * count * near * inner * 9 * cell * HDIM * 6,
            bytes_accessed=4 * SPAN * (near * count + 2) * span + 4 * SPAN * near * count * inner,
            transcendentals=OWN_HEADS * count * near * inner * 9 * cell,
        ),
    )(meta, query, *parts, valid)


def collect_body(member, *rest):
    out = rest[-1]
    for flip, piece in enumerate(rest[:-1]):
        column = pl.multiple_of((member[0] ^ flip) * SPAN, SPAN)
        out[:, pl.ds(column, SPAN)] = piece[...]


def collect(member, pieces):
    rows = pieces[0].shape[0]
    whole = pl.BlockSpec((rows, SPAN), lambda i, m: (0, 0))
    return pl.pallas_call(
        collect_body,
        grid_spec=pltpu.PrefetchScalarGridSpec(
            num_scalar_prefetch=1,
            grid=(1,),
            in_specs=[whole] * MATES,
            out_specs=pl.BlockSpec((rows, HEADS * HDIM), lambda i, m: (0, 0)),
        ),
        out_shape=jax.ShapeDtypeStruct((rows, HEADS * HDIM), jnp.bfloat16),
        compiler_params=pltpu.CompilerParams(vmem_limit_bytes=16 * MIB),
    )(member.reshape(1), *pieces)


def gather_lines(share):
    return [share] + [swap(share, "height", d) for d in range(1, lax.axis_size("height"))]


def gather_blocks(lines, spots, places):
    blocks = list(lines)
    for e in range(1, lax.axis_size("rest")):
        blocks += [swap(line, "rest", e) for line in lines]
    depth = lines[0].shape[0] // MATES
    if depth % 16:
        pieces = jnp.concatenate(blocks, axis=0).reshape(-1, depth, lines[0].shape[1])
        ordered = jnp.zeros_like(pieces).at[jnp.stack(places)].set(pieces)
        return [ordered.reshape(-1, pieces.shape[2])], (None,)
    return blocks, spots


def per_device(tokens, mod_scale, mod_shift, w_qkv, q_gain, k_gain, window, valid):
    frames, rows, width, features = tokens.shape
    count = frames * rows * width
    inner = rows * width
    model = w_qkv.shape[1] // 3
    rest, pair, core, height = (lax.axis_index(a) for a in ("rest", "pair", "core", "height"))
    member = pair * CORES + core
    high = lax.axis_size("height")
    many = lax.axis_size("rest")
    r_odd = rest % 2

    def columns_of(mate):
        return jnp.concatenate(
            [lax.dynamic_slice_in_dim(w_qkv, s * model + mate * SPAN, SPAN, axis=1) for s in range(3)], axis=1
        )

    shares = [columns_of(member)] + [swap(columns_of(member ^ flip), TEAM, flip) for flip in range(1, MATES)]
    stacked = jnp.concatenate(shares, axis=0)
    kv_share, q_share = stacked[:, SPAN:], stacked[:, :SPAN]
    flat = tokens.reshape(count, features)
    cut = count * 5 // 8 // width * width
    mine = [
        modulate(flat, mod_scale, mod_shift, 0, cut, width),
        modulate(flat, mod_scale, mod_shift, cut, count - cut, width),
    ]
    mine[0], kv_share, q_share = lax.optimization_barrier((mine[0], kv_share, q_share))

    meta = jnp.concatenate(
        [
            window.reshape(-1),
            jnp.stack([member, pair, core, height % 2, r_odd, rest, height]).astype(jnp.int32),
        ]
    )
    total_frames = MATES * frames
    valid_pad = jnp.pad(valid, ((TT, TT), (TH, TH), (0, 0)))
    around = lax.dynamic_slice(
        valid_pad,
        (rest * total_frames, height * rows, jnp.int32(0)),
        (total_frames + 2 * TT, rows + 2 * TH, width),
    )
    seen = (around > 0).astype(jnp.bfloat16).reshape(total_frames + 2 * TT, 1, -1)

    spots, places = [], []
    for e in range(many):
        for d in range(high):
            for j in range(MATES):
                spots.append((e, j, d, high))
                places.append(((rest ^ e) * MATES + (member ^ j)) * high + (height ^ d))
    kv_lines = gather_lines(kv_share)
    q_share, kv_lines[-1] = lax.optimization_barrier((q_share, kv_lines[-1]))
    kv_blocks, kv_spots = gather_blocks(kv_lines, tuple(spots), places)

    across = [swap(mine[0], "pair", 1)]
    held = kv_blocks[: 2 * high - 1]
    across[0], meta, seen, mates, held = lax.optimization_barrier((across[0], meta, seen, mine, held))
    kv_blocks[: 2 * high - 1] = held
    across.append(swap(mates[1], "pair", 1))
    beside = [swap(x, "core", 1) for x in mates]
    q_lines = gather_lines(q_share)
    kv_blocks[0], q_lines[:3] = lax.optimization_barrier((kv_blocks[0], q_lines[:3]))
    q_blocks, q_spots = gather_blocks(q_lines, tuple(spots), places)

    def cells_of(sources):
        return project(meta, sources, CORES, frames, kv_blocks, kv_spots, k_gain, 2, 1, True)

    def exchanged(even, odd):
        return (even, odd, swap_neighbours(even, "height", 0), swap_neighbours(odd, "height", 1))

    even, odd = cells_of([*mine, *beside])
    begun = q_blocks[: high + 2]
    even, odd, across[-1], begun = lax.optimization_barrier((even, odd, across[-1], begun))
    q_blocks[: high + 2] = begun
    near_set = exchanged(even, odd)
    beyond = [swap(x, "core", 1) for x in across]
    even, odd = cells_of([*across, *beyond])
    even, odd, *near_back = lax.optimization_barrier((even, odd, *near_set[2:]))
    near_set = (*near_set[:2], *near_back)
    far_set = exchanged(even, odd)

    def border(side):
        last = r_odd == side
        chosen = jnp.where(last, 1, 0) == pair
        frame = jnp.stack(
            [
                jnp.where(
                    chosen,
                    jnp.where(last, a[:, -1], a[:, 0]),
                    jnp.where(last, b[:, -1], b[:, 0]),
                )
                for a, b in zip(near_set[:2], far_set[:2])
            ]
        )
        frame = swap_neighbours(frame, "rest", side)
        return frame, swap_neighbours(frame[0], "height", 0), swap_neighbours(frame[1], "height", 1)

    borders = [border(side) for side in range(min(2, many - 1))]
    q_blocks[0], even = lax.optimization_barrier((q_blocks[0], even))
    far_set = (even, *far_set[1:])
    everyone = [*mine, *beside, *across, *beyond]
    (query,) = project(meta, everyone, MATES, frames, q_blocks, q_spots, q_gain, 1, 1, False)
    query, *far_back = lax.optimization_barrier((query, *far_set[2:]))
    far_set = (*far_set[:2], *far_back)

    parts = (query, near_set, far_set, borders, seen)
    travelled = []
    for flip in range(CORES):
        (out,) = attend(meta, *parts, True, (flip,))
        meta, out = lax.optimization_barrier((meta, out))
        travelled.append(swap(out.reshape(count, SPAN), TEAM, CORES + flip))
    meta, travelled[0] = lax.optimization_barrier((meta, travelled[0]))
    near_out = attend(meta, *parts, False, (0, 1))
    other, *travelled = lax.optimization_barrier((near_out[1], *travelled))
    pieces = [near_out[0].reshape(count, SPAN), swap(other.reshape(count, SPAN), TEAM, 1), *travelled]
    return collect(member.astype(jnp.int32), pieces).reshape(frames, rows, width, model)


def solution(mesh):
    split = Mesh(
        mesh.devices.reshape(mesh.shape["tm"] // MATES, MATES // CORES, CORES, mesh.shape["height"]),
        ("rest", "pair", "core", "height"),
    )
    along = ("rest", "pair", "core")
    in_specs = (
        P(along, "height", None, None),
        P(),
        P(),
        P((*along, "height"), None),
        P(),
        P(),
        P(),
        P(),
    )
    out_specs = P(along, "height", None, None)
    return jax.shard_map(
        per_device, mesh=split, in_specs=in_specs, out_specs=out_specs, check_vma=False
    )
```

```python
import functools

import jax
import jax.numpy as jnp
import numpy as np
from jax import lax
from jax.experimental import pallas as pl
from jax.experimental.pallas import tpu as pltpu
from jax.sharding import Mesh
from jax.sharding import PartitionSpec as P

HDIM = 128
HEADS = 12
TT = 1
TH = 2
TW = 8
CORES = 2
MATES = 4
OWN_HEADS = HEADS // MATES
SPAN = OWN_HEADS * HDIM
EPS = 1e-06
MIB = 1024 * 1024
TEAM = ("pair", "core")

MEMBER, PAIR, CORE, Z_ODD, R_ODD, REST, HEIGHT = (3 * HEADS + i for i in range(7))


def swap(x, axis, flip):
    names = axis if isinstance(axis, tuple) else (axis,)
    count = int(np.prod([lax.axis_size(name) for name in names]))
    return lax.ppermute(x, axis, [(i, i ^ flip) for i in range(count)])


def swap_neighbours(x, axis, odd):
    count = lax.axis_size(axis)
    pairs = [(i, i + 1) for i in range(odd, count - 1, 2)]
    flat = x.reshape(-1, x.shape[-1])
    return lax.ppermute(flat, axis, pairs + [(j, i) for i, j in pairs]).reshape(x.shape)


def modulate_body(tokens, scale, shift, out):
    values = tokens[...].astype(jnp.float32)
    centred = values - jnp.mean(values, axis=-1, keepdims=True)
    variance = jnp.mean(centred * centred, axis=-1, keepdims=True)
    normed = centred * lax.rsqrt(variance + EPS)
    out[...] = (normed * (1.0 + scale[...]) + shift[...]).astype(out.dtype)


def modulate(tokens, scale, shift, first, count, block):
    features = tokens.shape[1]
    row = lambda start: pl.BlockSpec((block, features), lambda i: (start // block + i, 0))
    whole = pl.BlockSpec((1, features), lambda i: (0, 0))
    return pl.pallas_call(
        modulate_body,
        grid=(count // block,),
        in_specs=[row(first), whole, whole],
        out_specs=row(0),
        out_shape=jax.ShapeDtypeStruct((count, features), jnp.bfloat16),
        compiler_params=pltpu.CompilerParams(vmem_limit_bytes=12 * MIB),
        cost_estimate=pl.CostEstimate(
            flops=12 * count * features, bytes_accessed=4 * count * features, transcendentals=0
        ),
    )(tokens, scale.reshape(1, features), shift.reshape(1, features))


def project_body(meta, *rest, sources, members, frames, arrays, depth, spots, normed, halves):
    xs, blocks, gain = rest[:sources], rest[sources : sources + arrays], rest[sources + arrays]
    outs, weights = rest[sources + arrays + 1 : -1], rest[-1]
    columns = weights.shape[1]
    each = sources // members
    inner = sum(x.shape[0] for x in xs[:each]) // frames
    cell = inner // 2

    held = len(spots) // arrays
    for p, spot in enumerate(spots):
        place = 0
        if spot is not None:
            e, j, d, high = spot
            place = ((meta[REST] ^ e) * MATES + (meta[MEMBER] ^ j)) * high + (meta[HEIGHT] ^ d)
        row = pl.multiple_of(place * depth, depth)
        start = p % held * depth
        weights[pl.ds(row, depth), :] = blocks[p // held][start : start + depth, :]

    def store(i, first, part, lanes, head):
        at = first
        while at < first + head.shape[0]:
            frame, half, offset = at // inner, at % inner // cell, at % cell
            length = min(cell - offset, first + head.shape[0] - at)
            one = head[at - first : at - first + length]
            place = (meta[CORE if halves else MEMBER] ^ i) * frames + frame
            if halves:
                for which, out in enumerate(outs):
                    pl.when((meta[Z_ODD] == 1) == (half == which))(
                        functools.partial(
                            out.__setitem__, (part, place, slice(offset, offset + length), lanes), one
                        )
                    )
            else:
                start = half * cell + offset
                outs[0][part, place, start : start + length, lanes] = one
            at += length

    wide = 2 * HDIM
    for i in range(members):
        first = 0
        for x in xs[i * each : (i + 1) * each]:
            for start in range(0, columns, wide):
                stop = min(start + wide, columns)
                total = jnp.dot(x[...], weights[:, start:stop], preferred_element_type=jnp.float32)
                for column in range(start, stop, HDIM):
                    head = total[:, column - start : column - start + HDIM]
                    part, offset = divmod(column, SPAN)
                    if part < normed:
                        power = jnp.mean(head * head, axis=-1, keepdims=True)
                        head = head * lax.rsqrt(power + EPS) * gain[...]
                    store(i, first, part, slice(offset, offset + HDIM), head.astype(jnp.bfloat16))
            first += x.shape[0]


def project(meta, sources, members, frames, blocks, spots, gain, parts, normed, halves):
    features = sources[0].shape[1]
    total = sum(x.shape[0] for x in sources)
    inner = total // members // frames
    columns = blocks[0].shape[1]
    count = len(sources)
    vmem = pl.BlockSpec(memory_space=pltpu.VMEM)
    outs = 2 if halves else 1
    return pl.pallas_call(
        functools.partial(
            project_body,
            sources=count,
            members=members,
            frames=frames,
            arrays=len(blocks),
            depth=features // len(spots),
            spots=spots,
            normed=normed,
            halves=halves,
        ),
        grid_spec=pltpu.PrefetchScalarGridSpec(
            num_scalar_prefetch=1,
            grid=(),
            in_specs=[vmem] * (count + len(blocks) + 1),
            out_specs=[vmem] * outs,
            scratch_shapes=[pltpu.VMEM((features, columns), jnp.bfloat16)],
        ),
        out_shape=[jax.ShapeDtypeStruct((parts, members * frames, inner // outs, SPAN), jnp.bfloat16)] * outs,
        compiler_params=pltpu.CompilerParams(vmem_limit_bytes=28 * MIB),
        cost_estimate=pl.CostEstimate(
            flops=2 * total * features * columns,
            bytes_accessed=2 * features * columns + 2 * total * (features + columns),
            transcendentals=0,
        ),
    )(meta, *sources, *blocks, gain.reshape(1, HDIM))


def attend_body(meta, *rest, near, far, sides, cell, inner, pieces):
    count = len(pieces)
    query, main = rest[0], rest[1 : -4 - count]
    valid, outs = rest[-4 - count], rest[-3 - count : -3]
    cells, band, result_cells = rest[-3:]
    member, pair, core, z_odd, r_odd = (meta[i] for i in (MEMBER, PAIR, CORE, Z_ODD, R_ODD))
    chip = 1 - pair if far else pair
    width = cell // TH
    frames = cells.shape[0] - 2

    row_of = [jnp.where(z_odd == 1, a, b) * cell for a, b in ((1, 2), (2, 1), (0, 3), (3, 0))]
    own_set, other_set, borders = main[0:4], main[4:8], main[8:]
    own_frame = lambda i: tuple(part[:, i] for part in own_set)
    other_frame = lambda i: tuple(part[:, i] for part in other_set)

    def load(slot, found):
        for part, row in zip(found(), row_of):
            rows = pl.ds(pl.multiple_of(row, cell), cell)
            cells[slot, :, rows, :] = part

    def border(side):
        frame, even, odd = borders[3 * side : 3 * side + 3]
        return frame[0], frame[1], even[...], odd[...]

    low = jnp.bool_(True) if count > 1 else (core ^ pieces[0]) == 0
    high = jnp.bool_(True) if count > 1 else (core ^ pieces[0]) == 1
    for end, slot, used in ((0, 0, low), (1, frames + 1, high)):
        found = functools.partial(other_frame, 0 if end else frames - 1)
        pl.when(used & (chip != end))(functools.partial(load, slot, found))
        for side in range(sides):
            pl.when(used & (chip == end) & ((r_odd == 1) == (end == side)))(
                functools.partial(load, slot, functools.partial(border, side))
            )

        if sides < 2:

            @pl.when(used & (chip == end) & ((r_odd == 1) == (end == 1)))
            def _():
                cells[slot] = jnp.zeros(cells.shape[1:], cells.dtype)

    for index in range(frames):
        slot = index + 1
        found = functools.partial(own_frame, index)
        if near <= slot <= near + 1:
            load(slot, found)
        else:
            pl.when(low if slot < near else high)(functools.partial(load, slot, found))
    q_tile = lax.broadcasted_iota(jnp.int32, (cell, 3 * cell), 0)
    k_tile = lax.broadcasted_iota(jnp.int32, (cell, 3 * cell), 1)
    apart = jnp.abs(lax.rem(q_tile, width) // TW - lax.rem(k_tile, width) // TW)
    for reach in range(3):
        band[reach] = jnp.where(apart <= reach, 1.0, 0.0).astype(band.dtype)

    def serve(step, carry):
        slot = (core ^ pieces[0] ^ (step // near)) * near + step % near
        attend_frame(
            meta, query, valid, outs, cells, band, result_cells, step, slot, chip * frames + slot, near, cell, inner
        )
        return carry

    lax.fori_loop(0, near * count, serve, 0)


def attend_frame(
    meta, query, valid, outs, cells, band, result_cells, step, slot, first, near, cell, inner
):
    member = meta[MEMBER]
    scale = np.float32(np.log2(np.e) / np.sqrt(HDIM))
    mine_valid = valid[first + 1, :, cell : cell + inner].astype(jnp.float32)
    real = jnp.transpose(jnp.broadcast_to(mine_valid, (HDIM, inner)))

    def attend(out, head, over_t, over_h):
        lanes = slice(head * HDIM, (head + 1) * HDIM)
        seen = (3 if over_h else 1) * cell
        mask = band[meta[3 * (member * OWN_HEADS + head) + 2], :, :seen]
        ones = jnp.ones((seen, HDIM), jnp.bfloat16)
        for tile in range(inner // cell):
            rows = pl.ds((tile + (0 if over_h else 1)) * cell, seen)
            mine = query[0, first, pl.ds(tile * cell, cell), lanes]
            total = None
            for near_step in (0, 1, 2) if over_t else (1,):
                scores = lax.dot_general(
                    mine,
                    cells[slot + near_step, 0, rows, lanes],
                    (((1,), (1,)), ((), ())),
                    preferred_element_type=jnp.float32,
                )
                start = (tile + (0 if over_h else 1)) * cell
                allowed = mask * valid[first + near_step, :, start : start + seen]
                terms = jnp.exp2(scores * scale).astype(jnp.bfloat16) * allowed
                both = jnp.concatenate([cells[slot + near_step, 1, rows, lanes], ones], axis=1)
                part = jnp.dot(terms, both, preferred_element_type=jnp.float32)
                total = part if total is None else total + part
            here = real[tile * cell : (tile + 1) * cell] > 0
            weight = jnp.where(here, total[:, HDIM:], 1.0)
            result = jnp.where(here, total[:, :HDIM] / weight, 0.0)
            out[0, pl.ds(tile * cell, cell), lanes] = result.astype(out.dtype)

    for head in range(OWN_HEADS):
        reach_t, reach_h = (meta[3 * (member * OWN_HEADS + head) + i] for i in range(2))
        for over_t in (False, True):
            for over_h in (False, True):
                pl.when(((reach_t > 0) == over_t) & ((reach_h > 0) == over_h))(
                    functools.partial(attend, result_cells, head, over_t, over_h)
                )

    for index, out in enumerate(outs):
        pl.when(step // near == index)(functools.partial(out.__setitem__, step % near, result_cells[0]))


def attend(meta, query, near_set, far_set, borders, valid, far, pieces):
    _, chip_frames, cell, _ = near_set[0].shape
    inner = 2 * cell
    span = 4 * cell
    near = chip_frames // CORES
    sets = (*far_set, *near_set) if far else (*near_set, *far_set)
    parts = [*sets, *(p for pair in borders for p in pair)]
    count = len(pieces)
    vmem = pl.BlockSpec(memory_space=pltpu.VMEM)
    piece = jax.ShapeDtypeStruct((near, inner, SPAN), jnp.bfloat16)
    return pl.pallas_call(
        functools.partial(
            attend_body, near=near, far=far, sides=len(borders), cell=cell, inner=inner, pieces=pieces
        ),
        grid_spec=pltpu.PrefetchScalarGridSpec(
            num_scalar_prefetch=1,
            grid=(),
            in_specs=[vmem] * (len(parts) + 2),
            out_specs=[vmem] * count,
            scratch_shapes=[
                pltpu.VMEM((chip_frames + 2, 2, span, SPAN), jnp.bfloat16),
                pltpu.VMEM((3, cell, 3 * cell), jnp.bfloat16),
                pltpu.VMEM((1, inner, SPAN), jnp.bfloat16),
            ],
        ),
        out_shape=[piece] * count,
        compiler_params=pltpu.CompilerParams(vmem_limit_bytes=24 * MIB),
        cost_estimate=pl.CostEstimate(
            flops=OWN_HEADS * count * near * inner * 9 * cell * HDIM * 6,
            bytes_accessed=4 * SPAN * (near * count + 2) * span + 4 * SPAN * near * count * inner,
            transcendentals=OWN_HEADS * count * near * inner * 9 * cell,
        ),
    )(meta, query, *parts, valid)


def collect_body(member, *rest):
    out = rest[-1]
    for flip, piece in enumerate(rest[:-1]):
        column = pl.multiple_of((member[0] ^ flip) * SPAN, SPAN)
        out[:, pl.ds(column, SPAN)] = piece[...]


def collect(member, pieces):
    rows = pieces[0].shape[0]
    whole = pl.BlockSpec((rows, SPAN), lambda i, m: (0, 0))
    return pl.pallas_call(
        collect_body,
        grid_spec=pltpu.PrefetchScalarGridSpec(
            num_scalar_prefetch=1,
            grid=(1,),
            in_specs=[whole] * MATES,
            out_specs=pl.BlockSpec((rows, HEADS * HDIM), lambda i, m: (0, 0)),
        ),
        out_shape=jax.ShapeDtypeStruct((rows, HEADS * HDIM), jnp.bfloat16),
        compiler_params=pltpu.CompilerParams(vmem_limit_bytes=16 * MIB),
    )(member.reshape(1), *pieces)


def gather_lines(share):
    return [share] + [swap(share, "height", d) for d in range(1, lax.axis_size("height"))]


def gather_blocks(lines, spots, places):
    blocks = list(lines)
    for e in range(1, lax.axis_size("rest")):
        blocks += [swap(line, "rest", e) for line in lines]
    depth = lines[0].shape[0] // MATES
    if depth % 16:
        pieces = jnp.concatenate(blocks, axis=0).reshape(-1, depth, lines[0].shape[1])
        ordered = jnp.zeros_like(pieces).at[jnp.stack(places)].set(pieces)
        return [ordered.reshape(-1, pieces.shape[2])], (None,)
    return blocks, spots


def per_device(tokens, mod_scale, mod_shift, w_qkv, q_gain, k_gain, window, valid):
    frames, rows, width, features = tokens.shape
    count = frames * rows * width
    inner = rows * width
    model = w_qkv.shape[1] // 3
    rest, pair, core, height = (lax.axis_index(a) for a in ("rest", "pair", "core", "height"))
    member = pair * CORES + core
    high = lax.axis_size("height")
    many = lax.axis_size("rest")
    r_odd = rest % 2

    def columns_of(mate):
        return jnp.concatenate(
            [lax.dynamic_slice_in_dim(w_qkv, s * model + mate * SPAN, SPAN, axis=1) for s in range(3)], axis=1
        )

    shares = [columns_of(member)] + [swap(columns_of(member ^ flip), TEAM, flip) for flip in range(1, MATES)]
    stacked = jnp.concatenate(shares, axis=0)
    kv_share, q_share = stacked[:, SPAN:], stacked[:, :SPAN]
    flat = tokens.reshape(count, features)
    cut = count * 5 // 8 // width * width
    mine = [
        modulate(flat, mod_scale, mod_shift, 0, cut, width),
        modulate(flat, mod_scale, mod_shift, cut, count - cut, width),
    ]
    mine, kv_share, q_share = lax.optimization_barrier((mine, kv_share, q_share))
    beside = [swap(x, "core", 1) for x in mine]
    kv_share, beside = lax.optimization_barrier((kv_share, beside))

    meta = jnp.concatenate(
        [
            window.reshape(-1),
            jnp.stack([member, pair, core, height % 2, r_odd, rest, height]).astype(jnp.int32),
        ]
    )
    total_frames = MATES * frames
    valid_pad = jnp.pad(valid, ((TT, TT), (TH, TH), (0, 0)))
    around = lax.dynamic_slice(
        valid_pad,
        (rest * total_frames, height * rows, jnp.int32(0)),
        (total_frames + 2 * TT, rows + 2 * TH, width),
    )
    seen = (around > 0).astype(jnp.bfloat16).reshape(total_frames + 2 * TT, 1, -1)

    spots, places = [], []
    for e in range(many):
        for d in range(high):
            for j in range(MATES):
                spots.append((e, j, d, high))
                places.append(((rest ^ e) * MATES + (member ^ j)) * high + (height ^ d))
    kv_lines = gather_lines(kv_share)
    q_share, kv_lines[-1] = lax.optimization_barrier((q_share, kv_lines[-1]))
    kv_blocks, kv_spots = gather_blocks(kv_lines, tuple(spots), places)

    across = [swap(mine[0], "pair", 1)]
    held = kv_blocks[: 2 * high - 1]
    across[0], meta, seen, later, held = lax.optimization_barrier((across[0], meta, seen, mine[1], held))
    kv_blocks[: 2 * high - 1] = held
    across.append(swap(later, "pair", 1))
    q_lines = gather_lines(q_share)
    kv_blocks[0], q_lines[:3] = lax.optimization_barrier((kv_blocks[0], q_lines[:3]))
    q_blocks, q_spots = gather_blocks(q_lines, tuple(spots), places)

    def cells_of(sources):
        return project(meta, sources, CORES, frames, kv_blocks, kv_spots, k_gain, 2, 1, True)

    def exchanged(even, odd):
        return (even, odd, swap_neighbours(even, "height", 0), swap_neighbours(odd, "height", 1))

    even, odd = cells_of([*mine, *beside])
    even, odd, across[-1], q_blocks = lax.optimization_barrier((even, odd, across[-1], q_blocks))
    near_set = exchanged(even, odd)
    beyond = [swap(x, "core", 1) for x in across]
    even, odd = cells_of([*across, *beyond])
    far_set = exchanged(even, odd)

    def border(side):
        last = r_odd == side
        chosen = jnp.where(last, 1, 0) == pair
        frame = jnp.stack(
            [
                jnp.where(
                    chosen,
                    jnp.where(last, a[:, -1], a[:, 0]),
                    jnp.where(last, b[:, -1], b[:, 0]),
                )
                for a, b in zip(near_set[:2], far_set[:2])
            ]
        )
        frame, *back = lax.optimization_barrier((swap_neighbours(frame, "rest", side), *near_set[2:]))
        return frame, swap_neighbours(frame[0], "height", 0), swap_neighbours(frame[1], "height", 1)

    borders = [border(side) for side in range(min(2, many - 1))]
    q_blocks[0], even = lax.optimization_barrier((q_blocks[0], even))
    far_set = (even, *far_set[1:])
    everyone = [*mine, *beside, *across, *beyond]
    (query,) = project(meta, everyone, MATES, frames, q_blocks, q_spots, q_gain, 1, 1, False)
    query, *far_back = lax.optimization_barrier((query, *far_set[2:]))
    far_set = (*far_set[:2], *far_back)

    parts = (query, near_set, far_set, borders, seen)
    travelled = []
    for flip in range(CORES):
        (out,) = attend(meta, *parts, True, (flip,))
        meta, out = lax.optimization_barrier((meta, out))
        travelled.append(swap(out.reshape(count, SPAN), TEAM, CORES + flip))
    meta, travelled[0] = lax.optimization_barrier((meta, travelled[0]))
    near_out = attend(meta, *parts, False, (0, 1))
    other, *travelled = lax.optimization_barrier((near_out[1], *travelled))
    pieces = [near_out[0].reshape(count, SPAN), swap(other.reshape(count, SPAN), TEAM, 1), *travelled]
    return collect(member.astype(jnp.int32), pieces).reshape(frames, rows, width, model)


def solution(mesh):
    split = Mesh(
        mesh.devices.reshape(mesh.shape["tm"] // MATES, MATES // CORES, CORES, mesh.shape["height"]),
        ("rest", "pair", "core", "height"),
    )
    along = ("rest", "pair", "core")
    in_specs = (
        P(along, "height", None, None),
        P(),
        P(),
        P((*along, "height"), None),
        P(),
        P(),
        P(),
        P(),
    )
    out_specs = P(along, "height", None, None)
    return jax.shard_map(
        per_device, mesh=split, in_specs=in_specs, out_specs=out_specs, check_vma=False
    )
```

```python
import functools

import jax
import jax.numpy as jnp
import numpy as np
from jax import lax
from jax.experimental import pallas as pl
from jax.experimental.pallas import tpu as pltpu
from jax.sharding import Mesh
from jax.sharding import PartitionSpec as P

HDIM = 128
HEADS = 12
TT = 1
TH = 2
TW = 8
CORES = 2
MATES = 4
OWN_HEADS = HEADS // MATES
SPAN = OWN_HEADS * HDIM
EPS = 1e-06
MIB = 1024 * 1024
TEAM = ("pair", "core")

MEMBER, PAIR, CORE, Z_ODD, R_ODD, REST, HEIGHT = (3 * HEADS + i for i in range(7))


def swap(x, axis, flip):
    names = axis if isinstance(axis, tuple) else (axis,)
    count = int(np.prod([lax.axis_size(name) for name in names]))
    return lax.ppermute(x, axis, [(i, i ^ flip) for i in range(count)])


def swap_neighbours(x, axis, odd):
    count = lax.axis_size(axis)
    pairs = [(i, i + 1) for i in range(odd, count - 1, 2)]
    flat = x.reshape(-1, x.shape[-1])
    return lax.ppermute(flat, axis, pairs + [(j, i) for i, j in pairs]).reshape(x.shape)


def modulate_body(tokens, scale, shift, whole, first, second, *, steps):
    values = tokens[...].astype(jnp.float32)
    centred = values - jnp.mean(values, axis=-1, keepdims=True)
    variance = jnp.mean(centred * centred, axis=-1, keepdims=True)
    normed = centred * lax.rsqrt(variance + EPS)
    result = (normed * (1.0 + scale[...]) + shift[...]).astype(whole.dtype)
    whole[...] = result
    step = pl.program_id(0)
    pl.when(step < steps)(functools.partial(first.__setitem__, ..., result))
    pl.when(step >= steps)(functools.partial(second.__setitem__, ..., result))


def modulate(tokens, scale, shift, cut, block):
    count, features = tokens.shape
    steps = cut // block
    row = lambda place: pl.BlockSpec((block, features), lambda i: (place(i), 0))
    whole = pl.BlockSpec((1, features), lambda i: (0, 0))
    rows = lambda length: jax.ShapeDtypeStruct((length, features), jnp.bfloat16)
    return pl.pallas_call(
        functools.partial(modulate_body, steps=steps),
        grid=(count // block,),
        in_specs=[row(lambda i: i), whole, whole],
        out_specs=[
            row(lambda i: i),
            row(lambda i: jnp.minimum(i, steps - 1)),
            row(lambda i: jnp.maximum(i - steps, 0)),
        ],
        out_shape=[rows(count), rows(cut), rows(count - cut)],
        compiler_params=pltpu.CompilerParams(vmem_limit_bytes=12 * MIB),
        cost_estimate=pl.CostEstimate(
            flops=12 * count * features, bytes_accessed=6 * count * features, transcendentals=0
        ),
    )(tokens, scale.reshape(1, features), shift.reshape(1, features))


def project_body(meta, *rest, groups, frames, arrays, depth, spots, normed, halves):
    sources, members = sum(groups), len(groups)
    xs, blocks, gain = rest[:sources], rest[sources : sources + arrays], rest[sources + arrays]
    outs, (rows, weights, row_sems, weight_sems) = rest[sources + arrays + 1 : -4], rest[-4:]
    columns = weights.shape[1]
    count = rows.shape[0] // members
    inner = count // frames
    cell = inner // 2

    loads, first = [], 0
    for i, x in enumerate(xs):
        loads.append(pltpu.make_async_copy(x, rows.at[pl.ds(first, x.shape[0]), :], row_sems.at[i]))
        first += x.shape[0]
    copies = []
    for p, spot in enumerate(spots):
        place = 0
        if spot is not None:
            e, j, d, high = spot
            place = ((meta[REST] ^ e) * MATES + (meta[MEMBER] ^ j)) * high + (meta[HEIGHT] ^ d)
        held = len(spots) // arrays
        source = blocks[p // held].at[pl.ds(p % held * depth, depth), :]
        row = pl.multiple_of(place * depth, depth)
        copies.append(pltpu.make_async_copy(source, weights.at[pl.ds(row, depth), :], weight_sems.at[p]))
    for load in loads[: groups[0]]:
        load.start()
    for copy in copies:
        copy.start()
    for load in loads[groups[0] :]:
        load.start()
    for copy in copies:
        copy.wait()
    wide = 2 * HDIM
    for i in range(members):
        for load in loads[sum(groups[:i]) : sum(groups[: i + 1])]:
            load.wait()
        for start in range(0, columns, wide):
            stop = min(start + wide, columns)
            total = jnp.dot(
                rows[i * count : (i + 1) * count, :], weights[:, start:stop], preferred_element_type=jnp.float32
            )
            for column in range(start, stop, HDIM):
                head = total[:, column - start : column - start + HDIM]
                part, offset = divmod(column, SPAN)
                if part < normed:
                    power = jnp.mean(head * head, axis=-1, keepdims=True)
                    head = head * lax.rsqrt(power + EPS) * gain[...]
                head = head.astype(jnp.bfloat16)
                lanes = slice(offset, offset + HDIM)
                for frame in range(frames):
                    place = (meta[CORE if halves else MEMBER] ^ i) * frames + frame
                    one = head[frame * inner : (frame + 1) * inner]
                    if halves:
                        top, bottom = one[:cell], one[cell:]
                        odd = meta[Z_ODD] == 1
                        outs[0][part, place, :, lanes] = jnp.where(odd, top, bottom)
                        outs[1][part, place, :, lanes] = jnp.where(odd, bottom, top)
                    else:
                        outs[0][part, place, :, lanes] = one


def project(meta, tokens, frames, blocks, spots, gain, parts, normed, halves):
    members = len(tokens)
    groups = tuple(len(pieces) for pieces in tokens)
    sources = [x for pieces in tokens for x in pieces]
    features = sources[0].shape[1]
    total = sum(x.shape[0] for x in sources)
    inner = total // members // frames
    columns = blocks[0].shape[1]
    count = len(sources)
    any_space = pl.BlockSpec(memory_space=pl.ANY)
    vmem = pl.BlockSpec(memory_space=pltpu.VMEM)
    outs = 2 if halves else 1
    return pl.pallas_call(
        functools.partial(
            project_body,
            groups=groups,
            frames=frames,
            arrays=len(blocks),
            depth=features // len(spots),
            spots=spots,
            normed=normed,
            halves=halves,
        ),
        grid_spec=pltpu.PrefetchScalarGridSpec(
            num_scalar_prefetch=1,
            grid=(),
            in_specs=[any_space] * (count + len(blocks)) + [vmem],
            out_specs=[vmem] * outs,
            scratch_shapes=[
                pltpu.VMEM((total, features), jnp.bfloat16),
                pltpu.VMEM((features, columns), jnp.bfloat16),
                pltpu.SemaphoreType.DMA((count,)),
                pltpu.SemaphoreType.DMA((len(spots),)),
            ],
        ),
        out_shape=[jax.ShapeDtypeStruct((parts, members * frames, inner // outs, SPAN), jnp.bfloat16)] * outs,
        compiler_params=pltpu.CompilerParams(vmem_limit_bytes=24 * MIB),
        cost_estimate=pl.CostEstimate(
            flops=2 * total * features * columns,
            bytes_accessed=2 * features * columns + 2 * total * (features + columns),
            transcendentals=0,
        ),
    )(meta, *sources, *blocks, gain.reshape(1, HDIM))


def attend_body(meta, *rest, near, far, sides, cell, inner, pieces):
    count = len(pieces)
    query, main = rest[0], rest[1 : -4 - count]
    valid, outs = rest[-4 - count], rest[-3 - count : -3]
    cells, band, result_cells = rest[-3:]
    member, pair, core, z_odd, r_odd = (meta[i] for i in (MEMBER, PAIR, CORE, Z_ODD, R_ODD))
    chip = 1 - pair if far else pair
    width = cell // TH
    frames = cells.shape[0] - 2

    row_of = [jnp.where(z_odd == 1, a, b) * cell for a, b in ((1, 2), (2, 1), (0, 3), (3, 0))]
    own_set, other_set, borders = main[0:4], main[4:8], main[8:]
    own_frame = lambda i: tuple(part[:, i] for part in own_set)
    other_frame = lambda i: tuple(part[:, i] for part in other_set)

    def load(slot, found):
        for part, row in zip(found(), row_of):
            rows = pl.ds(pl.multiple_of(row, cell), cell)
            cells[slot, :, rows, :] = part

    def border(side):
        frame, even, odd = borders[3 * side : 3 * side + 3]
        return frame[0], frame[1], even[...], odd[...]

    low = jnp.bool_(True) if count > 1 else (core ^ pieces[0]) == 0
    high = jnp.bool_(True) if count > 1 else (core ^ pieces[0]) == 1
    for end, slot, used in ((0, 0, low), (1, frames + 1, high)):
        found = functools.partial(other_frame, 0 if end else frames - 1)
        pl.when(used & (chip != end))(functools.partial(load, slot, found))
        for side in range(sides):
            pl.when(used & (chip == end) & ((r_odd == 1) == (end == side)))(
                functools.partial(load, slot, functools.partial(border, side))
            )

        if sides < 2:

            @pl.when(used & (chip == end) & ((r_odd == 1) == (end == 1)))
            def _():
                cells[slot] = jnp.zeros(cells.shape[1:], cells.dtype)

    for index in range(frames):
        slot = index + 1
        found = functools.partial(own_frame, index)
        if near <= slot <= near + 1:
            load(slot, found)
        else:
            pl.when(low if slot < near else high)(functools.partial(load, slot, found))
    q_tile = lax.broadcasted_iota(jnp.int32, (cell, 3 * cell), 0)
    k_tile = lax.broadcasted_iota(jnp.int32, (cell, 3 * cell), 1)
    apart = jnp.abs(lax.rem(q_tile, width) // TW - lax.rem(k_tile, width) // TW)
    for reach in range(3):
        band[reach] = jnp.where(apart <= reach, 1.0, 0.0).astype(band.dtype)

    def serve(step, carry):
        slot = (core ^ pieces[0] ^ (step // near)) * near + step % near
        attend_frame(
            meta, query, valid, outs, cells, band, result_cells, step, slot, chip * frames + slot, near, cell, inner
        )
        return carry

    lax.fori_loop(0, near * count, serve, 0)


def attend_frame(
    meta, query, valid, outs, cells, band, result_cells, step, slot, first, near, cell, inner
):
    member = meta[MEMBER]
    scale = np.float32(np.log2(np.e) / np.sqrt(HDIM))
    mine_valid = valid[first + 1, :, cell : cell + inner].astype(jnp.float32)
    real = jnp.transpose(jnp.broadcast_to(mine_valid, (HDIM, inner)))

    def attend(out, head, over_t, over_h):
        lanes = slice(head * HDIM, (head + 1) * HDIM)
        seen = (3 if over_h else 1) * cell
        mask = band[meta[3 * (member * OWN_HEADS + head) + 2], :, :seen]
        ones = jnp.ones((seen, HDIM), jnp.bfloat16)
        for tile in range(inner // cell):
            rows = pl.ds((tile + (0 if over_h else 1)) * cell, seen)
            mine = query[0, first, pl.ds(tile * cell, cell), lanes]
            total = None
            for near_step in (0, 1, 2) if over_t else (1,):
                scores = lax.dot_general(
                    mine,
                    cells[slot + near_step, 0, rows, lanes],
                    (((1,), (1,)), ((), ())),
                    preferred_element_type=jnp.float32,
                )
                start = (tile + (0 if over_h else 1)) * cell
                allowed = mask * valid[first + near_step, :, start : start + seen]
                terms = jnp.exp2(scores * scale).astype(jnp.bfloat16) * allowed
                both = jnp.concatenate([cells[slot + near_step, 1, rows, lanes], ones], axis=1)
                part = jnp.dot(terms, both, preferred_element_type=jnp.float32)
                total = part if total is None else total + part
            here = real[tile * cell : (tile + 1) * cell] > 0
            weight = jnp.where(here, total[:, HDIM:], 1.0)
            result = jnp.where(here, total[:, :HDIM] / weight, 0.0)
            out[0, pl.ds(tile * cell, cell), lanes] = result.astype(out.dtype)

    for head in range(OWN_HEADS):
        reach_t, reach_h = (meta[3 * (member * OWN_HEADS + head) + i] for i in range(2))
        for over_t in (False, True):
            for over_h in (False, True):
                pl.when(((reach_t > 0) == over_t) & ((reach_h > 0) == over_h))(
                    functools.partial(attend, result_cells, head, over_t, over_h)
                )

    for index, out in enumerate(outs):
        pl.when(step // near == index)(functools.partial(out.__setitem__, step % near, result_cells[0]))


def attend(meta, query, near_set, far_set, borders, valid, far, pieces):
    _, chip_frames, cell, _ = near_set[0].shape
    inner = 2 * cell
    span = 4 * cell
    near = chip_frames // CORES
    sets = (*far_set, *near_set) if far else (*near_set, *far_set)
    parts = [*sets, *(p for pair in borders for p in pair)]
    count = len(pieces)
    vmem = pl.BlockSpec(memory_space=pltpu.VMEM)
    piece = jax.ShapeDtypeStruct((near, inner, SPAN), jnp.bfloat16)
    return pl.pallas_call(
        functools.partial(
            attend_body, near=near, far=far, sides=len(borders), cell=cell, inner=inner, pieces=pieces
        ),
        grid_spec=pltpu.PrefetchScalarGridSpec(
            num_scalar_prefetch=1,
            grid=(),
            in_specs=[vmem] * (len(parts) + 2),
            out_specs=[vmem] * count,
            scratch_shapes=[
                pltpu.VMEM((chip_frames + 2, 2, span, SPAN), jnp.bfloat16),
                pltpu.VMEM((3, cell, 3 * cell), jnp.bfloat16),
                pltpu.VMEM((1, inner, SPAN), jnp.bfloat16),
            ],
        ),
        out_shape=[piece] * count,
        compiler_params=pltpu.CompilerParams(vmem_limit_bytes=24 * MIB),
        cost_estimate=pl.CostEstimate(
            flops=OWN_HEADS * count * near * inner * 9 * cell * HDIM * 6,
            bytes_accessed=4 * SPAN * (near * count + 2) * span + 4 * SPAN * near * count * inner,
            transcendentals=OWN_HEADS * count * near * inner * 9 * cell,
        ),
    )(meta, query, *parts, valid)


def collect_body(member, *rest):
    out = rest[-1]
    for flip, piece in enumerate(rest[:-1]):
        column = pl.multiple_of((member[0] ^ flip) * SPAN, SPAN)
        out[:, pl.ds(column, SPAN)] = piece[...]


def collect(member, pieces):
    rows = pieces[0].shape[0]
    whole = pl.BlockSpec((rows, SPAN), lambda i, m: (0, 0))
    return pl.pallas_call(
        collect_body,
        grid_spec=pltpu.PrefetchScalarGridSpec(
            num_scalar_prefetch=1,
            grid=(1,),
            in_specs=[whole] * MATES,
            out_specs=pl.BlockSpec((rows, HEADS * HDIM), lambda i, m: (0, 0)),
        ),
        out_shape=jax.ShapeDtypeStruct((rows, HEADS * HDIM), jnp.bfloat16),
        compiler_params=pltpu.CompilerParams(vmem_limit_bytes=16 * MIB),
    )(member.reshape(1), *pieces)


def gather_lines(share):
    return [share] + [swap(share, "height", d) for d in range(1, lax.axis_size("height"))]


def gather_blocks(lines, spots, places):
    blocks = list(lines)
    for e in range(1, lax.axis_size("rest")):
        blocks += [swap(line, "rest", e) for line in lines]
    depth = lines[0].shape[0] // MATES
    if depth % 16:
        pieces = jnp.concatenate(blocks, axis=0).reshape(-1, depth, lines[0].shape[1])
        ordered = jnp.zeros_like(pieces).at[jnp.stack(places)].set(pieces)
        return [ordered.reshape(-1, pieces.shape[2])], (None,)
    return blocks, spots


def per_device(tokens, mod_scale, mod_shift, w_qkv, q_gain, k_gain, window, valid):
    frames, rows, width, features = tokens.shape
    count = frames * rows * width
    inner = rows * width
    model = w_qkv.shape[1] // 3
    rest, pair, core, height = (lax.axis_index(a) for a in ("rest", "pair", "core", "height"))
    member = pair * CORES + core
    high = lax.axis_size("height")
    many = lax.axis_size("rest")
    r_odd = rest % 2

    def columns_of(mate):
        return jnp.concatenate(
            [lax.dynamic_slice_in_dim(w_qkv, s * model + mate * SPAN, SPAN, axis=1) for s in range(3)], axis=1
        )

    shares = [columns_of(member)] + [swap(columns_of(member ^ flip), TEAM, flip) for flip in range(1, MATES)]
    stacked = jnp.concatenate(shares, axis=0)
    kv_share, q_share = stacked[:, SPAN:], stacked[:, :SPAN]
    flat = tokens.reshape(count, features)
    cut = count * 5 // 8 // width * width
    mine, most, last_rows = modulate(flat, mod_scale, mod_shift, cut, width)
    most, kv_share, q_share = lax.optimization_barrier((most, kv_share, q_share))

    meta = jnp.concatenate(
        [
            window.reshape(-1),
            jnp.stack([member, pair, core, height % 2, r_odd, rest, height]).astype(jnp.int32),
        ]
    )
    total_frames = MATES * frames
    valid_pad = jnp.pad(valid, ((TT, TT), (TH, TH), (0, 0)))
    around = lax.dynamic_slice(
        valid_pad,
        (rest * total_frames, height * rows, jnp.int32(0)),
        (total_frames + 2 * TT, rows + 2 * TH, width),
    )
    seen = (around > 0).astype(jnp.bfloat16).reshape(total_frames + 2 * TT, 1, -1)

    spots, places = [], []
    for e in range(many):
        for d in range(high):
            for j in range(MATES):
                spots.append((e, j, d, high))
                places.append(((rest ^ e) * MATES + (member ^ j)) * high + (height ^ d))
    kv_lines = gather_lines(kv_share)
    q_share, kv_lines[-1] = lax.optimization_barrier((q_share, kv_lines[-1]))
    kv_blocks, kv_spots = gather_blocks(kv_lines, tuple(spots), places)

    across = [swap(most, "pair", 1)]
    held = kv_blocks[: 2 * high - 1]
    across[0], meta, seen, last_rows, mates, held = lax.optimization_barrier(
        (across[0], meta, seen, last_rows, mine, held)
    )
    kv_blocks[: 2 * high - 1] = held
    across.append(swap(last_rows, "pair", 1))
    beside = swap(mates, "core", 1)
    nearest = swap(q_share, "height", 1)
    q_share, nearest = lax.optimization_barrier((q_share, nearest))
    q_lines = [q_share, nearest] + [swap(q_share, "height", d) for d in range(2, high)]
    q_lines[0], beside = lax.optimization_barrier((q_lines[0], beside))
    kv_blocks[0], q_lines[1] = lax.optimization_barrier((kv_blocks[0], q_lines[1]))
    q_blocks, q_spots = gather_blocks(q_lines, tuple(spots), places)

    def cells_of(tokens):
        return project(meta, tokens, frames, kv_blocks, kv_spots, k_gain, 2, 1, True)

    def exchanged(even, odd):
        return (even, odd, swap_neighbours(even, "height", 0), swap_neighbours(odd, "height", 1))

    even, odd = cells_of([[mine], [beside]])
    near_set = exchanged(even, odd)
    begun = q_blocks[: high + 2]
    _, across, begun = lax.optimization_barrier((even, across, begun))
    q_blocks[: high + 2] = begun
    beyond = [swap(x, "core", 1) for x in across]
    even, odd = cells_of([across, beyond])
    far_set = exchanged(even, odd)

    def border(side):
        last = r_odd == side
        chosen = jnp.where(last, 1, 0) == pair
        frame = jnp.stack(
            [
                jnp.where(
                    chosen,
                    jnp.where(last, a[:, -1], a[:, 0]),
                    jnp.where(last, b[:, -1], b[:, 0]),
                )
                for a, b in zip(near_set[:2], far_set[:2])
            ]
        )
        frame, *back = lax.optimization_barrier((swap_neighbours(frame, "rest", side), *near_set[2:]))
        return frame, swap_neighbours(frame[0], "height", 0), swap_neighbours(frame[1], "height", 1)

    borders = [border(side) for side in range(min(2, many - 1))]
    q_blocks[0], even = lax.optimization_barrier((q_blocks[0], even))
    far_set = (even, *far_set[1:])
    everyone = [[mine], [beside], across, beyond]
    (query,) = project(meta, everyone, frames, q_blocks, q_spots, q_gain, 1, 1, False)
    query, *far_back = lax.optimization_barrier((query, *far_set[2:]))
    far_set = (*far_set[:2], *far_back)

    parts = (query, near_set, far_set, borders, seen)
    travelled = []
    for flip in range(CORES):
        (out,) = attend(meta, *parts, True, (flip,))
        meta, out = lax.optimization_barrier((meta, out))
        travelled.append(swap(out.reshape(count, SPAN), TEAM, CORES + flip))
    meta, travelled[0] = lax.optimization_barrier((meta, travelled[0]))
    near_out = attend(meta, *parts, False, (0, 1))
    other, *travelled = lax.optimization_barrier((near_out[1], *travelled))
    pieces = [near_out[0].reshape(count, SPAN), swap(other.reshape(count, SPAN), TEAM, 1), *travelled]
    return collect(member.astype(jnp.int32), pieces).reshape(frames, rows, width, model)


def solution(mesh):
    split = Mesh(
        mesh.devices.reshape(mesh.shape["tm"] // MATES, MATES // CORES, CORES, mesh.shape["height"]),
        ("rest", "pair", "core", "height"),
    )
    along = ("rest", "pair", "core")
    in_specs = (
        P(along, "height", None, None),
        P(),
        P(),
        P((*along, "height"), None),
        P(),
        P(),
        P(),
        P(),
    )
    out_specs = P(along, "height", None, None)
    return jax.shard_map(
        per_device, mesh=split, in_specs=in_specs, out_specs=out_specs, check_vma=False
    )
```

```python
import functools

import jax
import jax.numpy as jnp
import numpy as np
from jax import lax
from jax.experimental import pallas as pl
from jax.experimental.pallas import tpu as pltpu
from jax.sharding import Mesh
from jax.sharding import PartitionSpec as P

HDIM = 128
HEADS = 12
TT = 1
TH = 2
TW = 8
CORES = 2
MATES = 4
OWN_HEADS = HEADS // MATES
SPAN = OWN_HEADS * HDIM
EPS = 1e-06
MIB = 1024 * 1024
TEAM = ("pair", "core")

MEMBER, PAIR, CORE, Z_ODD, R_ODD, REST, HEIGHT = (3 * HEADS + i for i in range(7))


def swap(x, axis, flip):
    names = axis if isinstance(axis, tuple) else (axis,)
    count = int(np.prod([lax.axis_size(name) for name in names]))
    return lax.ppermute(x, axis, [(i, i ^ flip) for i in range(count)])


def swap_neighbours(x, axis, odd):
    count = lax.axis_size(axis)
    pairs = [(i, i + 1) for i in range(odd, count - 1, 2)]
    flat = x.reshape(-1, x.shape[-1])
    return lax.ppermute(flat, axis, pairs + [(j, i) for i, j in pairs]).reshape(x.shape)


def modulate_body(tokens, scale, shift, whole, first, second, *, steps):
    values = tokens[...].astype(jnp.float32)
    centred = values - jnp.mean(values, axis=-1, keepdims=True)
    variance = jnp.mean(centred * centred, axis=-1, keepdims=True)
    normed = centred * lax.rsqrt(variance + EPS)
    result = (normed * (1.0 + scale[...]) + shift[...]).astype(whole.dtype)
    whole[...] = result
    step = pl.program_id(0)
    pl.when(step < steps)(functools.partial(first.__setitem__, ..., result))
    pl.when(step >= steps)(functools.partial(second.__setitem__, ..., result))


def modulate(tokens, scale, shift, cut, block):
    count, features = tokens.shape
    steps = cut // block
    row = lambda place: pl.BlockSpec((block, features), lambda i: (place(i), 0))
    whole = pl.BlockSpec((1, features), lambda i: (0, 0))
    rows = lambda length: jax.ShapeDtypeStruct((length, features), jnp.bfloat16)
    return pl.pallas_call(
        functools.partial(modulate_body, steps=steps),
        grid=(count // block,),
        in_specs=[row(lambda i: i), whole, whole],
        out_specs=[
            row(lambda i: i),
            row(lambda i: jnp.minimum(i, steps - 1)),
            row(lambda i: jnp.maximum(i - steps, 0)),
        ],
        out_shape=[rows(count), rows(cut), rows(count - cut)],
        compiler_params=pltpu.CompilerParams(vmem_limit_bytes=12 * MIB),
        cost_estimate=pl.CostEstimate(
            flops=12 * count * features, bytes_accessed=6 * count * features, transcendentals=0
        ),
    )(tokens, scale.reshape(1, features), shift.reshape(1, features))


def project_body(meta, *rest, groups, frames, arrays, depth, spots, normed, halves):
    sources, members = sum(groups), len(groups)
    xs, blocks, gain = rest[:sources], rest[sources : sources + arrays], rest[sources + arrays]
    outs, (rows, weights, row_sems, weight_sems) = rest[sources + arrays + 1 : -4], rest[-4:]
    columns = weights.shape[1]
    count = rows.shape[0] // members
    inner = count // frames
    cell = inner // 2

    loads, first = [], 0
    for i, x in enumerate(xs):
        loads.append(pltpu.make_async_copy(x, rows.at[pl.ds(first, x.shape[0]), :], row_sems.at[i]))
        first += x.shape[0]
    copies = []
    for p, spot in enumerate(spots):
        place = 0
        if spot is not None:
            e, j, d, high = spot
            place = ((meta[REST] ^ e) * MATES + (meta[MEMBER] ^ j)) * high + (meta[HEIGHT] ^ d)
        held = len(spots) // arrays
        source = blocks[p // held].at[pl.ds(p % held * depth, depth), :]
        row = pl.multiple_of(place * depth, depth)
        copies.append(pltpu.make_async_copy(source, weights.at[pl.ds(row, depth), :], weight_sems.at[p]))
    for load in loads[: groups[0]]:
        load.start()
    for copy in copies:
        copy.start()
    for load in loads[groups[0] :]:
        load.start()
    for copy in copies:
        copy.wait()
    wide = 2 * HDIM
    for i in range(members):
        for load in loads[sum(groups[:i]) : sum(groups[: i + 1])]:
            load.wait()
        for start in range(0, columns, wide):
            stop = min(start + wide, columns)
            total = jnp.dot(
                rows[i * count : (i + 1) * count, :], weights[:, start:stop], preferred_element_type=jnp.float32
            )
            for column in range(start, stop, HDIM):
                head = total[:, column - start : column - start + HDIM]
                part, offset = divmod(column, SPAN)
                if part < normed:
                    power = jnp.mean(head * head, axis=-1, keepdims=True)
                    head = head * lax.rsqrt(power + EPS) * gain[...]
                head = head.astype(jnp.bfloat16)
                lanes = slice(offset, offset + HDIM)
                for frame in range(frames):
                    place = (meta[CORE if halves else MEMBER] ^ i) * frames + frame
                    one = head[frame * inner : (frame + 1) * inner]
                    if halves:
                        top, bottom = one[:cell], one[cell:]
                        odd = meta[Z_ODD] == 1
                        outs[0][part, place, :, lanes] = jnp.where(odd, top, bottom)
                        outs[1][part, place, :, lanes] = jnp.where(odd, bottom, top)
                    else:
                        outs[0][part, place, :, lanes] = one


def project(meta, tokens, frames, blocks, spots, gain, parts, normed, halves):
    members = len(tokens)
    groups = tuple(len(pieces) for pieces in tokens)
    sources = [x for pieces in tokens for x in pieces]
    features = sources[0].shape[1]
    total = sum(x.shape[0] for x in sources)
    inner = total // members // frames
    columns = blocks[0].shape[1]
    count = len(sources)
    any_space = pl.BlockSpec(memory_space=pl.ANY)
    vmem = pl.BlockSpec(memory_space=pltpu.VMEM)
    outs = 2 if halves else 1
    return pl.pallas_call(
        functools.partial(
            project_body,
            groups=groups,
            frames=frames,
            arrays=len(blocks),
            depth=features // len(spots),
            spots=spots,
            normed=normed,
            halves=halves,
        ),
        grid_spec=pltpu.PrefetchScalarGridSpec(
            num_scalar_prefetch=1,
            grid=(),
            in_specs=[any_space] * (count + len(blocks)) + [vmem],
            out_specs=[vmem] * outs,
            scratch_shapes=[
                pltpu.VMEM((total, features), jnp.bfloat16),
                pltpu.VMEM((features, columns), jnp.bfloat16),
                pltpu.SemaphoreType.DMA((count,)),
                pltpu.SemaphoreType.DMA((len(spots),)),
            ],
        ),
        out_shape=[jax.ShapeDtypeStruct((parts, members * frames, inner // outs, SPAN), jnp.bfloat16)] * outs,
        compiler_params=pltpu.CompilerParams(vmem_limit_bytes=24 * MIB),
        cost_estimate=pl.CostEstimate(
            flops=2 * total * features * columns,
            bytes_accessed=2 * features * columns + 2 * total * (features + columns),
            transcendentals=0,
        ),
    )(meta, *sources, *blocks, gain.reshape(1, HDIM))


def attend_body(meta, *rest, near, far, sides, cell, inner, pieces):
    count = len(pieces)
    query, main = rest[0], rest[1 : -4 - count]
    valid, outs = rest[-4 - count], rest[-3 - count : -3]
    cells, band, result_cells = rest[-3:]
    member, pair, core, z_odd, r_odd = (meta[i] for i in (MEMBER, PAIR, CORE, Z_ODD, R_ODD))
    chip = 1 - pair if far else pair
    width = cell // TH
    frames = cells.shape[0] - 2

    row_of = [jnp.where(z_odd == 1, a, b) * cell for a, b in ((1, 2), (2, 1), (0, 3), (3, 0))]
    own_set, other_set, borders = main[0:4], main[4:8], main[8:]
    own_frame = lambda i: tuple(part[:, i] for part in own_set)
    other_frame = lambda i: tuple(part[:, i] for part in other_set)

    def load(slot, found):
        for part, row in zip(found(), row_of):
            rows = pl.ds(pl.multiple_of(row, cell), cell)
            cells[slot, :, rows, :] = part

    def border(side):
        frame, even, odd = borders[3 * side : 3 * side + 3]
        return frame[0], frame[1], even[...], odd[...]

    low = jnp.bool_(True) if count > 1 else (core ^ pieces[0]) == 0
    high = jnp.bool_(True) if count > 1 else (core ^ pieces[0]) == 1
    for end, slot, used in ((0, 0, low), (1, frames + 1, high)):
        found = functools.partial(other_frame, 0 if end else frames - 1)
        pl.when(used & (chip != end))(functools.partial(load, slot, found))
        for side in range(sides):
            pl.when(used & (chip == end) & ((r_odd == 1) == (end == side)))(
                functools.partial(load, slot, functools.partial(border, side))
            )

        if sides < 2:

            @pl.when(used & (chip == end) & ((r_odd == 1) == (end == 1)))
            def _():
                cells[slot] = jnp.zeros(cells.shape[1:], cells.dtype)

    for index in range(frames):
        slot = index + 1
        found = functools.partial(own_frame, index)
        if near <= slot <= near + 1:
            load(slot, found)
        else:
            pl.when(low if slot < near else high)(functools.partial(load, slot, found))
    q_tile = lax.broadcasted_iota(jnp.int32, (cell, 3 * cell), 0)
    k_tile = lax.broadcasted_iota(jnp.int32, (cell, 3 * cell), 1)
    apart = jnp.abs(lax.rem(q_tile, width) // TW - lax.rem(k_tile, width) // TW)
    for reach in range(3):
        band[reach] = jnp.where(apart <= reach, 1.0, 0.0).astype(band.dtype)

    def serve(step, carry):
        slot = (core ^ pieces[0] ^ (step // near)) * near + step % near
        attend_frame(
            meta, query, valid, outs, cells, band, result_cells, step, slot, chip * frames + slot, near, cell, inner
        )
        return carry

    lax.fori_loop(0, near * count, serve, 0)


def attend_frame(
    meta, query, valid, outs, cells, band, result_cells, step, slot, first, near, cell, inner
):
    member = meta[MEMBER]
    scale = np.float32(np.log2(np.e) / np.sqrt(HDIM))
    mine_valid = valid[first + 1, :, cell : cell + inner].astype(jnp.float32)
    real = jnp.transpose(jnp.broadcast_to(mine_valid, (HDIM, inner)))

    def attend(out, head, over_t, over_h):
        lanes = slice(head * HDIM, (head + 1) * HDIM)
        seen = (3 if over_h else 1) * cell
        mask = band[meta[3 * (member * OWN_HEADS + head) + 2], :, :seen]
        ones = jnp.ones((seen, HDIM), jnp.bfloat16)
        for tile in range(inner // cell):
            rows = pl.ds((tile + (0 if over_h else 1)) * cell, seen)
            mine = query[0, first, pl.ds(tile * cell, cell), lanes]
            total = None
            for near_step in (0, 1, 2) if over_t else (1,):
                scores = lax.dot_general(
                    mine,
                    cells[slot + near_step, 0, rows, lanes],
                    (((1,), (1,)), ((), ())),
                    preferred_element_type=jnp.float32,
                )
                start = (tile + (0 if over_h else 1)) * cell
                allowed = mask * valid[first + near_step, :, start : start + seen]
                terms = jnp.exp2(scores * scale).astype(jnp.bfloat16) * allowed
                both = jnp.concatenate([cells[slot + near_step, 1, rows, lanes], ones], axis=1)
                part = jnp.dot(terms, both, preferred_element_type=jnp.float32)
                total = part if total is None else total + part
            here = real[tile * cell : (tile + 1) * cell] > 0
            weight = jnp.where(here, total[:, HDIM:], 1.0)
            result = jnp.where(here, total[:, :HDIM] / weight, 0.0)
            out[0, pl.ds(tile * cell, cell), lanes] = result.astype(out.dtype)

    for head in range(OWN_HEADS):
        reach_t, reach_h = (meta[3 * (member * OWN_HEADS + head) + i] for i in range(2))
        for over_t in (False, True):
            for over_h in (False, True):
                pl.when(((reach_t > 0) == over_t) & ((reach_h > 0) == over_h))(
                    functools.partial(attend, result_cells, head, over_t, over_h)
                )

    for index, out in enumerate(outs):
        pl.when(step // near == index)(functools.partial(out.__setitem__, step % near, result_cells[0]))


def attend(meta, query, near_set, far_set, borders, valid, far, pieces):
    _, chip_frames, cell, _ = near_set[0].shape
    inner = 2 * cell
    span = 4 * cell
    near = chip_frames // CORES
    sets = (*far_set, *near_set) if far else (*near_set, *far_set)
    parts = [*sets, *(p for pair in borders for p in pair)]
    count = len(pieces)
    vmem = pl.BlockSpec(memory_space=pltpu.VMEM)
    piece = jax.ShapeDtypeStruct((near, inner, SPAN), jnp.bfloat16)
    return pl.pallas_call(
        functools.partial(
            attend_body, near=near, far=far, sides=len(borders), cell=cell, inner=inner, pieces=pieces
        ),
        grid_spec=pltpu.PrefetchScalarGridSpec(
            num_scalar_prefetch=1,
            grid=(),
            in_specs=[vmem] * (len(parts) + 2),
            out_specs=[vmem] * count,
            scratch_shapes=[
                pltpu.VMEM((chip_frames + 2, 2, span, SPAN), jnp.bfloat16),
                pltpu.VMEM((3, cell, 3 * cell), jnp.bfloat16),
                pltpu.VMEM((1, inner, SPAN), jnp.bfloat16),
            ],
        ),
        out_shape=[piece] * count,
        compiler_params=pltpu.CompilerParams(vmem_limit_bytes=24 * MIB),
        cost_estimate=pl.CostEstimate(
            flops=OWN_HEADS * count * near * inner * 9 * cell * HDIM * 6,
            bytes_accessed=4 * SPAN * (near * count + 2) * span + 4 * SPAN * near * count * inner,
            transcendentals=OWN_HEADS * count * near * inner * 9 * cell,
        ),
    )(meta, query, *parts, valid)


def collect_body(member, *rest):
    out = rest[-1]
    for flip, piece in enumerate(rest[:-1]):
        column = pl.multiple_of((member[0] ^ flip) * SPAN, SPAN)
        out[:, pl.ds(column, SPAN)] = piece[...]


def collect(member, pieces):
    rows = pieces[0].shape[0]
    whole = pl.BlockSpec((rows, SPAN), lambda i, m: (0, 0))
    return pl.pallas_call(
        collect_body,
        grid_spec=pltpu.PrefetchScalarGridSpec(
            num_scalar_prefetch=1,
            grid=(1,),
            in_specs=[whole] * MATES,
            out_specs=pl.BlockSpec((rows, HEADS * HDIM), lambda i, m: (0, 0)),
        ),
        out_shape=jax.ShapeDtypeStruct((rows, HEADS * HDIM), jnp.bfloat16),
        compiler_params=pltpu.CompilerParams(vmem_limit_bytes=16 * MIB),
    )(member.reshape(1), *pieces)


def gather_blocks(share):
    high, many = lax.axis_size("height"), lax.axis_size("rest")
    along = lambda x: [swap(x, "rest", e) for e in range(1, many)]
    beside = swap(share, "height", 1)
    if high != 4:
        lines = [share, beside] + [swap(share, "height", d) for d in range(2, high)]
        forwards = [along(line) for line in lines]
    else:
        inner = (lax.axis_index("height") + 1) // 2 == 1
        outward = lambda x: lax.ppermute(x, "height", [(1, 0), (2, 3)])
        middle = swap_neighbours(share, "height", 1)
        forwards = [along(share)]
        beside, forwards = lax.optimization_barrier((beside, forwards))
        end = swap_neighbours(beside, "height", 1)
        forwards.append(along(beside))
        end, forwards[1] = lax.optimization_barrier((end, forwards[1]))
        lines = [share, beside, jnp.where(inner, end, outward(middle)), jnp.where(inner, middle, outward(end))]
        forwards += [along(line) for line in lines[2:]]
    return lines + [forward[e] for e in range(many - 1) for forward in forwards]


def settle(blocks, spots, places):
    depth = blocks[0].shape[0] // MATES
    if depth % 16:
        pieces = jnp.concatenate(blocks, axis=0).reshape(-1, depth, blocks[0].shape[1])
        ordered = jnp.zeros_like(pieces).at[jnp.stack(places)].set(pieces)
        return [ordered.reshape(-1, pieces.shape[2])], (None,)
    return blocks, tuple(spots)


def per_device(tokens, mod_scale, mod_shift, w_qkv, q_gain, k_gain, window, valid):
    frames, rows, width, features = tokens.shape
    count = frames * rows * width
    inner = rows * width
    model = w_qkv.shape[1] // 3
    rest, pair, core, height = (lax.axis_index(a) for a in ("rest", "pair", "core", "height"))
    member = pair * CORES + core
    high = lax.axis_size("height")
    many = lax.axis_size("rest")
    r_odd = rest % 2

    def columns_of(mate):
        return jnp.concatenate(
            [lax.dynamic_slice_in_dim(w_qkv, s * model + mate * SPAN, SPAN, axis=1) for s in range(3)], axis=1
        )

    shares = [columns_of(member)] + [swap(columns_of(member ^ flip), TEAM, flip) for flip in range(1, MATES)]
    stacked = jnp.concatenate(shares, axis=0)
    kv_share, q_share = stacked[:, SPAN:], stacked[:, :SPAN]
    flat = tokens.reshape(count, features)
    cut = count * 3 // 4 // width * width
    mine, most, last_rows = modulate(flat, mod_scale, mod_shift, cut, width)
    most, kv_share, q_share = lax.optimization_barrier((most, kv_share, q_share))

    meta = jnp.concatenate(
        [
            window.reshape(-1),
            jnp.stack([member, pair, core, height % 2, r_odd, rest, height]).astype(jnp.int32),
        ]
    )
    total_frames = MATES * frames
    valid_pad = jnp.pad(valid, ((TT, TT), (TH, TH), (0, 0)))
    around = lax.dynamic_slice(
        valid_pad,
        (rest * total_frames, height * rows, jnp.int32(0)),
        (total_frames + 2 * TT, rows + 2 * TH, width),
    )
    seen = (around > 0).astype(jnp.bfloat16).reshape(total_frames + 2 * TT, 1, -1)

    spots, places = [], []
    for e in range(many):
        for d in range(high):
            for j in range(MATES):
                spots.append((e, j, d, high))
                places.append(((rest ^ e) * MATES + (member ^ j)) * high + (height ^ d))
    kv_blocks = gather_blocks(kv_share)
    q_share, kv_blocks[high - 1] = lax.optimization_barrier((q_share, kv_blocks[high - 1]))
    q_blocks = gather_blocks(q_share)

    across = [swap(most, "pair", 1)]
    here = q_blocks[: high + 2]
    across[0], meta, seen, last_rows, mates, kv_blocks, here = lax.optimization_barrier(
        (across[0], meta, seen, last_rows, mine, kv_blocks, here)
    )
    q_blocks[: high + 2] = here
    across.append(swap(last_rows, "pair", 1))
    beside = swap(mates, "core", 1)
    kv_blocks, kv_spots = settle(kv_blocks, spots, places)

    def cells_of(tokens):
        return project(meta, tokens, frames, kv_blocks, kv_spots, k_gain, 2, 1, True)

    def exchanged(even, odd):
        return (even, odd, swap_neighbours(even, "height", 0), swap_neighbours(odd, "height", 1))

    even, odd = cells_of([[mine], [beside]])
    near_set = exchanged(even, odd)
    _, across, q_blocks = lax.optimization_barrier((even, across, q_blocks))
    beyond = [swap(x, "core", 1) for x in across]
    even, odd = cells_of([across, beyond])
    far_set = exchanged(even, odd)

    def border(side):
        last = r_odd == side
        chosen = jnp.where(last, 1, 0) == pair
        frame = jnp.stack(
            [
                jnp.where(
                    chosen,
                    jnp.where(last, a[:, -1], a[:, 0]),
                    jnp.where(last, b[:, -1], b[:, 0]),
                )
                for a, b in zip(near_set[:2], far_set[:2])
            ]
        )
        frame, *back = lax.optimization_barrier((swap_neighbours(frame, "rest", side), *near_set[2:]))
        return frame, swap_neighbours(frame[0], "height", 0), swap_neighbours(frame[1], "height", 1)

    borders = [border(side) for side in range(min(2, many - 1))]
    q_blocks[0], even = lax.optimization_barrier((q_blocks[0], even))
    far_set = (even, *far_set[1:])
    q_blocks, q_spots = settle(q_blocks, spots, places)
    everyone = [[mine], [beside], across, beyond]
    (query,) = project(meta, everyone, frames, q_blocks, q_spots, q_gain, 1, 1, False)
    query, *far_back = lax.optimization_barrier((query, *far_set[2:]))
    far_set = (*far_set[:2], *far_back)

    parts = (query, near_set, far_set, borders, seen)
    travelled = []
    for flip in range(CORES):
        (out,) = attend(meta, *parts, True, (flip,))
        meta, out = lax.optimization_barrier((meta, out))
        travelled.append(swap(out.reshape(count, SPAN), TEAM, CORES + flip))
    meta, travelled[0] = lax.optimization_barrier((meta, travelled[0]))
    near_out = attend(meta, *parts, False, (0, 1))
    other, *travelled = lax.optimization_barrier((near_out[1], *travelled))
    pieces = [near_out[0].reshape(count, SPAN), swap(other.reshape(count, SPAN), TEAM, 1), *travelled]
    return collect(member.astype(jnp.int32), pieces).reshape(frames, rows, width, model)


def solution(mesh):
    split = Mesh(
        mesh.devices.reshape(mesh.shape["tm"] // MATES, MATES // CORES, CORES, mesh.shape["height"]),
        ("rest", "pair", "core", "height"),
    )
    along = ("rest", "pair", "core")
    in_specs = (
        P(along, "height", None, None),
        P(),
        P(),
        P((*along, "height"), None),
        P(),
        P(),
        P(),
        P(),
    )
    out_specs = P(along, "height", None, None)
    return jax.shard_map(
        per_device, mesh=split, in_specs=in_specs, out_specs=out_specs, check_vma=False
    )
```

```python
import functools

import jax
import jax.numpy as jnp
import numpy as np
from jax import lax
from jax.experimental import pallas as pl
from jax.experimental.pallas import tpu as pltpu
from jax.sharding import Mesh
from jax.sharding import PartitionSpec as P

HDIM = 128
HEADS = 12
TT = 1
TH = 2
TW = 8
CORES = 2
MATES = 4
OWN_HEADS = HEADS // MATES
SPAN = OWN_HEADS * HDIM
EPS = 1e-06
MIB = 1024 * 1024
TEAM = ("pair", "core")

MEMBER, PAIR, CORE, Z_ODD, R_ODD, REST, HEIGHT = (3 * HEADS + i for i in range(7))


def swap(x, axis, flip):
    names = axis if isinstance(axis, tuple) else (axis,)
    count = int(np.prod([lax.axis_size(name) for name in names]))
    return lax.ppermute(x, axis, [(i, i ^ flip) for i in range(count)])


def swap_neighbours(x, axis, odd):
    count = lax.axis_size(axis)
    pairs = [(i, i + 1) for i in range(odd, count - 1, 2)]
    flat = x.reshape(-1, x.shape[-1])
    return lax.ppermute(flat, axis, pairs + [(j, i) for i, j in pairs]).reshape(x.shape)


def modulate_body(tokens, scale, shift, whole, first, second, *, steps):
    values = tokens[...].astype(jnp.float32)
    centred = values - jnp.mean(values, axis=-1, keepdims=True)
    variance = jnp.mean(centred * centred, axis=-1, keepdims=True)
    normed = centred * lax.rsqrt(variance + EPS)
    result = (normed * (1.0 + scale[...]) + shift[...]).astype(whole.dtype)
    whole[...] = result
    step = pl.program_id(0)
    pl.when(step < steps)(functools.partial(first.__setitem__, ..., result))
    pl.when(step >= steps)(functools.partial(second.__setitem__, ..., result))


def modulate(tokens, scale, shift, cut, block):
    count, features = tokens.shape
    steps = cut // block
    row = lambda place: pl.BlockSpec((block, features), lambda i: (place(i), 0))
    whole = pl.BlockSpec((1, features), lambda i: (0, 0))
    rows = lambda length: jax.ShapeDtypeStruct((length, features), jnp.bfloat16)
    return pl.pallas_call(
        functools.partial(modulate_body, steps=steps),
        grid=(count // block,),
        in_specs=[row(lambda i: i), whole, whole],
        out_specs=[
            row(lambda i: i),
            row(lambda i: jnp.minimum(i, steps - 1)),
            row(lambda i: jnp.maximum(i - steps, 0)),
        ],
        out_shape=[rows(count), rows(cut), rows(count - cut)],
        compiler_params=pltpu.CompilerParams(vmem_limit_bytes=12 * MIB),
        cost_estimate=pl.CostEstimate(
            flops=12 * count * features, bytes_accessed=6 * count * features, transcendentals=0
        ),
    )(tokens, scale.reshape(1, features), shift.reshape(1, features))


def project_body(meta, *rest, groups, frames, arrays, depth, spots, normed, halves):
    sources, members = sum(groups), len(groups)
    xs, blocks, gain = rest[:sources], rest[sources : sources + arrays], rest[sources + arrays]
    outs, (rows, weights, row_sems, weight_sems) = rest[sources + arrays + 1 : -4], rest[-4:]
    columns = weights.shape[1]
    count = rows.shape[0] // members
    inner = count // frames
    cell = inner // 2

    loads, first = [], 0
    for i, x in enumerate(xs):
        loads.append(pltpu.make_async_copy(x, rows.at[pl.ds(first, x.shape[0]), :], row_sems.at[i]))
        first += x.shape[0]
    copies = []
    for p, spot in enumerate(spots):
        place = 0
        if spot is not None:
            e, j, d, high = spot
            place = ((meta[REST] ^ e) * MATES + (meta[MEMBER] ^ j)) * high + (meta[HEIGHT] ^ d)
        held = len(spots) // arrays
        source = blocks[p // held].at[pl.ds(p % held * depth, depth), :]
        row = pl.multiple_of(place * depth, depth)
        copies.append(pltpu.make_async_copy(source, weights.at[pl.ds(row, depth), :], weight_sems.at[p]))
    for load in loads[: groups[0]]:
        load.start()
    for copy in copies:
        copy.start()
    for load in loads[groups[0] :]:
        load.start()
    for copy in copies:
        copy.wait()
    wide = 2 * HDIM
    for i in range(members):
        for load in loads[sum(groups[:i]) : sum(groups[: i + 1])]:
            load.wait()
        for start in range(0, columns, wide):
            stop = min(start + wide, columns)
            total = jnp.dot(
                rows[i * count : (i + 1) * count, :], weights[:, start:stop], preferred_element_type=jnp.float32
            )
            for column in range(start, stop, HDIM):
                head = total[:, column - start : column - start + HDIM]
                part, offset = divmod(column, SPAN)
                if part < normed:
                    power = jnp.mean(head * head, axis=-1, keepdims=True)
                    head = head * lax.rsqrt(power + EPS) * gain[...]
                head = head.astype(jnp.bfloat16)
                lanes = slice(offset, offset + HDIM)
                for frame in range(frames):
                    place = (meta[CORE if halves else MEMBER] ^ i) * frames + frame
                    one = head[frame * inner : (frame + 1) * inner]
                    if halves:
                        top, bottom = one[:cell], one[cell:]
                        odd = meta[Z_ODD] == 1
                        outs[0][part, place, :, lanes] = jnp.where(odd, top, bottom)
                        outs[1][part, place, :, lanes] = jnp.where(odd, bottom, top)
                    else:
                        outs[0][part, place, :, lanes] = one


def project(meta, tokens, frames, blocks, spots, gain, parts, normed, halves):
    members = len(tokens)
    groups = tuple(len(pieces) for pieces in tokens)
    sources = [x for pieces in tokens for x in pieces]
    features = sources[0].shape[1]
    total = sum(x.shape[0] for x in sources)
    inner = total // members // frames
    columns = blocks[0].shape[1]
    count = len(sources)
    any_space = pl.BlockSpec(memory_space=pl.ANY)
    vmem = pl.BlockSpec(memory_space=pltpu.VMEM)
    outs = 2 if halves else 1
    return pl.pallas_call(
        functools.partial(
            project_body,
            groups=groups,
            frames=frames,
            arrays=len(blocks),
            depth=features // len(spots),
            spots=spots,
            normed=normed,
            halves=halves,
        ),
        grid_spec=pltpu.PrefetchScalarGridSpec(
            num_scalar_prefetch=1,
            grid=(),
            in_specs=[any_space] * (count + len(blocks)) + [vmem],
            out_specs=[vmem] * outs,
            scratch_shapes=[
                pltpu.VMEM((total, features), jnp.bfloat16),
                pltpu.VMEM((features, columns), jnp.bfloat16),
                pltpu.SemaphoreType.DMA((count,)),
                pltpu.SemaphoreType.DMA((len(spots),)),
            ],
        ),
        out_shape=[jax.ShapeDtypeStruct((parts, members * frames, inner // outs, SPAN), jnp.bfloat16)] * outs,
        compiler_params=pltpu.CompilerParams(vmem_limit_bytes=24 * MIB),
        cost_estimate=pl.CostEstimate(
            flops=2 * total * features * columns,
            bytes_accessed=2 * features * columns + 2 * total * (features + columns),
            transcendentals=0,
        ),
    )(meta, *sources, *blocks, gain.reshape(1, HDIM))


def attend_body(meta, *rest, near, far, sides, cell, inner, pieces):
    count = len(pieces)
    query, main = rest[0], rest[1 : -4 - count]
    valid, outs = rest[-4 - count], rest[-3 - count : -3]
    cells, band, result_cells = rest[-3:]
    member, pair, core, z_odd, r_odd = (meta[i] for i in (MEMBER, PAIR, CORE, Z_ODD, R_ODD))
    chip = 1 - pair if far else pair
    width = cell // TH
    frames = cells.shape[0] - 2

    row_of = [jnp.where(z_odd == 1, a, b) * cell for a, b in ((1, 2), (2, 1), (0, 3), (3, 0))]
    own_set, other_set, borders = main[0:4], main[4:8], main[8:]
    own_frame = lambda i: tuple(part[:, i] for part in own_set)
    other_frame = lambda i: tuple(part[:, i] for part in other_set)

    def load(slot, found):
        for part, row in zip(found(), row_of):
            rows = pl.ds(pl.multiple_of(row, cell), cell)
            cells[slot, :, rows, :] = part

    def border(side):
        frame, even, odd = borders[3 * side : 3 * side + 3]
        return frame[0], frame[1], even[...], odd[...]

    low = jnp.bool_(True) if count > 1 else (core ^ pieces[0]) == 0
    high = jnp.bool_(True) if count > 1 else (core ^ pieces[0]) == 1
    for end, slot, used in ((0, 0, low), (1, frames + 1, high)):
        found = functools.partial(other_frame, 0 if end else frames - 1)
        pl.when(used & (chip != end))(functools.partial(load, slot, found))
        for side in range(sides):
            pl.when(used & (chip == end) & ((r_odd == 1) == (end == side)))(
                functools.partial(load, slot, functools.partial(border, side))
            )

        if sides < 2:

            @pl.when(used & (chip == end) & ((r_odd == 1) == (end == 1)))
            def _():
                cells[slot] = jnp.zeros(cells.shape[1:], cells.dtype)

    for index in range(frames):
        slot = index + 1
        found = functools.partial(own_frame, index)
        if near <= slot <= near + 1:
            load(slot, found)
        else:
            pl.when(low if slot < near else high)(functools.partial(load, slot, found))
    q_tile = lax.broadcasted_iota(jnp.int32, (cell, 3 * cell), 0)
    k_tile = lax.broadcasted_iota(jnp.int32, (cell, 3 * cell), 1)
    apart = jnp.abs(lax.rem(q_tile, width) // TW - lax.rem(k_tile, width) // TW)
    for reach in range(3):
        band[reach] = jnp.where(apart <= reach, 1.0, 0.0).astype(band.dtype)

    def serve(step, carry):
        slot = (core ^ pieces[0] ^ (step // near)) * near + step % near
        attend_frame(
            meta, query, valid, outs, cells, band, result_cells, step, slot, chip * frames + slot, near, cell, inner
        )
        return carry

    lax.fori_loop(0, near * count, serve, 0)


def attend_frame(
    meta, query, valid, outs, cells, band, result_cells, step, slot, first, near, cell, inner
):
    member = meta[MEMBER]
    scale = np.float32(np.log2(np.e) / np.sqrt(HDIM))
    mine_valid = valid[first + 1, :, cell : cell + inner].astype(jnp.float32)
    real = jnp.transpose(jnp.broadcast_to(mine_valid, (HDIM, inner)))

    def attend(out, head, over_t, over_h):
        lanes = slice(head * HDIM, (head + 1) * HDIM)
        seen = (3 if over_h else 1) * cell
        mask = band[meta[3 * (member * OWN_HEADS + head) + 2], :, :seen]
        ones = jnp.ones((seen, HDIM), jnp.bfloat16)
        for tile in range(inner // cell):
            rows = pl.ds((tile + (0 if over_h else 1)) * cell, seen)
            mine = query[0, first, pl.ds(tile * cell, cell), lanes]
            total = None
            for near_step in (0, 1, 2) if over_t else (1,):
                scores = lax.dot_general(
                    mine,
                    cells[slot + near_step, 0, rows, lanes],
                    (((1,), (1,)), ((), ())),
                    preferred_element_type=jnp.float32,
                )
                start = (tile + (0 if over_h else 1)) * cell
                allowed = mask * valid[first + near_step, :, start : start + seen]
                terms = jnp.exp2(scores * scale).astype(jnp.bfloat16) * allowed
                both = jnp.concatenate([cells[slot + near_step, 1, rows, lanes], ones], axis=1)
                part = jnp.dot(terms, both, preferred_element_type=jnp.float32)
                total = part if total is None else total + part
            here = real[tile * cell : (tile + 1) * cell] > 0
            weight = jnp.where(here, total[:, HDIM:], 1.0)
            result = jnp.where(here, total[:, :HDIM] / weight, 0.0)
            out[0, pl.ds(tile * cell, cell), lanes] = result.astype(out.dtype)

    for head in range(OWN_HEADS):
        reach_t, reach_h = (meta[3 * (member * OWN_HEADS + head) + i] for i in range(2))
        for over_t in (False, True):
            for over_h in (False, True):
                pl.when(((reach_t > 0) == over_t) & ((reach_h > 0) == over_h))(
                    functools.partial(attend, result_cells, head, over_t, over_h)
                )

    for index, out in enumerate(outs):
        pl.when(step // near == index)(functools.partial(out.__setitem__, step % near, result_cells[0]))


def attend(meta, query, near_set, far_set, borders, valid, far, pieces):
    _, chip_frames, cell, _ = near_set[0].shape
    inner = 2 * cell
    span = 4 * cell
    near = chip_frames // CORES
    sets = (*far_set, *near_set) if far else (*near_set, *far_set)
    parts = [*sets, *(p for pair in borders for p in pair)]
    count = len(pieces)
    vmem = pl.BlockSpec(memory_space=pltpu.VMEM)
    piece = jax.ShapeDtypeStruct((near, inner, SPAN), jnp.bfloat16)
    return pl.pallas_call(
        functools.partial(
            attend_body, near=near, far=far, sides=len(borders), cell=cell, inner=inner, pieces=pieces
        ),
        grid_spec=pltpu.PrefetchScalarGridSpec(
            num_scalar_prefetch=1,
            grid=(),
            in_specs=[vmem] * (len(parts) + 2),
            out_specs=[vmem] * count,
            scratch_shapes=[
                pltpu.VMEM((chip_frames + 2, 2, span, SPAN), jnp.bfloat16),
                pltpu.VMEM((3, cell, 3 * cell), jnp.bfloat16),
                pltpu.VMEM((1, inner, SPAN), jnp.bfloat16),
            ],
        ),
        out_shape=[piece] * count,
        compiler_params=pltpu.CompilerParams(vmem_limit_bytes=24 * MIB),
        cost_estimate=pl.CostEstimate(
            flops=OWN_HEADS * count * near * inner * 9 * cell * HDIM * 6,
            bytes_accessed=4 * SPAN * (near * count + 2) * span + 4 * SPAN * near * count * inner,
            transcendentals=OWN_HEADS * count * near * inner * 9 * cell,
        ),
    )(meta, query, *parts, valid)


def collect_body(member, *rest):
    out = rest[-1]
    for flip, piece in enumerate(rest[:-1]):
        column = pl.multiple_of((member[0] ^ flip) * SPAN, SPAN)
        out[:, pl.ds(column, SPAN)] = piece[...]


def collect(member, pieces):
    rows = pieces[0].shape[0]
    whole = pl.BlockSpec((rows, SPAN), lambda i, m: (0, 0))
    return pl.pallas_call(
        collect_body,
        grid_spec=pltpu.PrefetchScalarGridSpec(
            num_scalar_prefetch=1,
            grid=(1,),
            in_specs=[whole] * MATES,
            out_specs=pl.BlockSpec((rows, HEADS * HDIM), lambda i, m: (0, 0)),
        ),
        out_shape=jax.ShapeDtypeStruct((rows, HEADS * HDIM), jnp.bfloat16),
        compiler_params=pltpu.CompilerParams(vmem_limit_bytes=16 * MIB),
    )(member.reshape(1), *pieces)


def gather_lines(share):
    return [share] + [swap(share, "height", d) for d in range(1, lax.axis_size("height"))]


def gather_blocks(lines, spots, places):
    blocks = list(lines)
    for e in range(1, lax.axis_size("rest")):
        blocks += [swap(line, "rest", e) for line in lines]
    depth = lines[0].shape[0] // MATES
    if depth % 16:
        pieces = jnp.concatenate(blocks, axis=0).reshape(-1, depth, lines[0].shape[1])
        ordered = jnp.zeros_like(pieces).at[jnp.stack(places)].set(pieces)
        return [ordered.reshape(-1, pieces.shape[2])], (None,)
    return blocks, spots


def per_device(tokens, mod_scale, mod_shift, w_qkv, q_gain, k_gain, window, valid):
    frames, rows, width, features = tokens.shape
    count = frames * rows * width
    inner = rows * width
    model = w_qkv.shape[1] // 3
    rest, pair, core, height = (lax.axis_index(a) for a in ("rest", "pair", "core", "height"))
    member = pair * CORES + core
    high = lax.axis_size("height")
    many = lax.axis_size("rest")
    r_odd = rest % 2

    def columns_of(mate):
        return jnp.concatenate(
            [lax.dynamic_slice_in_dim(w_qkv, s * model + mate * SPAN, SPAN, axis=1) for s in range(3)], axis=1
        )

    shares = [columns_of(member)] + [swap(columns_of(member ^ flip), TEAM, flip) for flip in range(1, MATES)]
    stacked = jnp.concatenate(shares, axis=0)
    kv_share, q_share = stacked[:, SPAN:], stacked[:, :SPAN]
    flat = tokens.reshape(count, features)
    cut = count * 5 // 8 // width * width
    mine, most, last_rows = modulate(flat, mod_scale, mod_shift, cut, width)
    most, kv_share, q_share = lax.optimization_barrier((most, kv_share, q_share))

    meta = jnp.concatenate(
        [
            window.reshape(-1),
            jnp.stack([member, pair, core, height % 2, r_odd, rest, height]).astype(jnp.int32),
        ]
    )
    total_frames = MATES * frames
    valid_pad = jnp.pad(valid, ((TT, TT), (TH, TH), (0, 0)))
    around = lax.dynamic_slice(
        valid_pad,
        (rest * total_frames, height * rows, jnp.int32(0)),
        (total_frames + 2 * TT, rows + 2 * TH, width),
    )
    seen = (around > 0).astype(jnp.bfloat16).reshape(total_frames + 2 * TT, 1, -1)

    spots, places = [], []
    for e in range(many):
        for d in range(high):
            for j in range(MATES):
                spots.append((e, j, d, high))
                places.append(((rest ^ e) * MATES + (member ^ j)) * high + (height ^ d))
    kv_lines = gather_lines(kv_share)
    q_share, kv_lines[-1] = lax.optimization_barrier((q_share, kv_lines[-1]))
    kv_blocks, kv_spots = gather_blocks(kv_lines, tuple(spots), places)

    across = [swap(most, "pair", 1)]
    held = kv_blocks[: 2 * high - 1]
    nearest = swap(q_share, "height", 1)
    across[0], meta, seen, last_rows, mates, held, q_share, nearest = lax.optimization_barrier(
        (across[0], meta, seen, last_rows, mine, held, q_share, nearest)
    )
    kv_blocks[: 2 * high - 1] = held
    across.append(swap(last_rows, "pair", 1))
    beside = swap(mates, "core", 1)
    q_lines = [q_share, nearest] + [swap(q_share, "height", d) for d in range(2, high)]
    q_lines[0], beside = lax.optimization_barrier((q_lines[0], beside))
    q_blocks, q_spots = gather_blocks(q_lines, tuple(spots), places)

    def cells_of(tokens):
        return project(meta, tokens, frames, kv_blocks, kv_spots, k_gain, 2, 1, True)

    def exchanged(even, odd):
        return (even, odd, swap_neighbours(even, "height", 0), swap_neighbours(odd, "height", 1))

    even, odd = cells_of([[mine], [beside]])
    near_set = exchanged(even, odd)
    begun = q_blocks[: high + 2]
    _, across, begun = lax.optimization_barrier((even, across, begun))
    q_blocks[: high + 2] = begun
    beyond = [swap(x, "core", 1) for x in across]
    even, odd = cells_of([across, beyond])
    far_set = exchanged(even, odd)

    def border(side):
        last = r_odd == side
        chosen = jnp.where(last, 1, 0) == pair
        frame = jnp.stack(
            [
                jnp.where(
                    chosen,
                    jnp.where(last, a[:, -1], a[:, 0]),
                    jnp.where(last, b[:, -1], b[:, 0]),
                )
                for a, b in zip(near_set[:2], far_set[:2])
            ]
        )
        frame, *back = lax.optimization_barrier((swap_neighbours(frame, "rest", side), *near_set[2:]))
        return frame, swap_neighbours(frame[0], "height", 0), swap_neighbours(frame[1], "height", 1)

    borders = [border(side) for side in range(min(2, many - 1))]
    q_blocks[0], even = lax.optimization_barrier((q_blocks[0], even))
    far_set = (even, *far_set[1:])
    everyone = [[mine], [beside], across, beyond]
    (query,) = project(meta, everyone, frames, q_blocks, q_spots, q_gain, 1, 1, False)
    query, *far_back = lax.optimization_barrier((query, *far_set[2:]))
    far_set = (*far_set[:2], *far_back)

    parts = (query, near_set, far_set, borders, seen)
    travelled = []
    for flip in range(CORES):
        (out,) = attend(meta, *parts, True, (flip,))
        meta, out = lax.optimization_barrier((meta, out))
        travelled.append(swap(out.reshape(count, SPAN), TEAM, CORES + flip))
    meta, travelled[0] = lax.optimization_barrier((meta, travelled[0]))
    near_out = attend(meta, *parts, False, (0, 1))
    other, *travelled = lax.optimization_barrier((near_out[1], *travelled))
    pieces = [near_out[0].reshape(count, SPAN), swap(other.reshape(count, SPAN), TEAM, 1), *travelled]
    return collect(member.astype(jnp.int32), pieces).reshape(frames, rows, width, model)


def solution(mesh):
    split = Mesh(
        mesh.devices.reshape(mesh.shape["tm"] // MATES, MATES // CORES, CORES, mesh.shape["height"]),
        ("rest", "pair", "core", "height"),
    )
    along = ("rest", "pair", "core")
    in_specs = (
        P(along, "height", None, None),
        P(),
        P(),
        P((*along, "height"), None),
        P(),
        P(),
        P(),
        P(),
    )
    out_specs = P(along, "height", None, None)
    return jax.shard_map(
        per_device, mesh=split, in_specs=in_specs, out_specs=out_specs, check_vma=False
    )
```

```python
import functools

import jax
import jax.numpy as jnp
import numpy as np
from jax import lax
from jax.experimental import pallas as pl
from jax.experimental.pallas import tpu as pltpu
from jax.sharding import Mesh
from jax.sharding import PartitionSpec as P

HDIM = 128
HEADS = 12
TT = 1
TH = 2
TW = 8
CORES = 2
MATES = 4
OWN_HEADS = HEADS // MATES
SPAN = OWN_HEADS * HDIM
EPS = 1e-06
MIB = 1024 * 1024
TEAM = ("pair", "core")

MEMBER, PAIR, CORE, Z_ODD, R_ODD, REST, HEIGHT = (3 * HEADS + i for i in range(7))


def swap(x, axis, flip):
    names = axis if isinstance(axis, tuple) else (axis,)
    count = int(np.prod([lax.axis_size(name) for name in names]))
    return lax.ppermute(x, axis, [(i, i ^ flip) for i in range(count)])


def swap_neighbours(x, axis, odd):
    count = lax.axis_size(axis)
    pairs = [(i, i + 1) for i in range(odd, count - 1, 2)]
    flat = x.reshape(-1, x.shape[-1])
    return lax.ppermute(flat, axis, pairs + [(j, i) for i, j in pairs]).reshape(x.shape)


def modulate_body(tokens, scale, shift, whole, first, second, *, steps):
    values = tokens[...].astype(jnp.float32)
    centred = values - jnp.mean(values, axis=-1, keepdims=True)
    variance = jnp.mean(centred * centred, axis=-1, keepdims=True)
    normed = centred * lax.rsqrt(variance + EPS)
    result = (normed * (1.0 + scale[...]) + shift[...]).astype(whole.dtype)
    whole[...] = result
    step = pl.program_id(0)
    pl.when(step < steps)(functools.partial(first.__setitem__, ..., result))
    pl.when(step >= steps)(functools.partial(second.__setitem__, ..., result))


def modulate(tokens, scale, shift, cut, block):
    count, features = tokens.shape
    steps = cut // block
    row = lambda place: pl.BlockSpec((block, features), lambda i: (place(i), 0))
    whole = pl.BlockSpec((1, features), lambda i: (0, 0))
    rows = lambda length: jax.ShapeDtypeStruct((length, features), jnp.bfloat16)
    return pl.pallas_call(
        functools.partial(modulate_body, steps=steps),
        grid=(count // block,),
        in_specs=[row(lambda i: i), whole, whole],
        out_specs=[
            row(lambda i: i),
            row(lambda i: jnp.minimum(i, steps - 1)),
            row(lambda i: jnp.maximum(i - steps, 0)),
        ],
        out_shape=[rows(count), rows(cut), rows(count - cut)],
        compiler_params=pltpu.CompilerParams(vmem_limit_bytes=12 * MIB),
        cost_estimate=pl.CostEstimate(
            flops=12 * count * features, bytes_accessed=6 * count * features, transcendentals=0
        ),
    )(tokens, scale.reshape(1, features), shift.reshape(1, features))


def project_body(meta, *rest, groups, frames, arrays, depth, spots, normed, halves):
    sources, members = sum(groups), len(groups)
    xs, blocks, gain = rest[:sources], rest[sources : sources + arrays], rest[sources + arrays]
    outs, (rows, weights, row_sems, weight_sems) = rest[sources + arrays + 1 : -4], rest[-4:]
    columns = weights.shape[1]
    count = rows.shape[0] // members
    inner = count // frames
    cell = inner // 2

    loads, first = [], 0
    for i, x in enumerate(xs):
        loads.append(pltpu.make_async_copy(x, rows.at[pl.ds(first, x.shape[0]), :], row_sems.at[i]))
        first += x.shape[0]
    wide = 2 * HDIM
    spans = [(start, min(start + wide, columns)) for start in range(0, columns, wide)]
    copies = [[] for _ in spans]
    for p, spot in enumerate(spots):
        place = 0
        if spot is not None:
            e, j, d, high = spot
            place = ((meta[REST] ^ e) * MATES + (meta[MEMBER] ^ j)) * high + (meta[HEIGHT] ^ d)
        held = len(spots) // arrays
        row = pl.multiple_of(place * depth, depth)
        for group, (start, stop) in enumerate(spans):
            source = blocks[p // held].at[pl.ds(p % held * depth, depth), start:stop]
            goal = weights.at[pl.ds(row, depth), start:stop]
            copies[group].append(pltpu.make_async_copy(source, goal, weight_sems.at[group, p]))
    for copy in [*loads[: groups[0]], *copies[0], *loads[groups[0] :]]:
        copy.start()
    for group in copies[1:]:
        for copy in group:
            copy.start()
    for group, (start, stop) in enumerate(spans):
        for copy in copies[group]:
            copy.wait()
        for i in range(members):
            if group == 0:
                for load in loads[sum(groups[:i]) : sum(groups[: i + 1])]:
                    load.wait()
            total = jnp.dot(
                rows[i * count : (i + 1) * count, :], weights[:, start:stop], preferred_element_type=jnp.float32
            )
            for column in range(start, stop, HDIM):
                head = total[:, column - start : column - start + HDIM]
                part, offset = divmod(column, SPAN)
                if part < normed:
                    power = jnp.mean(head * head, axis=-1, keepdims=True)
                    head = head * lax.rsqrt(power + EPS) * gain[...]
                head = head.astype(jnp.bfloat16)
                lanes = slice(offset, offset + HDIM)
                for frame in range(frames):
                    place = (meta[CORE if halves else MEMBER] ^ i) * frames + frame
                    one = head[frame * inner : (frame + 1) * inner]
                    if halves:
                        top, bottom = one[:cell], one[cell:]
                        odd = meta[Z_ODD] == 1
                        outs[0][part, place, :, lanes] = jnp.where(odd, top, bottom)
                        outs[1][part, place, :, lanes] = jnp.where(odd, bottom, top)
                    else:
                        outs[0][part, place, :, lanes] = one


def project(meta, tokens, frames, blocks, spots, gain, parts, normed, halves):
    members = len(tokens)
    groups = tuple(len(pieces) for pieces in tokens)
    sources = [x for pieces in tokens for x in pieces]
    features = sources[0].shape[1]
    total = sum(x.shape[0] for x in sources)
    inner = total // members // frames
    columns = blocks[0].shape[1]
    count = len(sources)
    any_space = pl.BlockSpec(memory_space=pl.ANY)
    vmem = pl.BlockSpec(memory_space=pltpu.VMEM)
    outs = 2 if halves else 1
    return pl.pallas_call(
        functools.partial(
            project_body,
            groups=groups,
            frames=frames,
            arrays=len(blocks),
            depth=features // len(spots),
            spots=spots,
            normed=normed,
            halves=halves,
        ),
        grid_spec=pltpu.PrefetchScalarGridSpec(
            num_scalar_prefetch=1,
            grid=(),
            in_specs=[any_space] * (count + len(blocks)) + [vmem],
            out_specs=[vmem] * outs,
            scratch_shapes=[
                pltpu.VMEM((total, features), jnp.bfloat16),
                pltpu.VMEM((features, columns), jnp.bfloat16),
                pltpu.SemaphoreType.DMA((count,)),
                pltpu.SemaphoreType.DMA((-(-columns // (2 * HDIM)), len(spots))),
            ],
        ),
        out_shape=[jax.ShapeDtypeStruct((parts, members * frames, inner // outs, SPAN), jnp.bfloat16)] * outs,
        compiler_params=pltpu.CompilerParams(vmem_limit_bytes=24 * MIB),
        cost_estimate=pl.CostEstimate(
            flops=2 * total * features * columns,
            bytes_accessed=2 * features * columns + 2 * total * (features + columns),
            transcendentals=0,
        ),
    )(meta, *sources, *blocks, gain.reshape(1, HDIM))


def attend_body(meta, *rest, near, far, sides, cell, inner, pieces):
    count = len(pieces)
    query, main = rest[0], rest[1 : -4 - count]
    valid, outs = rest[-4 - count], rest[-3 - count : -3]
    cells, band, result_cells = rest[-3:]
    member, pair, core, z_odd, r_odd = (meta[i] for i in (MEMBER, PAIR, CORE, Z_ODD, R_ODD))
    chip = 1 - pair if far else pair
    width = cell // TH
    frames = cells.shape[0] - 2

    row_of = [jnp.where(z_odd == 1, a, b) * cell for a, b in ((1, 2), (2, 1), (0, 3), (3, 0))]
    own_set, other_set, borders = main[0:4], main[4:8], main[8:]
    own_frame = lambda i: tuple(part[:, i] for part in own_set)
    other_frame = lambda i: tuple(part[:, i] for part in other_set)

    def load(slot, found):
        for part, row in zip(found(), row_of):
            rows = pl.ds(pl.multiple_of(row, cell), cell)
            cells[slot, :, rows, :] = part

    def border(side):
        frame, even, odd = borders[3 * side : 3 * side + 3]
        return frame[0], frame[1], even[...], odd[...]

    low = jnp.bool_(True) if count > 1 else (core ^ pieces[0]) == 0
    high = jnp.bool_(True) if count > 1 else (core ^ pieces[0]) == 1
    for end, slot, used in ((0, 0, low), (1, frames + 1, high)):
        found = functools.partial(other_frame, 0 if end else frames - 1)
        pl.when(used & (chip != end))(functools.partial(load, slot, found))
        for side in range(sides):
            pl.when(used & (chip == end) & ((r_odd == 1) == (end == side)))(
                functools.partial(load, slot, functools.partial(border, side))
            )

        if sides < 2:

            @pl.when(used & (chip == end) & ((r_odd == 1) == (end == 1)))
            def _():
                cells[slot] = jnp.zeros(cells.shape[1:], cells.dtype)

    for index in range(frames):
        slot = index + 1
        found = functools.partial(own_frame, index)
        if near <= slot <= near + 1:
            load(slot, found)
        else:
            pl.when(low if slot < near else high)(functools.partial(load, slot, found))
    q_tile = lax.broadcasted_iota(jnp.int32, (cell, 3 * cell), 0)
    k_tile = lax.broadcasted_iota(jnp.int32, (cell, 3 * cell), 1)
    apart = jnp.abs(lax.rem(q_tile, width) // TW - lax.rem(k_tile, width) // TW)
    for reach in range(3):
        band[reach] = jnp.where(apart <= reach, 1.0, 0.0).astype(band.dtype)

    def serve(step, carry):
        slot = (core ^ pieces[0] ^ (step // near)) * near + step % near
        attend_frame(
            meta, query, valid, outs, cells, band, result_cells, step, slot, chip * frames + slot, near, cell, inner
        )
        return carry

    lax.fori_loop(0, near * count, serve, 0)


def attend_frame(
    meta, query, valid, outs, cells, band, result_cells, step, slot, first, near, cell, inner
):
    member = meta[MEMBER]
    scale = np.float32(np.log2(np.e) / np.sqrt(HDIM))
    mine_valid = valid[first + 1, :, cell : cell + inner].astype(jnp.float32)
    real = jnp.transpose(jnp.broadcast_to(mine_valid, (HDIM, inner)))

    def attend(out, head, over_t, over_h):
        lanes = slice(head * HDIM, (head + 1) * HDIM)
        seen = (3 if over_h else 1) * cell
        mask = band[meta[3 * (member * OWN_HEADS + head) + 2], :, :seen]
        ones = jnp.ones((seen, HDIM), jnp.bfloat16)
        for tile in range(inner // cell):
            rows = pl.ds((tile + (0 if over_h else 1)) * cell, seen)
            mine = query[0, first, pl.ds(tile * cell, cell), lanes]
            total = None
            for near_step in (0, 1, 2) if over_t else (1,):
                scores = lax.dot_general(
                    mine,
                    cells[slot + near_step, 0, rows, lanes],
                    (((1,), (1,)), ((), ())),
                    preferred_element_type=jnp.float32,
                )
                start = (tile + (0 if over_h else 1)) * cell
                allowed = mask * valid[first + near_step, :, start : start + seen]
                terms = jnp.exp2(scores * scale).astype(jnp.bfloat16) * allowed
                both = jnp.concatenate([cells[slot + near_step, 1, rows, lanes], ones], axis=1)
                part = jnp.dot(terms, both, preferred_element_type=jnp.float32)
                total = part if total is None else total + part
            here = real[tile * cell : (tile + 1) * cell] > 0
            weight = jnp.where(here, total[:, HDIM:], 1.0)
            result = jnp.where(here, total[:, :HDIM] / weight, 0.0)
            out[0, pl.ds(tile * cell, cell), lanes] = result.astype(out.dtype)

    for head in range(OWN_HEADS):
        reach_t, reach_h = (meta[3 * (member * OWN_HEADS + head) + i] for i in range(2))
        for over_t in (False, True):
            for over_h in (False, True):
                pl.when(((reach_t > 0) == over_t) & ((reach_h > 0) == over_h))(
                    functools.partial(attend, result_cells, head, over_t, over_h)
                )

    for index, out in enumerate(outs):
        pl.when(step // near == index)(functools.partial(out.__setitem__, step % near, result_cells[0]))


def attend(meta, query, near_set, far_set, borders, valid, far, pieces):
    _, chip_frames, cell, _ = near_set[0].shape
    inner = 2 * cell
    span = 4 * cell
    near = chip_frames // CORES
    sets = (*far_set, *near_set) if far else (*near_set, *far_set)
    parts = [*sets, *(p for pair in borders for p in pair)]
    count = len(pieces)
    vmem = pl.BlockSpec(memory_space=pltpu.VMEM)
    piece = jax.ShapeDtypeStruct((near, inner, SPAN), jnp.bfloat16)
    return pl.pallas_call(
        functools.partial(
            attend_body, near=near, far=far, sides=len(borders), cell=cell, inner=inner, pieces=pieces
        ),
        grid_spec=pltpu.PrefetchScalarGridSpec(
            num_scalar_prefetch=1,
            grid=(),
            in_specs=[vmem] * (len(parts) + 2),
            out_specs=[vmem] * count,
            scratch_shapes=[
                pltpu.VMEM((chip_frames + 2, 2, span, SPAN), jnp.bfloat16),
                pltpu.VMEM((3, cell, 3 * cell), jnp.bfloat16),
                pltpu.VMEM((1, inner, SPAN), jnp.bfloat16),
            ],
        ),
        out_shape=[piece] * count,
        compiler_params=pltpu.CompilerParams(vmem_limit_bytes=24 * MIB),
        cost_estimate=pl.CostEstimate(
            flops=OWN_HEADS * count * near * inner * 9 * cell * HDIM * 6,
            bytes_accessed=4 * SPAN * (near * count + 2) * span + 4 * SPAN * near * count * inner,
            transcendentals=OWN_HEADS * count * near * inner * 9 * cell,
        ),
    )(meta, query, *parts, valid)


def collect_body(member, *rest):
    out = rest[-1]
    for flip, piece in enumerate(rest[:-1]):
        column = pl.multiple_of((member[0] ^ flip) * SPAN, SPAN)
        out[:, pl.ds(column, SPAN)] = piece[...]


def collect(member, pieces):
    rows = pieces[0].shape[0]
    whole = pl.BlockSpec((rows, SPAN), lambda i, m: (0, 0))
    return pl.pallas_call(
        collect_body,
        grid_spec=pltpu.PrefetchScalarGridSpec(
            num_scalar_prefetch=1,
            grid=(1,),
            in_specs=[whole] * MATES,
            out_specs=pl.BlockSpec((rows, HEADS * HDIM), lambda i, m: (0, 0)),
        ),
        out_shape=jax.ShapeDtypeStruct((rows, HEADS * HDIM), jnp.bfloat16),
        compiler_params=pltpu.CompilerParams(vmem_limit_bytes=16 * MIB),
    )(member.reshape(1), *pieces)


def gather_lines(share):
    return [share] + [swap(share, "height", d) for d in range(1, lax.axis_size("height"))]


def gather_blocks(lines, spots, places):
    blocks = list(lines)
    for e in range(1, lax.axis_size("rest")):
        blocks += [swap(line, "rest", e) for line in lines]
    depth = lines[0].shape[0] // MATES
    if depth % 16:
        pieces = jnp.concatenate(blocks, axis=0).reshape(-1, depth, lines[0].shape[1])
        ordered = jnp.zeros_like(pieces).at[jnp.stack(places)].set(pieces)
        return [ordered.reshape(-1, pieces.shape[2])], (None,)
    return blocks, spots


def per_device(tokens, mod_scale, mod_shift, w_qkv, q_gain, k_gain, window, valid):
    frames, rows, width, features = tokens.shape
    count = frames * rows * width
    inner = rows * width
    model = w_qkv.shape[1] // 3
    rest, pair, core, height = (lax.axis_index(a) for a in ("rest", "pair", "core", "height"))
    member = pair * CORES + core
    high = lax.axis_size("height")
    many = lax.axis_size("rest")
    r_odd = rest % 2

    def columns_of(mate):
        return jnp.concatenate(
            [lax.dynamic_slice_in_dim(w_qkv, s * model + mate * SPAN, SPAN, axis=1) for s in range(3)], axis=1
        )

    shares = [columns_of(member)] + [swap(columns_of(member ^ flip), TEAM, flip) for flip in range(1, MATES)]
    stacked = jnp.concatenate(shares, axis=0)
    kv_share, q_share = stacked[:, SPAN:], stacked[:, :SPAN]
    flat = tokens.reshape(count, features)
    cut = count * 5 // 8 // width * width
    mine, most, last_rows = modulate(flat, mod_scale, mod_shift, cut, width)
    most, kv_share, q_share = lax.optimization_barrier((most, kv_share, q_share))

    meta = jnp.concatenate(
        [
            window.reshape(-1),
            jnp.stack([member, pair, core, height % 2, r_odd, rest, height]).astype(jnp.int32),
        ]
    )
    total_frames = MATES * frames
    valid_pad = jnp.pad(valid, ((TT, TT), (TH, TH), (0, 0)))
    around = lax.dynamic_slice(
        valid_pad,
        (rest * total_frames, height * rows, jnp.int32(0)),
        (total_frames + 2 * TT, rows + 2 * TH, width),
    )
    seen = (around > 0).astype(jnp.bfloat16).reshape(total_frames + 2 * TT, 1, -1)

    spots, places = [], []
    for e in range(many):
        for d in range(high):
            for j in range(MATES):
                spots.append((e, j, d, high))
                places.append(((rest ^ e) * MATES + (member ^ j)) * high + (height ^ d))
    kv_lines = gather_lines(kv_share)
    q_share, kv_lines[-1] = lax.optimization_barrier((q_share, kv_lines[-1]))
    kv_blocks, kv_spots = gather_blocks(kv_lines, tuple(spots), places)

    across = [swap(most, "pair", 1)]
    held = kv_blocks[: 2 * high - 1]
    across[0], meta, seen, last_rows, mates, held = lax.optimization_barrier(
        (across[0], meta, seen, last_rows, mine, held)
    )
    kv_blocks[: 2 * high - 1] = held
    across.append(swap(last_rows, "pair", 1))
    beside = swap(mates, "core", 1)
    nearest = swap(q_share, "height", 1)
    q_share, nearest = lax.optimization_barrier((q_share, nearest))
    q_lines = [q_share, nearest] + [swap(q_share, "height", d) for d in range(2, high)]
    q_lines[0], beside = lax.optimization_barrier((q_lines[0], beside))
    kv_blocks[0], q_lines[1] = lax.optimization_barrier((kv_blocks[0], q_lines[1]))
    q_blocks, q_spots = gather_blocks(q_lines, tuple(spots), places)

    def cells_of(tokens):
        return project(meta, tokens, frames, kv_blocks, kv_spots, k_gain, 2, 1, True)

    def exchanged(even, odd):
        return (even, odd, swap_neighbours(even, "height", 0), swap_neighbours(odd, "height", 1))

    even, odd = cells_of([[mine], [beside]])
    near_set = exchanged(even, odd)
    begun = q_blocks[: high + 2]
    _, across, begun = lax.optimization_barrier((even, across, begun))
    q_blocks[: high + 2] = begun
    beyond = [swap(x, "core", 1) for x in across]
    even, odd = cells_of([across, beyond])
    far_set = exchanged(even, odd)

    def border(side):
        last = r_odd == side
        chosen = jnp.where(last, 1, 0) == pair
        frame = jnp.stack(
            [
                jnp.where(
                    chosen,
                    jnp.where(last, a[:, -1], a[:, 0]),
                    jnp.where(last, b[:, -1], b[:, 0]),
                )
                for a, b in zip(near_set[:2], far_set[:2])
            ]
        )
        frame, *back = lax.optimization_barrier((swap_neighbours(frame, "rest", side), *near_set[2:]))
        return frame, swap_neighbours(frame[0], "height", 0), swap_neighbours(frame[1], "height", 1)

    borders = [border(side) for side in range(min(2, many - 1))]
    q_blocks[0], even = lax.optimization_barrier((q_blocks[0], even))
    far_set = (even, *far_set[1:])
    everyone = [[mine], [beside], across, beyond]
    (query,) = project(meta, everyone, frames, q_blocks, q_spots, q_gain, 1, 1, False)
    query, *far_back = lax.optimization_barrier((query, *far_set[2:]))
    far_set = (*far_set[:2], *far_back)

    parts = (query, near_set, far_set, borders, seen)
    travelled = []
    for flip in range(CORES):
        (out,) = attend(meta, *parts, True, (flip,))
        meta, out = lax.optimization_barrier((meta, out))
        travelled.append(swap(out.reshape(count, SPAN), TEAM, CORES + flip))
    (other,) = attend(meta, *parts, False, (1,))
    meta, other, travelled[0] = lax.optimization_barrier((meta, other, travelled[0]))
    (own,) = attend(meta, *parts, False, (0,))
    pieces = [own.reshape(count, SPAN), swap(other.reshape(count, SPAN), TEAM, 1), *travelled]
    return collect(member.astype(jnp.int32), pieces).reshape(frames, rows, width, model)


def solution(mesh):
    split = Mesh(
        mesh.devices.reshape(mesh.shape["tm"] // MATES, MATES // CORES, CORES, mesh.shape["height"]),
        ("rest", "pair", "core", "height"),
    )
    along = ("rest", "pair", "core")
    in_specs = (
        P(along, "height", None, None),
        P(),
        P(),
        P((*along, "height"), None),
        P(),
        P(),
        P(),
        P(),
    )
    out_specs = P(along, "height", None, None)
    return jax.shard_map(
        per_device, mesh=split, in_specs=in_specs, out_specs=out_specs, check_vma=False
    )
```

```python
import functools

import jax
import jax.numpy as jnp
import numpy as np
from jax import lax
from jax.experimental import pallas as pl
from jax.experimental.pallas import tpu as pltpu
from jax.sharding import Mesh
from jax.sharding import PartitionSpec as P

HDIM = 128
HEADS = 12
TT = 1
TH = 2
TW = 8
CORES = 2
MATES = 4
OWN_HEADS = HEADS // MATES
SPAN = OWN_HEADS * HDIM
EPS = 1e-06
MIB = 1024 * 1024
TEAM = ("pair", "core")

MEMBER, PAIR, CORE, Z_ODD, R_ODD, REST, HEIGHT = (3 * HEADS + i for i in range(7))


def swap(x, axis, flip):
    names = axis if isinstance(axis, tuple) else (axis,)
    count = int(np.prod([lax.axis_size(name) for name in names]))
    return lax.ppermute(x, axis, [(i, i ^ flip) for i in range(count)])


def swap_neighbours(x, axis, odd):
    count = lax.axis_size(axis)
    pairs = [(i, i + 1) for i in range(odd, count - 1, 2)]
    flat = x.reshape(-1, x.shape[-1])
    return lax.ppermute(flat, axis, pairs + [(j, i) for i, j in pairs]).reshape(x.shape)


def modulate_body(tokens, scale, shift, whole, first, second, *, steps):
    values = tokens[...].astype(jnp.float32)
    centred = values - jnp.mean(values, axis=-1, keepdims=True)
    variance = jnp.mean(centred * centred, axis=-1, keepdims=True)
    normed = centred * lax.rsqrt(variance + EPS)
    result = (normed * (1.0 + scale[...]) + shift[...]).astype(whole.dtype)
    whole[...] = result
    step = pl.program_id(0)
    pl.when(step < steps)(functools.partial(first.__setitem__, ..., result))
    pl.when(step >= steps)(functools.partial(second.__setitem__, ..., result))


def modulate(tokens, scale, shift, cut, block):
    count, features = tokens.shape
    steps = cut // block
    row = lambda place: pl.BlockSpec((block, features), lambda i: (place(i), 0))
    whole = pl.BlockSpec((1, features), lambda i: (0, 0))
    rows = lambda length: jax.ShapeDtypeStruct((length, features), jnp.bfloat16)
    return pl.pallas_call(
        functools.partial(modulate_body, steps=steps),
        grid=(count // block,),
        in_specs=[row(lambda i: i), whole, whole],
        out_specs=[
            row(lambda i: i),
            row(lambda i: jnp.minimum(i, steps - 1)),
            row(lambda i: jnp.maximum(i - steps, 0)),
        ],
        out_shape=[rows(count), rows(cut), rows(count - cut)],
        compiler_params=pltpu.CompilerParams(vmem_limit_bytes=12 * MIB),
        cost_estimate=pl.CostEstimate(
            flops=12 * count * features, bytes_accessed=6 * count * features, transcendentals=0
        ),
    )(tokens, scale.reshape(1, features), shift.reshape(1, features))


def project_body(meta, *rest, groups, frames, arrays, depth, spots, normed, halves):
    sources, members = sum(groups), len(groups)
    xs, blocks, gain = rest[:sources], rest[sources : sources + arrays], rest[sources + arrays]
    outs, (rows, weights, row_sems, weight_sems) = rest[sources + arrays + 1 : -4], rest[-4:]
    columns = weights.shape[1]
    count = rows.shape[0] // members
    inner = count // frames
    cell = inner // 2

    loads, first = [], 0
    for i, x in enumerate(xs):
        loads.append(pltpu.make_async_copy(x, rows.at[pl.ds(first, x.shape[0]), :], row_sems.at[i]))
        first += x.shape[0]
    copies = []
    for p, spot in enumerate(spots):
        place = 0
        if spot is not None:
            e, j, d, high = spot
            place = ((meta[REST] ^ e) * MATES + (meta[MEMBER] ^ j)) * high + (meta[HEIGHT] ^ d)
        held = len(spots) // arrays
        source = blocks[p // held].at[pl.ds(p % held * depth, depth), :]
        row = pl.multiple_of(place * depth, depth)
        copies.append(pltpu.make_async_copy(source, weights.at[pl.ds(row, depth), :], weight_sems.at[p]))
    for load in loads[: groups[0]]:
        load.start()
    for copy in copies:
        copy.start()
    for load in loads[groups[0] :]:
        load.start()
    for copy in copies:
        copy.wait()
    wide = 2 * HDIM
    for i in range(members):
        for load in loads[sum(groups[:i]) : sum(groups[: i + 1])]:
            load.wait()
        for start in range(0, columns, wide):
            stop = min(start + wide, columns)
            total = jnp.dot(
                rows[i * count : (i + 1) * count, :], weights[:, start:stop], preferred_element_type=jnp.float32
            )
            for column in range(start, stop, HDIM):
                head = total[:, column - start : column - start + HDIM]
                part, offset = divmod(column, SPAN)
                if part < normed:
                    power = jnp.mean(head * head, axis=-1, keepdims=True)
                    head = head * lax.rsqrt(power + EPS) * gain[...]
                head = head.astype(jnp.bfloat16)
                lanes = slice(offset, offset + HDIM)
                for frame in range(frames):
                    place = (meta[CORE if halves else MEMBER] ^ i) * frames + frame
                    one = head[frame * inner : (frame + 1) * inner]
                    if halves:
                        top, bottom = one[:cell], one[cell:]
                        odd = meta[Z_ODD] == 1
                        outs[0][part, place, :, lanes] = jnp.where(odd, top, bottom)
                        outs[1][part, place, :, lanes] = jnp.where(odd, bottom, top)
                    else:
                        outs[0][part, place, :, lanes] = one


def project(meta, tokens, frames, blocks, spots, gain, parts, normed, halves):
    members = len(tokens)
    groups = tuple(len(pieces) for pieces in tokens)
    sources = [x for pieces in tokens for x in pieces]
    features = sources[0].shape[1]
    total = sum(x.shape[0] for x in sources)
    inner = total // members // frames
    columns = blocks[0].shape[1]
    count = len(sources)
    any_space = pl.BlockSpec(memory_space=pl.ANY)
    vmem = pl.BlockSpec(memory_space=pltpu.VMEM)
    outs = 2 if halves else 1
    return pl.pallas_call(
        functools.partial(
            project_body,
            groups=groups,
            frames=frames,
            arrays=len(blocks),
            depth=features // len(spots),
            spots=spots,
            normed=normed,
            halves=halves,
        ),
        grid_spec=pltpu.PrefetchScalarGridSpec(
            num_scalar_prefetch=1,
            grid=(),
            in_specs=[any_space] * (count + len(blocks)) + [vmem],
            out_specs=[vmem] * outs,
            scratch_shapes=[
                pltpu.VMEM((total, features), jnp.bfloat16),
                pltpu.VMEM((features, columns), jnp.bfloat16),
                pltpu.SemaphoreType.DMA((count,)),
                pltpu.SemaphoreType.DMA((len(spots),)),
            ],
        ),
        out_shape=[jax.ShapeDtypeStruct((parts, members * frames, inner // outs, SPAN), jnp.bfloat16)] * outs,
        compiler_params=pltpu.CompilerParams(vmem_limit_bytes=24 * MIB),
        cost_estimate=pl.CostEstimate(
            flops=2 * total * features * columns,
            bytes_accessed=2 * features * columns + 2 * total * (features + columns),
            transcendentals=0,
        ),
    )(meta, *sources, *blocks, gain.reshape(1, HDIM))


def attend_body(meta, *rest, near, far, sides, cell, inner, pieces):
    count = len(pieces)
    query, main = rest[0], rest[1 : -4 - count]
    valid, outs = rest[-4 - count], rest[-3 - count : -3]
    cells, band, result_cells = rest[-3:]
    member, pair, core, z_odd, r_odd = (meta[i] for i in (MEMBER, PAIR, CORE, Z_ODD, R_ODD))
    chip = 1 - pair if far else pair
    width = cell // TH
    frames = cells.shape[0] - 2

    row_of = [jnp.where(z_odd == 1, a, b) * cell for a, b in ((1, 2), (2, 1), (0, 3), (3, 0))]
    own_set, other_set, borders = main[0:4], main[4:8], main[8:]
    own_frame = lambda i: tuple(part[:, i] for part in own_set)
    other_frame = lambda i: tuple(part[:, i] for part in other_set)

    def load(slot, found):
        for part, row in zip(found(), row_of):
            rows = pl.ds(pl.multiple_of(row, cell), cell)
            cells[slot, :, rows, :] = part

    def border(side):
        frame, even, odd = borders[3 * side : 3 * side + 3]
        return frame[0], frame[1], even[...], odd[...]

    low = jnp.bool_(True) if count > 1 else (core ^ pieces[0]) == 0
    high = jnp.bool_(True) if count > 1 else (core ^ pieces[0]) == 1
    for end, slot, used in ((0, 0, low), (1, frames + 1, high)):
        found = functools.partial(other_frame, 0 if end else frames - 1)
        pl.when(used & (chip != end))(functools.partial(load, slot, found))
        for side in range(sides):
            pl.when(used & (chip == end) & ((r_odd == 1) == (end == side)))(
                functools.partial(load, slot, functools.partial(border, side))
            )

        if sides < 2:

            @pl.when(used & (chip == end) & ((r_odd == 1) == (end == 1)))
            def _():
                cells[slot] = jnp.zeros(cells.shape[1:], cells.dtype)

    for index in range(frames):
        slot = index + 1
        found = functools.partial(own_frame, index)
        if near <= slot <= near + 1:
            load(slot, found)
        else:
            pl.when(low if slot < near else high)(functools.partial(load, slot, found))
    q_tile = lax.broadcasted_iota(jnp.int32, (cell, 3 * cell), 0)
    k_tile = lax.broadcasted_iota(jnp.int32, (cell, 3 * cell), 1)
    apart = jnp.abs(lax.rem(q_tile, width) // TW - lax.rem(k_tile, width) // TW)
    for reach in range(3):
        band[reach] = jnp.where(apart <= reach, 1.0, 0.0).astype(band.dtype)

    def serve(step, carry):
        slot = (core ^ pieces[0] ^ (step // near)) * near + step % near
        attend_frame(
            meta, query, valid, outs, cells, band, result_cells, step, slot, chip * frames + slot, near, cell, inner
        )
        return carry

    lax.fori_loop(0, near * count, serve, 0)


def attend_frame(
    meta, query, valid, outs, cells, band, result_cells, step, slot, first, near, cell, inner
):
    member = meta[MEMBER]
    scale = np.float32(np.log2(np.e) / np.sqrt(HDIM))
    mine_valid = valid[first + 1, :, cell : cell + inner].astype(jnp.float32)
    real = jnp.transpose(jnp.broadcast_to(mine_valid, (HDIM, inner)))

    def attend(out, head, over_t, over_h):
        lanes = slice(head * HDIM, (head + 1) * HDIM)
        seen = (3 if over_h else 1) * cell
        mask = band[meta[3 * (member * OWN_HEADS + head) + 2], :, :seen]
        ones = jnp.ones((seen, HDIM), jnp.bfloat16)
        for tile in range(inner // cell):
            rows = pl.ds((tile + (0 if over_h else 1)) * cell, seen)
            mine = query[0, first, pl.ds(tile * cell, cell), lanes]
            total = None
            for near_step in (0, 1, 2) if over_t else (1,):
                scores = lax.dot_general(
                    mine,
                    cells[slot + near_step, 0, rows, lanes],
                    (((1,), (1,)), ((), ())),
                    preferred_element_type=jnp.float32,
                )
                start = (tile + (0 if over_h else 1)) * cell
                allowed = mask * valid[first + near_step, :, start : start + seen]
                terms = jnp.exp2(scores * scale).astype(jnp.bfloat16) * allowed
                both = jnp.concatenate([cells[slot + near_step, 1, rows, lanes], ones], axis=1)
                part = jnp.dot(terms, both, preferred_element_type=jnp.float32)
                total = part if total is None else total + part
            here = real[tile * cell : (tile + 1) * cell] > 0
            weight = jnp.where(here, total[:, HDIM:], 1.0)
            result = jnp.where(here, total[:, :HDIM] / weight, 0.0)
            out[0, pl.ds(tile * cell, cell), lanes] = result.astype(out.dtype)

    for head in range(OWN_HEADS):
        reach_t, reach_h = (meta[3 * (member * OWN_HEADS + head) + i] for i in range(2))
        for over_t in (False, True):
            for over_h in (False, True):
                pl.when(((reach_t > 0) == over_t) & ((reach_h > 0) == over_h))(
                    functools.partial(attend, result_cells, head, over_t, over_h)
                )

    for index, out in enumerate(outs):
        pl.when(step // near == index)(functools.partial(out.__setitem__, step % near, result_cells[0]))


def attend(meta, query, near_set, far_set, borders, valid, far, pieces):
    _, chip_frames, cell, _ = near_set[0].shape
    inner = 2 * cell
    span = 4 * cell
    near = chip_frames // CORES
    sets = (*far_set, *near_set) if far else (*near_set, *far_set)
    parts = [*sets, *(p for pair in borders for p in pair)]
    count = len(pieces)
    vmem = pl.BlockSpec(memory_space=pltpu.VMEM)
    piece = jax.ShapeDtypeStruct((near, inner, SPAN), jnp.bfloat16)
    return pl.pallas_call(
        functools.partial(
            attend_body, near=near, far=far, sides=len(borders), cell=cell, inner=inner, pieces=pieces
        ),
        grid_spec=pltpu.PrefetchScalarGridSpec(
            num_scalar_prefetch=1,
            grid=(),
            in_specs=[vmem] * (len(parts) + 2),
            out_specs=[vmem] * count,
            scratch_shapes=[
                pltpu.VMEM((chip_frames + 2, 2, span, SPAN), jnp.bfloat16),
                pltpu.VMEM((3, cell, 3 * cell), jnp.bfloat16),
                pltpu.VMEM((1, inner, SPAN), jnp.bfloat16),
            ],
        ),
        out_shape=[piece] * count,
        compiler_params=pltpu.CompilerParams(vmem_limit_bytes=24 * MIB),
        cost_estimate=pl.CostEstimate(
            flops=OWN_HEADS * count * near * inner * 9 * cell * HDIM * 6,
            bytes_accessed=4 * SPAN * (near * count + 2) * span + 4 * SPAN * near * count * inner,
            transcendentals=OWN_HEADS * count * near * inner * 9 * cell,
        ),
    )(meta, query, *parts, valid)


def collect_body(member, *rest):
    out = rest[-1]
    for flip, piece in enumerate(rest[:-1]):
        column = pl.multiple_of((member[0] ^ flip) * SPAN, SPAN)
        out[:, pl.ds(column, SPAN)] = piece[...]


def collect(member, pieces):
    rows = pieces[0].shape[0]
    whole = pl.BlockSpec((rows, SPAN), lambda i, m: (0, 0))
    return pl.pallas_call(
        collect_body,
        grid_spec=pltpu.PrefetchScalarGridSpec(
            num_scalar_prefetch=1,
            grid=(1,),
            in_specs=[whole] * MATES,
            out_specs=pl.BlockSpec((rows, HEADS * HDIM), lambda i, m: (0, 0)),
        ),
        out_shape=jax.ShapeDtypeStruct((rows, HEADS * HDIM), jnp.bfloat16),
        compiler_params=pltpu.CompilerParams(vmem_limit_bytes=16 * MIB),
    )(member.reshape(1), *pieces)


def gather_lines(share):
    return [share] + [swap(share, "height", d) for d in range(1, lax.axis_size("height"))]


def gather_blocks(lines, spots, places):
    blocks = list(lines)
    for e in range(1, lax.axis_size("rest")):
        blocks += [swap(line, "rest", e) for line in lines]
    return settle(blocks, spots, places)


def settle(blocks, spots, places):
    depth = blocks[0].shape[0] // MATES
    if depth % 16:
        pieces = jnp.concatenate(blocks, axis=0).reshape(-1, depth, blocks[0].shape[1])
        ordered = jnp.zeros_like(pieces).at[jnp.stack(places)].set(pieces)
        return [ordered.reshape(-1, pieces.shape[2])], (None,)
    return blocks, spots


def per_device(tokens, mod_scale, mod_shift, w_qkv, q_gain, k_gain, window, valid):
    frames, rows, width, features = tokens.shape
    count = frames * rows * width
    inner = rows * width
    model = w_qkv.shape[1] // 3
    rest, pair, core, height = (lax.axis_index(a) for a in ("rest", "pair", "core", "height"))
    member = pair * CORES + core
    high = lax.axis_size("height")
    many = lax.axis_size("rest")
    r_odd = rest % 2

    def columns_of(mate):
        return jnp.concatenate(
            [lax.dynamic_slice_in_dim(w_qkv, s * model + mate * SPAN, SPAN, axis=1) for s in range(3)], axis=1
        )

    shares = [columns_of(member)] + [swap(columns_of(member ^ flip), TEAM, flip) for flip in range(1, MATES)]
    stacked = jnp.concatenate(shares, axis=0)
    kv_share, q_share = stacked[:, SPAN:], stacked[:, :SPAN]
    flat = tokens.reshape(count, features)
    cut = count * 5 // 8 // width * width
    mine, most, last_rows = modulate(flat, mod_scale, mod_shift, cut, width)
    most, kv_share, q_share = lax.optimization_barrier((most, kv_share, q_share))

    meta = jnp.concatenate(
        [
            window.reshape(-1),
            jnp.stack([member, pair, core, height % 2, r_odd, rest, height]).astype(jnp.int32),
        ]
    )
    total_frames = MATES * frames
    valid_pad = jnp.pad(valid, ((TT, TT), (TH, TH), (0, 0)))
    around = lax.dynamic_slice(
        valid_pad,
        (rest * total_frames, height * rows, jnp.int32(0)),
        (total_frames + 2 * TT, rows + 2 * TH, width),
    )
    seen = (around > 0).astype(jnp.bfloat16).reshape(total_frames + 2 * TT, 1, -1)

    spots, places = [], []
    for e in range(many):
        for d in range(high):
            for j in range(MATES):
                spots.append((e, j, d, high))
                places.append(((rest ^ e) * MATES + (member ^ j)) * high + (height ^ d))
    kv_lines = gather_lines(kv_share)
    q_share, kv_lines[-1] = lax.optimization_barrier((q_share, kv_lines[-1]))
    kv_blocks, kv_spots = gather_blocks(kv_lines, tuple(spots), places)

    across = [swap(most, "pair", 1)]
    held = kv_blocks[: 2 * high - 1]
    across[0], meta, seen, last_rows, mates, held = lax.optimization_barrier(
        (across[0], meta, seen, last_rows, mine, held)
    )
    kv_blocks[: 2 * high - 1] = held
    across.append(swap(last_rows, "pair", 1))
    beside = swap(mates, "core", 1)
    nearest = swap(q_share, "height", 1)
    q_share, nearest = lax.optimization_barrier((q_share, nearest))
    q_lines = [q_share, nearest] + [swap(q_share, "height", d) for d in range(2, high)]
    q_lines[0], beside = lax.optimization_barrier((q_lines[0], beside))
    kv_blocks[0], q_lines[1] = lax.optimization_barrier((kv_blocks[0], q_lines[1]))

    q_near = [[swap(line, "rest", e) for line in q_lines[:2]] for e in range(1, many)]

    def cells_of(tokens):
        return project(meta, tokens, frames, kv_blocks, kv_spots, k_gain, 2, 1, True)

    def exchanged(even, odd):
        return (even, odd, swap_neighbours(even, "height", 0), swap_neighbours(odd, "height", 1))

    even, odd = cells_of([[mine], [beside]])
    near_set = exchanged(even, odd)
    _, across, q_near, q_lines[2:] = lax.optimization_barrier((even, across, q_near, q_lines[2:]))
    together = jnp.concatenate(q_lines[2:], axis=0)
    q_far = [swap(together, "rest", e) for e in range(1, many)]
    beyond = [swap(x, "core", 1) for x in across]
    even, odd = cells_of([across, beyond])
    even, odd, q_far = lax.optimization_barrier((even, odd, q_far))
    q_blocks = list(q_lines)
    for first, rest_of in zip(q_near, q_far):
        q_blocks += [*first, *jnp.split(rest_of, high - 2, axis=0)]
    q_blocks, q_spots = settle(q_blocks, tuple(spots), places)
    far_set = exchanged(even, odd)

    def border(side):
        last = r_odd == side
        chosen = jnp.where(last, 1, 0) == pair
        frame = jnp.stack(
            [
                jnp.where(
                    chosen,
                    jnp.where(last, a[:, -1], a[:, 0]),
                    jnp.where(last, b[:, -1], b[:, 0]),
                )
                for a, b in zip(near_set[:2], far_set[:2])
            ]
        )
        frame, *back = lax.optimization_barrier((swap_neighbours(frame, "rest", side), *near_set[2:]))
        return frame, swap_neighbours(frame[0], "height", 0), swap_neighbours(frame[1], "height", 1)

    borders = [border(side) for side in range(min(2, many - 1))]
    q_blocks[0], even = lax.optimization_barrier((q_blocks[0], even))
    far_set = (even, *far_set[1:])
    everyone = [[mine], [beside], across, beyond]
    (query,) = project(meta, everyone, frames, q_blocks, q_spots, q_gain, 1, 1, False)
    query, *far_back = lax.optimization_barrier((query, *far_set[2:]))
    far_set = (*far_set[:2], *far_back)

    parts = (query, near_set, far_set, borders, seen)
    travelled = []
    for flip in range(CORES):
        (out,) = attend(meta, *parts, True, (flip,))
        meta, out = lax.optimization_barrier((meta, out))
        travelled.append(swap(out.reshape(count, SPAN), TEAM, CORES + flip))
    (other,) = attend(meta, *parts, False, (1,))
    meta, other, travelled[0] = lax.optimization_barrier((meta, other, travelled[0]))
    (own,) = attend(meta, *parts, False, (0,))
    pieces = [own.reshape(count, SPAN), swap(other.reshape(count, SPAN), TEAM, 1), *travelled]
    return collect(member.astype(jnp.int32), pieces).reshape(frames, rows, width, model)


def solution(mesh):
    split = Mesh(
        mesh.devices.reshape(mesh.shape["tm"] // MATES, MATES // CORES, CORES, mesh.shape["height"]),
        ("rest", "pair", "core", "height"),
    )
    along = ("rest", "pair", "core")
    in_specs = (
        P(along, "height", None, None),
        P(),
        P(),
        P((*along, "height"), None),
        P(),
        P(),
        P(),
        P(),
    )
    out_specs = P(along, "height", None, None)
    return jax.shard_map(
        per_device, mesh=split, in_specs=in_specs, out_specs=out_specs, check_vma=False
    )
```

```python
import functools

import jax
import jax.numpy as jnp
import numpy as np
from jax import lax
from jax.experimental import pallas as pl
from jax.experimental.pallas import tpu as pltpu
from jax.sharding import Mesh
from jax.sharding import PartitionSpec as P

HDIM = 128
HEADS = 12
TT = 1
TH = 2
TW = 8
CORES = 2
MATES = 4
OWN_HEADS = HEADS // MATES
SPAN = OWN_HEADS * HDIM
EPS = 1e-06
MIB = 1024 * 1024
TEAM = ("pair", "core")

MEMBER, PAIR, CORE, Z_ODD, R_ODD, REST, HEIGHT = (3 * HEADS + i for i in range(7))


def swap(x, axis, flip):
    names = axis if isinstance(axis, tuple) else (axis,)
    count = int(np.prod([lax.axis_size(name) for name in names]))
    return lax.ppermute(x, axis, [(i, i ^ flip) for i in range(count)])


def swap_neighbours(x, axis, odd):
    count = lax.axis_size(axis)
    pairs = [(i, i + 1) for i in range(odd, count - 1, 2)]
    flat = x.reshape(-1, x.shape[-1])
    return lax.ppermute(flat, axis, pairs + [(j, i) for i, j in pairs]).reshape(x.shape)


def modulate_body(tokens, scale, shift, whole, first, second, *, steps):
    values = tokens[...].astype(jnp.float32)
    centred = values - jnp.mean(values, axis=-1, keepdims=True)
    variance = jnp.mean(centred * centred, axis=-1, keepdims=True)
    normed = centred * lax.rsqrt(variance + EPS)
    result = (normed * (1.0 + scale[...]) + shift[...]).astype(whole.dtype)
    whole[...] = result
    step = pl.program_id(0)
    pl.when(step < steps)(functools.partial(first.__setitem__, ..., result))
    pl.when(step >= steps)(functools.partial(second.__setitem__, ..., result))


def modulate(tokens, scale, shift, cut, block):
    count, features = tokens.shape
    steps = cut // block
    row = lambda place: pl.BlockSpec((block, features), lambda i: (place(i), 0))
    whole = pl.BlockSpec((1, features), lambda i: (0, 0))
    rows = lambda length: jax.ShapeDtypeStruct((length, features), jnp.bfloat16)
    return pl.pallas_call(
        functools.partial(modulate_body, steps=steps),
        grid=(count // block,),
        in_specs=[row(lambda i: i), whole, whole],
        out_specs=[
            row(lambda i: i),
            row(lambda i: jnp.minimum(i, steps - 1)),
            row(lambda i: jnp.maximum(i - steps, 0)),
        ],
        out_shape=[rows(count), rows(cut), rows(count - cut)],
        compiler_params=pltpu.CompilerParams(vmem_limit_bytes=12 * MIB),
        cost_estimate=pl.CostEstimate(
            flops=12 * count * features, bytes_accessed=6 * count * features, transcendentals=0
        ),
    )(tokens, scale.reshape(1, features), shift.reshape(1, features))


def project_body(meta, *rest, groups, frames, arrays, depth, spots, normed, halves):
    sources, members = sum(groups), len(groups)
    xs, blocks, gain = rest[:sources], rest[sources : sources + arrays], rest[sources + arrays]
    outs, (rows, weights, row_sems, weight_sems) = rest[sources + arrays + 1 : -4], rest[-4:]
    columns = weights.shape[1]
    count = rows.shape[0] // members
    inner = count // frames
    cell = inner // 2

    loads, first = [], 0
    for i, x in enumerate(xs):
        loads.append(pltpu.make_async_copy(x, rows.at[pl.ds(first, x.shape[0]), :], row_sems.at[i]))
        first += x.shape[0]
    copies = []
    for p, spot in enumerate(spots):
        place = 0
        if spot is not None:
            e, j, d, high = spot
            place = ((meta[REST] ^ e) * MATES + (meta[MEMBER] ^ j)) * high + (meta[HEIGHT] ^ d)
        held = len(spots) // arrays
        source = blocks[p // held].at[pl.ds(p % held * depth, depth), :]
        row = pl.multiple_of(place * depth, depth)
        copies.append(pltpu.make_async_copy(source, weights.at[pl.ds(row, depth), :], weight_sems.at[p]))
    for load in loads[: groups[0]]:
        load.start()
    for copy in copies:
        copy.start()
    for load in loads[groups[0] :]:
        load.start()
    for copy in copies:
        copy.wait()
    wide = 2 * HDIM
    for i in range(members):
        for load in loads[sum(groups[:i]) : sum(groups[: i + 1])]:
            load.wait()
        for start in range(0, columns, wide):
            stop = min(start + wide, columns)
            total = jnp.dot(
                rows[i * count : (i + 1) * count, :], weights[:, start:stop], preferred_element_type=jnp.float32
            )
            for column in range(start, stop, HDIM):
                head = total[:, column - start : column - start + HDIM]
                part, offset = divmod(column, SPAN)
                if part < normed:
                    power = jnp.mean(head * head, axis=-1, keepdims=True)
                    head = head * lax.rsqrt(power + EPS) * gain[...]
                head = head.astype(jnp.bfloat16)
                lanes = slice(offset, offset + HDIM)
                for frame in range(frames):
                    place = (meta[CORE if halves else MEMBER] ^ i) * frames + frame
                    one = head[frame * inner : (frame + 1) * inner]
                    if halves:
                        top, bottom = one[:cell], one[cell:]
                        odd = meta[Z_ODD] == 1
                        outs[0][part, place, :, lanes] = jnp.where(odd, top, bottom)
                        outs[1][part, place, :, lanes] = jnp.where(odd, bottom, top)
                    else:
                        outs[0][part, place, :, lanes] = one


def project(meta, tokens, frames, blocks, spots, gain, parts, normed, halves):
    members = len(tokens)
    groups = tuple(len(pieces) for pieces in tokens)
    sources = [x for pieces in tokens for x in pieces]
    features = sources[0].shape[1]
    total = sum(x.shape[0] for x in sources)
    inner = total // members // frames
    columns = blocks[0].shape[1]
    count = len(sources)
    any_space = pl.BlockSpec(memory_space=pl.ANY)
    vmem = pl.BlockSpec(memory_space=pltpu.VMEM)
    outs = 2 if halves else 1
    return pl.pallas_call(
        functools.partial(
            project_body,
            groups=groups,
            frames=frames,
            arrays=len(blocks),
            depth=features // len(spots),
            spots=spots,
            normed=normed,
            halves=halves,
        ),
        grid_spec=pltpu.PrefetchScalarGridSpec(
            num_scalar_prefetch=1,
            grid=(),
            in_specs=[any_space] * (count + len(blocks)) + [vmem],
            out_specs=[vmem] * outs,
            scratch_shapes=[
                pltpu.VMEM((total, features), jnp.bfloat16),
                pltpu.VMEM((features, columns), jnp.bfloat16),
                pltpu.SemaphoreType.DMA((count,)),
                pltpu.SemaphoreType.DMA((len(spots),)),
            ],
        ),
        out_shape=[jax.ShapeDtypeStruct((parts, members * frames, inner // outs, SPAN), jnp.bfloat16)] * outs,
        compiler_params=pltpu.CompilerParams(vmem_limit_bytes=24 * MIB),
        cost_estimate=pl.CostEstimate(
            flops=2 * total * features * columns,
            bytes_accessed=2 * features * columns + 2 * total * (features + columns),
            transcendentals=0,
        ),
    )(meta, *sources, *blocks, gain.reshape(1, HDIM))


def attend_body(meta, *rest, near, far, sides, cell, inner, pieces):
    count = len(pieces)
    query, main = rest[0], rest[1 : -4 - count]
    valid, outs = rest[-4 - count], rest[-3 - count : -3]
    cells, band, result_cells = rest[-3:]
    member, pair, core, z_odd, r_odd = (meta[i] for i in (MEMBER, PAIR, CORE, Z_ODD, R_ODD))
    chip = 1 - pair if far else pair
    width = cell // TH
    frames = cells.shape[0] - 2

    row_of = [jnp.where(z_odd == 1, a, b) * cell for a, b in ((1, 2), (2, 1), (0, 3), (3, 0))]
    own_set, other_set, borders = main[0:4], main[4:8], main[8:]
    own_frame = lambda i: tuple(part[:, i] for part in own_set)
    other_frame = lambda i: tuple(part[:, i] for part in other_set)

    def load(slot, found):
        for part, row in zip(found(), row_of):
            rows = pl.ds(pl.multiple_of(row, cell), cell)
            cells[slot, :, rows, :] = part

    def border(side):
        frame, even, odd = borders[3 * side : 3 * side + 3]
        return frame[0], frame[1], even[...], odd[...]

    low = jnp.bool_(True) if count > 1 else (core ^ pieces[0]) == 0
    high = jnp.bool_(True) if count > 1 else (core ^ pieces[0]) == 1
    for end, slot, used in ((0, 0, low), (1, frames + 1, high)):
        found = functools.partial(other_frame, 0 if end else frames - 1)
        pl.when(used & (chip != end))(functools.partial(load, slot, found))
        for side in range(sides):
            pl.when(used & (chip == end) & ((r_odd == 1) == (end == side)))(
                functools.partial(load, slot, functools.partial(border, side))
            )

        if sides < 2:

            @pl.when(used & (chip == end) & ((r_odd == 1) == (end == 1)))
            def _():
                cells[slot] = jnp.zeros(cells.shape[1:], cells.dtype)

    for index in range(frames):
        slot = index + 1
        found = functools.partial(own_frame, index)
        if near <= slot <= near + 1:
            load(slot, found)
        else:
            pl.when(low if slot < near else high)(functools.partial(load, slot, found))
    q_tile = lax.broadcasted_iota(jnp.int32, (cell, 3 * cell), 0)
    k_tile = lax.broadcasted_iota(jnp.int32, (cell, 3 * cell), 1)
    apart = jnp.abs(lax.rem(q_tile, width) // TW - lax.rem(k_tile, width) // TW)
    for reach in range(3):
        band[reach] = jnp.where(apart <= reach, 1.0, 0.0).astype(band.dtype)

    def serve(step, carry):
        slot = (core ^ pieces[0] ^ (step // near)) * near + step % near
        attend_frame(
            meta, query, valid, outs, cells, band, result_cells, step, slot, chip * frames + slot, near, cell, inner
        )
        return carry

    lax.fori_loop(0, near * count, serve, 0)


def attend_frame(
    meta, query, valid, outs, cells, band, result_cells, step, slot, first, near, cell, inner
):
    member = meta[MEMBER]
    scale = np.float32(np.log2(np.e) / np.sqrt(HDIM))
    mine_valid = valid[first + 1, :, cell : cell + inner].astype(jnp.float32)
    real = jnp.transpose(jnp.broadcast_to(mine_valid, (HDIM, inner)))

    def attend(out, head, over_t, over_h):
        lanes = slice(head * HDIM, (head + 1) * HDIM)
        seen = (3 if over_h else 1) * cell
        mask = band[meta[3 * (member * OWN_HEADS + head) + 2], :, :seen]
        ones = jnp.ones((seen, HDIM), jnp.bfloat16)
        for tile in range(inner // cell):
            rows = pl.ds((tile + (0 if over_h else 1)) * cell, seen)
            mine = query[0, first, pl.ds(tile * cell, cell), lanes]
            total = None
            for near_step in (0, 1, 2) if over_t else (1,):
                scores = lax.dot_general(
                    mine,
                    cells[slot + near_step, 0, rows, lanes],
                    (((1,), (1,)), ((), ())),
                    preferred_element_type=jnp.float32,
                )
                start = (tile + (0 if over_h else 1)) * cell
                allowed = mask * valid[first + near_step, :, start : start + seen]
                terms = jnp.exp2(scores * scale).astype(jnp.bfloat16) * allowed
                both = jnp.concatenate([cells[slot + near_step, 1, rows, lanes], ones], axis=1)
                part = jnp.dot(terms, both, preferred_element_type=jnp.float32)
                total = part if total is None else total + part
            here = real[tile * cell : (tile + 1) * cell] > 0
            weight = jnp.where(here, total[:, HDIM:], 1.0)
            result = jnp.where(here, total[:, :HDIM] / weight, 0.0)
            out[0, pl.ds(tile * cell, cell), lanes] = result.astype(out.dtype)

    for head in range(OWN_HEADS):
        reach_t, reach_h = (meta[3 * (member * OWN_HEADS + head) + i] for i in range(2))
        for over_t in (False, True):
            for over_h in (False, True):
                pl.when(((reach_t > 0) == over_t) & ((reach_h > 0) == over_h))(
                    functools.partial(attend, result_cells, head, over_t, over_h)
                )

    for index, out in enumerate(outs):
        pl.when(step // near == index)(functools.partial(out.__setitem__, step % near, result_cells[0]))


def attend(meta, query, near_set, far_set, borders, valid, far, pieces):
    _, chip_frames, cell, _ = near_set[0].shape
    inner = 2 * cell
    span = 4 * cell
    near = chip_frames // CORES
    sets = (*far_set, *near_set) if far else (*near_set, *far_set)
    parts = [*sets, *(p for pair in borders for p in pair)]
    count = len(pieces)
    vmem = pl.BlockSpec(memory_space=pltpu.VMEM)
    piece = jax.ShapeDtypeStruct((near, inner, SPAN), jnp.bfloat16)
    return pl.pallas_call(
        functools.partial(
            attend_body, near=near, far=far, sides=len(borders), cell=cell, inner=inner, pieces=pieces
        ),
        grid_spec=pltpu.PrefetchScalarGridSpec(
            num_scalar_prefetch=1,
            grid=(),
            in_specs=[vmem] * (len(parts) + 2),
            out_specs=[vmem] * count,
            scratch_shapes=[
                pltpu.VMEM((chip_frames + 2, 2, span, SPAN), jnp.bfloat16),
                pltpu.VMEM((3, cell, 3 * cell), jnp.bfloat16),
                pltpu.VMEM((1, inner, SPAN), jnp.bfloat16),
            ],
        ),
        out_shape=[piece] * count,
        compiler_params=pltpu.CompilerParams(vmem_limit_bytes=24 * MIB),
        cost_estimate=pl.CostEstimate(
            flops=OWN_HEADS * count * near * inner * 9 * cell * HDIM * 6,
            bytes_accessed=4 * SPAN * (near * count + 2) * span + 4 * SPAN * near * count * inner,
            transcendentals=OWN_HEADS * count * near * inner * 9 * cell,
        ),
    )(meta, query, *parts, valid)


def collect_body(member, *rest):
    out = rest[-1]
    for flip, piece in enumerate(rest[:-1]):
        column = pl.multiple_of((member[0] ^ flip) * SPAN, SPAN)
        out[:, pl.ds(column, SPAN)] = piece[...]


def collect(member, pieces):
    rows = pieces[0].shape[0]
    whole = pl.BlockSpec((rows, SPAN), lambda i, m: (0, 0))
    return pl.pallas_call(
        collect_body,
        grid_spec=pltpu.PrefetchScalarGridSpec(
            num_scalar_prefetch=1,
            grid=(1,),
            in_specs=[whole] * MATES,
            out_specs=pl.BlockSpec((rows, HEADS * HDIM), lambda i, m: (0, 0)),
        ),
        out_shape=jax.ShapeDtypeStruct((rows, HEADS * HDIM), jnp.bfloat16),
        compiler_params=pltpu.CompilerParams(vmem_limit_bytes=16 * MIB),
    )(member.reshape(1), *pieces)


def gather_lines(share):
    return [share] + [swap(share, "height", d) for d in range(1, lax.axis_size("height"))]


def gather_blocks(lines, spots, places):
    blocks = list(lines)
    for e in range(1, lax.axis_size("rest")):
        blocks += [swap(line, "rest", e) for line in lines]
    return settle(blocks, spots, places)


def settle(blocks, spots, places):
    depth = blocks[0].shape[0] // MATES
    if depth % 16:
        pieces = jnp.concatenate(blocks, axis=0).reshape(-1, depth, blocks[0].shape[1])
        ordered = jnp.zeros_like(pieces).at[jnp.stack(places)].set(pieces)
        return [ordered.reshape(-1, pieces.shape[2])], (None,)
    return blocks, spots


def per_device(tokens, mod_scale, mod_shift, w_qkv, q_gain, k_gain, window, valid):
    frames, rows, width, features = tokens.shape
    count = frames * rows * width
    inner = rows * width
    model = w_qkv.shape[1] // 3
    rest, pair, core, height = (lax.axis_index(a) for a in ("rest", "pair", "core", "height"))
    member = pair * CORES + core
    high = lax.axis_size("height")
    many = lax.axis_size("rest")
    r_odd = rest % 2

    def columns_of(mate):
        return jnp.concatenate(
            [lax.dynamic_slice_in_dim(w_qkv, s * model + mate * SPAN, SPAN, axis=1) for s in range(3)], axis=1
        )

    shares = [columns_of(member)] + [swap(columns_of(member ^ flip), TEAM, flip) for flip in range(1, MATES)]
    stacked = jnp.concatenate(shares, axis=0)
    kv_share, q_share = stacked[:, SPAN:], stacked[:, :SPAN]
    flat = tokens.reshape(count, features)
    cut = count * 5 // 8 // width * width
    mine, most, last_rows = modulate(flat, mod_scale, mod_shift, cut, width)
    most, kv_share, q_share = lax.optimization_barrier((most, kv_share, q_share))

    meta = jnp.concatenate(
        [
            window.reshape(-1),
            jnp.stack([member, pair, core, height % 2, r_odd, rest, height]).astype(jnp.int32),
        ]
    )
    total_frames = MATES * frames
    valid_pad = jnp.pad(valid, ((TT, TT), (TH, TH), (0, 0)))
    around = lax.dynamic_slice(
        valid_pad,
        (rest * total_frames, height * rows, jnp.int32(0)),
        (total_frames + 2 * TT, rows + 2 * TH, width),
    )
    seen = (around > 0).astype(jnp.bfloat16).reshape(total_frames + 2 * TT, 1, -1)

    spots, places = [], []
    for e in range(many):
        for d in range(high):
            for j in range(MATES):
                spots.append((e, j, d, high))
                places.append(((rest ^ e) * MATES + (member ^ j)) * high + (height ^ d))
    kv_lines = gather_lines(kv_share)
    q_share, kv_lines[-1] = lax.optimization_barrier((q_share, kv_lines[-1]))
    kv_blocks, kv_spots = gather_blocks(kv_lines, tuple(spots), places)

    across = [swap(most, "pair", 1)]
    held = kv_blocks[: 2 * high - 1]
    across[0], meta, seen, last_rows, mates, held = lax.optimization_barrier(
        (across[0], meta, seen, last_rows, mine, held)
    )
    kv_blocks[: 2 * high - 1] = held
    across.append(swap(last_rows, "pair", 1))
    beside = swap(mates, "core", 1)
    nearest = swap(q_share, "height", 1)
    q_share, nearest = lax.optimization_barrier((q_share, nearest))
    q_lines = [q_share, nearest] + [swap(q_share, "height", d) for d in range(2, high)]
    q_lines[0], beside = lax.optimization_barrier((q_lines[0], beside))
    kv_blocks[0], q_lines[1] = lax.optimization_barrier((kv_blocks[0], q_lines[1]))

    q_near = [[swap(line, "rest", e) for line in q_lines[:2]] for e in range(1, many)]

    def cells_of(tokens):
        return project(meta, tokens, frames, kv_blocks, kv_spots, k_gain, 2, 1, True)

    def exchanged(even, odd):
        return (even, odd, swap_neighbours(even, "height", 0), swap_neighbours(odd, "height", 1))

    even, odd = cells_of([[mine], [beside]])
    near_set = exchanged(even, odd)
    _, across, q_near, q_lines[2:] = lax.optimization_barrier((even, across, q_near, q_lines[2:]))
    together = jnp.concatenate(q_lines[2:], axis=0)
    q_far = [swap(together, "rest", e) for e in range(1, many)]
    beyond = [swap(x, "core", 1) for x in across]
    even, odd = cells_of([across, beyond])
    even, odd, q_far = lax.optimization_barrier((even, odd, q_far))
    q_blocks = list(q_lines)
    for first, rest_of in zip(q_near, q_far):
        q_blocks += [*first, *jnp.split(rest_of, high - 2, axis=0)]
    q_blocks, q_spots = settle(q_blocks, tuple(spots), places)
    far_set = exchanged(even, odd)

    q_blocks[0], even = lax.optimization_barrier((q_blocks[0], even))
    far_set = (even, *far_set[1:])
    everyone = [[mine], [beside], across, beyond]
    (query,) = project(meta, everyone, frames, q_blocks, q_spots, q_gain, 1, 1, False)

    def border(side):
        last = r_odd == side
        chosen = jnp.where(last, 1, 0) == pair
        frame = jnp.stack(
            [
                jnp.where(
                    chosen,
                    jnp.where(last, a[:, -1], a[:, 0]),
                    jnp.where(last, b[:, -1], b[:, 0]),
                )
                for a, b in zip(near_set[:2], far_set[:2])
            ]
        )
        frame, *_ = lax.optimization_barrier((swap_neighbours(frame, "rest", side), query, *near_set[2:]))
        return frame, swap_neighbours(frame[0], "height", 0), swap_neighbours(frame[1], "height", 1)

    borders = [border(side) for side in range(min(2, many - 1))]
    query, *far_back = lax.optimization_barrier((query, *far_set[2:]))
    far_set = (*far_set[:2], *far_back)

    parts = (query, near_set, far_set, borders, seen)
    travelled = []
    for flip in range(CORES):
        (out,) = attend(meta, *parts, True, (flip,))
        meta, out = lax.optimization_barrier((meta, out))
        travelled.append(swap(out.reshape(count, SPAN), TEAM, CORES + flip))
    (other,) = attend(meta, *parts, False, (1,))
    meta, other, travelled[0] = lax.optimization_barrier((meta, other, travelled[0]))
    (own,) = attend(meta, *parts, False, (0,))
    pieces = [own.reshape(count, SPAN), swap(other.reshape(count, SPAN), TEAM, 1), *travelled]
    return collect(member.astype(jnp.int32), pieces).reshape(frames, rows, width, model)


def solution(mesh):
    split = Mesh(
        mesh.devices.reshape(mesh.shape["tm"] // MATES, MATES // CORES, CORES, mesh.shape["height"]),
        ("rest", "pair", "core", "height"),
    )
    along = ("rest", "pair", "core")
    in_specs = (
        P(along, "height", None, None),
        P(),
        P(),
        P((*along, "height"), None),
        P(),
        P(),
        P(),
        P(),
    )
    out_specs = P(along, "height", None, None)
    return jax.shard_map(
        per_device, mesh=split, in_specs=in_specs, out_specs=out_specs, check_vma=False
    )
```

```python
import functools

import jax
import jax.numpy as jnp
import numpy as np
from jax import lax
from jax.experimental import pallas as pl
from jax.experimental.pallas import tpu as pltpu
from jax.sharding import Mesh
from jax.sharding import PartitionSpec as P

HDIM = 128
HEADS = 12
TT = 1
TH = 2
TW = 8
CORES = 2
MATES = 4
OWN_HEADS = HEADS // MATES
SPAN = OWN_HEADS * HDIM
EPS = 1e-06
MIB = 1024 * 1024
TEAM = ("pair", "core")

MEMBER, PAIR, CORE, Z_ODD, R_ODD, REST, HEIGHT = (3 * HEADS + i for i in range(7))


def swap(x, axis, flip):
    names = axis if isinstance(axis, tuple) else (axis,)
    count = int(np.prod([lax.axis_size(name) for name in names]))
    return lax.ppermute(x, axis, [(i, i ^ flip) for i in range(count)])


def swap_neighbours(x, axis, odd):
    count = lax.axis_size(axis)
    pairs = [(i, i + 1) for i in range(odd, count - 1, 2)]
    flat = x.reshape(-1, x.shape[-1])
    return lax.ppermute(flat, axis, pairs + [(j, i) for i, j in pairs]).reshape(x.shape)


def modulate_body(tokens, scale, shift, whole, first, second, *, steps):
    values = tokens[...].astype(jnp.float32)
    centred = values - jnp.mean(values, axis=-1, keepdims=True)
    variance = jnp.mean(centred * centred, axis=-1, keepdims=True)
    normed = centred * lax.rsqrt(variance + EPS)
    result = (normed * (1.0 + scale[...]) + shift[...]).astype(whole.dtype)
    whole[...] = result
    step = pl.program_id(0)
    pl.when(step < steps)(functools.partial(first.__setitem__, ..., result))
    pl.when(step >= steps)(functools.partial(second.__setitem__, ..., result))


def modulate(tokens, scale, shift, cut, block):
    count, features = tokens.shape
    steps = cut // block
    row = lambda place: pl.BlockSpec((block, features), lambda i: (place(i), 0))
    whole = pl.BlockSpec((1, features), lambda i: (0, 0))
    rows = lambda length: jax.ShapeDtypeStruct((length, features), jnp.bfloat16)
    return pl.pallas_call(
        functools.partial(modulate_body, steps=steps),
        grid=(count // block,),
        in_specs=[row(lambda i: i), whole, whole],
        out_specs=[
            row(lambda i: i),
            row(lambda i: jnp.minimum(i, steps - 1)),
            row(lambda i: jnp.maximum(i - steps, 0)),
        ],
        out_shape=[rows(count), rows(cut), rows(count - cut)],
        compiler_params=pltpu.CompilerParams(vmem_limit_bytes=12 * MIB),
        cost_estimate=pl.CostEstimate(
            flops=12 * count * features, bytes_accessed=6 * count * features, transcendentals=0
        ),
    )(tokens, scale.reshape(1, features), shift.reshape(1, features))


def project_body(meta, *rest, groups, frames, arrays, depth, spots, normed, halves):
    sources, members = sum(groups), len(groups)
    xs, blocks, gain = rest[:sources], rest[sources : sources + arrays], rest[sources + arrays]
    outs, (rows, weights, row_sems, weight_sems) = rest[sources + arrays + 1 : -4], rest[-4:]
    columns = weights.shape[1]
    count = rows.shape[0] // members
    inner = count // frames
    cell = inner // 2

    loads, first = [], 0
    for i, x in enumerate(xs):
        loads.append(pltpu.make_async_copy(x, rows.at[pl.ds(first, x.shape[0]), :], row_sems.at[i]))
        first += x.shape[0]
    copies = []
    for p, spot in enumerate(spots):
        place = 0
        if spot is not None:
            e, j, d, high = spot
            place = ((meta[REST] ^ e) * MATES + (meta[MEMBER] ^ j)) * high + (meta[HEIGHT] ^ d)
        held = len(spots) // arrays
        source = blocks[p // held].at[pl.ds(p % held * depth, depth), :]
        row = pl.multiple_of(place * depth, depth)
        copies.append(pltpu.make_async_copy(source, weights.at[pl.ds(row, depth), :], weight_sems.at[p]))
    for load in loads[: groups[0]]:
        load.start()
    for copy in copies:
        copy.start()
    for load in loads[groups[0] :]:
        load.start()
    for copy in copies:
        copy.wait()
    wide = SPAN if columns == SPAN else 2 * HDIM
    for i in range(members):
        for load in loads[sum(groups[:i]) : sum(groups[: i + 1])]:
            load.wait()
        for start in range(0, columns, wide):
            stop = min(start + wide, columns)
            total = jnp.dot(
                rows[i * count : (i + 1) * count, :], weights[:, start:stop], preferred_element_type=jnp.float32
            )
            for column in range(start, stop, HDIM):
                head = total[:, column - start : column - start + HDIM]
                part, offset = divmod(column, SPAN)
                if part < normed:
                    power = jnp.mean(head * head, axis=-1, keepdims=True)
                    head = head * lax.rsqrt(power + EPS) * gain[...]
                head = head.astype(jnp.bfloat16)
                lanes = slice(offset, offset + HDIM)
                for frame in range(frames):
                    place = (meta[CORE if halves else MEMBER] ^ i) * frames + frame
                    one = head[frame * inner : (frame + 1) * inner]
                    if halves:
                        top, bottom = one[:cell], one[cell:]
                        odd = meta[Z_ODD] == 1
                        outs[0][part, place, :, lanes] = jnp.where(odd, top, bottom)
                        outs[1][part, place, :, lanes] = jnp.where(odd, bottom, top)
                    else:
                        outs[0][part, place, :, lanes] = one


def project(meta, tokens, frames, blocks, spots, gain, parts, normed, halves):
    members = len(tokens)
    groups = tuple(len(pieces) for pieces in tokens)
    sources = [x for pieces in tokens for x in pieces]
    features = sources[0].shape[1]
    total = sum(x.shape[0] for x in sources)
    inner = total // members // frames
    columns = blocks[0].shape[1]
    count = len(sources)
    any_space = pl.BlockSpec(memory_space=pl.ANY)
    vmem = pl.BlockSpec(memory_space=pltpu.VMEM)
    outs = 2 if halves else 1
    return pl.pallas_call(
        functools.partial(
            project_body,
            groups=groups,
            frames=frames,
            arrays=len(blocks),
            depth=features // len(spots),
            spots=spots,
            normed=normed,
            halves=halves,
        ),
        grid_spec=pltpu.PrefetchScalarGridSpec(
            num_scalar_prefetch=1,
            grid=(),
            in_specs=[any_space] * (count + len(blocks)) + [vmem],
            out_specs=[vmem] * outs,
            scratch_shapes=[
                pltpu.VMEM((total, features), jnp.bfloat16),
                pltpu.VMEM((features, columns), jnp.bfloat16),
                pltpu.SemaphoreType.DMA((count,)),
                pltpu.SemaphoreType.DMA((len(spots),)),
            ],
        ),
        out_shape=[jax.ShapeDtypeStruct((parts, members * frames, inner // outs, SPAN), jnp.bfloat16)] * outs,
        compiler_params=pltpu.CompilerParams(vmem_limit_bytes=24 * MIB),
        cost_estimate=pl.CostEstimate(
            flops=2 * total * features * columns,
            bytes_accessed=2 * features * columns + 2 * total * (features + columns),
            transcendentals=0,
        ),
    )(meta, *sources, *blocks, gain.reshape(1, HDIM))


def attend_body(meta, *rest, near, far, sides, cell, inner, pieces):
    count = len(pieces)
    query, main = rest[0], rest[1 : -4 - count]
    valid, outs = rest[-4 - count], rest[-3 - count : -3]
    cells, band, result_cells = rest[-3:]
    member, pair, core, z_odd, r_odd = (meta[i] for i in (MEMBER, PAIR, CORE, Z_ODD, R_ODD))
    chip = 1 - pair if far else pair
    width = cell // TH
    frames = cells.shape[0] - 2

    row_of = [jnp.where(z_odd == 1, a, b) * cell for a, b in ((1, 2), (2, 1), (0, 3), (3, 0))]
    own_set, other_set, borders = main[0:4], main[4:8], main[8:]
    own_frame = lambda i: tuple(part[:, i] for part in own_set)
    other_frame = lambda i: tuple(part[:, i] for part in other_set)

    def load(slot, found):
        for part, row in zip(found(), row_of):
            rows = pl.ds(pl.multiple_of(row, cell), cell)
            cells[slot, :, rows, :] = part

    def border(side):
        frame, even, odd = borders[3 * side : 3 * side + 3]
        return frame[0], frame[1], even[...], odd[...]

    low = jnp.bool_(True) if count > 1 else (core ^ pieces[0]) == 0
    high = jnp.bool_(True) if count > 1 else (core ^ pieces[0]) == 1
    for end, slot, used in ((0, 0, low), (1, frames + 1, high)):
        found = functools.partial(other_frame, 0 if end else frames - 1)
        pl.when(used & (chip != end))(functools.partial(load, slot, found))
        for side in range(sides):
            pl.when(used & (chip == end) & ((r_odd == 1) == (end == side)))(
                functools.partial(load, slot, functools.partial(border, side))
            )

        if sides < 2:

            @pl.when(used & (chip == end) & ((r_odd == 1) == (end == 1)))
            def _():
                cells[slot] = jnp.zeros(cells.shape[1:], cells.dtype)

    for index in range(frames):
        slot = index + 1
        found = functools.partial(own_frame, index)
        if near <= slot <= near + 1:
            load(slot, found)
        else:
            pl.when(low if slot < near else high)(functools.partial(load, slot, found))
    q_tile = lax.broadcasted_iota(jnp.int32, (cell, 3 * cell), 0)
    k_tile = lax.broadcasted_iota(jnp.int32, (cell, 3 * cell), 1)
    apart = jnp.abs(lax.rem(q_tile, width) // TW - lax.rem(k_tile, width) // TW)
    for reach in range(3):
        band[reach] = jnp.where(apart <= reach, 1.0, 0.0).astype(band.dtype)

    def serve(step, carry):
        slot = (core ^ pieces[0] ^ (step // near)) * near + step % near
        attend_frame(
            meta, query, valid, outs, cells, band, result_cells, step, slot, chip * frames + slot, near, cell, inner
        )
        return carry

    lax.fori_loop(0, near * count, serve, 0)


def attend_frame(
    meta, query, valid, outs, cells, band, result_cells, step, slot, first, near, cell, inner
):
    member = meta[MEMBER]
    scale = np.float32(np.log2(np.e) / np.sqrt(HDIM))
    mine_valid = valid[first + 1, :, cell : cell + inner].astype(jnp.float32)
    real = jnp.transpose(jnp.broadcast_to(mine_valid, (HDIM, inner)))

    def attend(out, head, over_t, over_h):
        lanes = slice(head * HDIM, (head + 1) * HDIM)
        seen = (3 if over_h else 1) * cell
        mask = band[meta[3 * (member * OWN_HEADS + head) + 2], :, :seen]
        ones = jnp.ones((seen, HDIM), jnp.bfloat16)
        for tile in range(inner // cell):
            rows = pl.ds((tile + (0 if over_h else 1)) * cell, seen)
            mine = query[0, first, pl.ds(tile * cell, cell), lanes]
            total = None
            for near_step in (0, 1, 2) if over_t else (1,):
                scores = lax.dot_general(
                    mine,
                    cells[slot + near_step, 0, rows, lanes],
                    (((1,), (1,)), ((), ())),
                    preferred_element_type=jnp.float32,
                )
                start = (tile + (0 if over_h else 1)) * cell
                allowed = mask * valid[first + near_step, :, start : start + seen]
                terms = jnp.exp2(scores * scale).astype(jnp.bfloat16) * allowed
                both = jnp.concatenate([cells[slot + near_step, 1, rows, lanes], ones], axis=1)
                part = jnp.dot(terms, both, preferred_element_type=jnp.float32)
                total = part if total is None else total + part
            here = real[tile * cell : (tile + 1) * cell] > 0
            weight = jnp.where(here, total[:, HDIM:], 1.0)
            result = jnp.where(here, total[:, :HDIM] / weight, 0.0)
            out[0, pl.ds(tile * cell, cell), lanes] = result.astype(out.dtype)

    for head in range(OWN_HEADS):
        reach_t, reach_h = (meta[3 * (member * OWN_HEADS + head) + i] for i in range(2))
        for over_t in (False, True):
            for over_h in (False, True):
                pl.when(((reach_t > 0) == over_t) & ((reach_h > 0) == over_h))(
                    functools.partial(attend, result_cells, head, over_t, over_h)
                )

    for index, out in enumerate(outs):
        pl.when(step // near == index)(functools.partial(out.__setitem__, step % near, result_cells[0]))


def attend(meta, query, near_set, far_set, borders, valid, far, pieces):
    _, chip_frames, cell, _ = near_set[0].shape
    inner = 2 * cell
    span = 4 * cell
    near = chip_frames // CORES
    sets = (*far_set, *near_set) if far else (*near_set, *far_set)
    parts = [*sets, *(p for pair in borders for p in pair)]
    count = len(pieces)
    vmem = pl.BlockSpec(memory_space=pltpu.VMEM)
    piece = jax.ShapeDtypeStruct((near, inner, SPAN), jnp.bfloat16)
    return pl.pallas_call(
        functools.partial(
            attend_body, near=near, far=far, sides=len(borders), cell=cell, inner=inner, pieces=pieces
        ),
        grid_spec=pltpu.PrefetchScalarGridSpec(
            num_scalar_prefetch=1,
            grid=(),
            in_specs=[vmem] * (len(parts) + 2),
            out_specs=[vmem] * count,
            scratch_shapes=[
                pltpu.VMEM((chip_frames + 2, 2, span, SPAN), jnp.bfloat16),
                pltpu.VMEM((3, cell, 3 * cell), jnp.bfloat16),
                pltpu.VMEM((1, inner, SPAN), jnp.bfloat16),
            ],
        ),
        out_shape=[piece] * count,
        compiler_params=pltpu.CompilerParams(vmem_limit_bytes=24 * MIB),
        cost_estimate=pl.CostEstimate(
            flops=OWN_HEADS * count * near * inner * 9 * cell * HDIM * 6,
            bytes_accessed=4 * SPAN * (near * count + 2) * span + 4 * SPAN * near * count * inner,
            transcendentals=OWN_HEADS * count * near * inner * 9 * cell,
        ),
    )(meta, query, *parts, valid)


def collect_body(member, *rest):
    out = rest[-1]
    for flip, piece in enumerate(rest[:-1]):
        column = pl.multiple_of((member[0] ^ flip) * SPAN, SPAN)
        out[:, pl.ds(column, SPAN)] = piece[...]


def collect(member, pieces):
    rows = pieces[0].shape[0]
    whole = pl.BlockSpec((rows, SPAN), lambda i, m: (0, 0))
    return pl.pallas_call(
        collect_body,
        grid_spec=pltpu.PrefetchScalarGridSpec(
            num_scalar_prefetch=1,
            grid=(1,),
            in_specs=[whole] * MATES,
            out_specs=pl.BlockSpec((rows, HEADS * HDIM), lambda i, m: (0, 0)),
        ),
        out_shape=jax.ShapeDtypeStruct((rows, HEADS * HDIM), jnp.bfloat16),
        compiler_params=pltpu.CompilerParams(vmem_limit_bytes=16 * MIB),
    )(member.reshape(1), *pieces)


def gather_lines(share):
    return [share] + [swap(share, "height", d) for d in range(1, lax.axis_size("height"))]


def gather_blocks(lines, spots, places):
    blocks = list(lines)
    for e in range(1, lax.axis_size("rest")):
        blocks += [swap(line, "rest", e) for line in lines]
    return settle(blocks, spots, places)


def settle(blocks, spots, places):
    depth = blocks[0].shape[0] // MATES
    if depth % 16:
        pieces = jnp.concatenate(blocks, axis=0).reshape(-1, depth, blocks[0].shape[1])
        ordered = jnp.zeros_like(pieces).at[jnp.stack(places)].set(pieces)
        return [ordered.reshape(-1, pieces.shape[2])], (None,)
    return blocks, spots


def per_device(tokens, mod_scale, mod_shift, w_qkv, q_gain, k_gain, window, valid):
    frames, rows, width, features = tokens.shape
    count = frames * rows * width
    inner = rows * width
    model = w_qkv.shape[1] // 3
    rest, pair, core, height = (lax.axis_index(a) for a in ("rest", "pair", "core", "height"))
    member = pair * CORES + core
    high = lax.axis_size("height")
    many = lax.axis_size("rest")
    r_odd = rest % 2

    def columns_of(mate):
        return jnp.concatenate(
            [lax.dynamic_slice_in_dim(w_qkv, s * model + mate * SPAN, SPAN, axis=1) for s in range(3)], axis=1
        )

    shares = [columns_of(member)] + [swap(columns_of(member ^ flip), TEAM, flip) for flip in range(1, MATES)]
    stacked = jnp.concatenate(shares, axis=0)
    kv_share, q_share = stacked[:, SPAN:], stacked[:, :SPAN]
    flat = tokens.reshape(count, features)
    cut = count * 5 // 8 // width * width
    mine, most, last_rows = modulate(flat, mod_scale, mod_shift, cut, width)
    most, kv_share, q_share = lax.optimization_barrier((most, kv_share, q_share))

    meta = jnp.concatenate(
        [
            window.reshape(-1),
            jnp.stack([member, pair, core, height % 2, r_odd, rest, height]).astype(jnp.int32),
        ]
    )
    total_frames = MATES * frames
    valid_pad = jnp.pad(valid, ((TT, TT), (TH, TH), (0, 0)))
    around = lax.dynamic_slice(
        valid_pad,
        (rest * total_frames, height * rows, jnp.int32(0)),
        (total_frames + 2 * TT, rows + 2 * TH, width),
    )
    seen = (around > 0).astype(jnp.bfloat16).reshape(total_frames + 2 * TT, 1, -1)

    spots, places = [], []
    for e in range(many):
        for d in range(high):
            for j in range(MATES):
                spots.append((e, j, d, high))
                places.append(((rest ^ e) * MATES + (member ^ j)) * high + (height ^ d))
    kv_lines = gather_lines(kv_share)
    q_share, kv_lines[-1] = lax.optimization_barrier((q_share, kv_lines[-1]))
    kv_blocks, kv_spots = gather_blocks(kv_lines, tuple(spots), places)

    across = [swap(most, "pair", 1)]
    held = kv_blocks[: 2 * high - 1]
    across[0], meta, seen, last_rows, mates, held = lax.optimization_barrier(
        (across[0], meta, seen, last_rows, mine, held)
    )
    kv_blocks[: 2 * high - 1] = held
    across.append(swap(last_rows, "pair", 1))
    beside = swap(mates, "core", 1)
    nearest = swap(q_share, "height", 1)
    q_share, nearest = lax.optimization_barrier((q_share, nearest))
    q_lines = [q_share, nearest] + [swap(q_share, "height", d) for d in range(2, high)]
    q_lines[0], beside = lax.optimization_barrier((q_lines[0], beside))
    kv_blocks[0], q_lines[1] = lax.optimization_barrier((kv_blocks[0], q_lines[1]))

    q_near = [[swap(line, "rest", e) for line in q_lines[:2]] for e in range(1, many)]

    def cells_of(tokens):
        return project(meta, tokens, frames, kv_blocks, kv_spots, k_gain, 2, 1, True)

    def exchanged(even, odd):
        return (even, odd, swap_neighbours(even, "height", 0), swap_neighbours(odd, "height", 1))

    even, odd = cells_of([[mine], [beside]])
    near_set = exchanged(even, odd)
    _, across, q_near, q_lines[2:] = lax.optimization_barrier((even, across, q_near, q_lines[2:]))
    together = jnp.concatenate(q_lines[2:], axis=0)
    q_far = [swap(together, "rest", e) for e in range(1, many)]
    beyond = [swap(x, "core", 1) for x in across]
    even, odd = cells_of([across, beyond])
    even, odd, q_far = lax.optimization_barrier((even, odd, q_far))
    q_blocks = list(q_lines)
    for first, rest_of in zip(q_near, q_far):
        q_blocks += [*first, *jnp.split(rest_of, high - 2, axis=0)]
    q_blocks, q_spots = settle(q_blocks, tuple(spots), places)
    far_set = exchanged(even, odd)

    q_blocks[0], even = lax.optimization_barrier((q_blocks[0], even))
    far_set = (even, *far_set[1:])
    everyone = [[mine], [beside], across, beyond]
    (query,) = project(meta, everyone, frames, q_blocks, q_spots, q_gain, 1, 1, False)

    def border(side):
        last = r_odd == side
        chosen = jnp.where(last, 1, 0) == pair
        frame = jnp.stack(
            [
                jnp.where(
                    chosen,
                    jnp.where(last, a[:, -1], a[:, 0]),
                    jnp.where(last, b[:, -1], b[:, 0]),
                )
                for a, b in zip(near_set[:2], far_set[:2])
            ]
        )
        frame, *_ = lax.optimization_barrier((swap_neighbours(frame, "rest", side), query, *near_set[2:]))
        return frame, swap_neighbours(frame[0], "height", 0), swap_neighbours(frame[1], "height", 1)

    borders = [border(side) for side in range(min(2, many - 1))]
    query, *far_back = lax.optimization_barrier((query, *far_set[2:]))
    far_set = (*far_set[:2], *far_back)

    parts = (query, near_set, far_set, borders, seen)
    travelled = []
    for flip in range(CORES):
        (out,) = attend(meta, *parts, True, (flip,))
        meta, out = lax.optimization_barrier((meta, out))
        travelled.append(swap(out.reshape(count, SPAN), TEAM, CORES + flip))
    (other,) = attend(meta, *parts, False, (1,))
    meta, other, travelled[0] = lax.optimization_barrier((meta, other, travelled[0]))
    (own,) = attend(meta, *parts, False, (0,))
    pieces = [own.reshape(count, SPAN), swap(other.reshape(count, SPAN), TEAM, 1), *travelled]
    return collect(member.astype(jnp.int32), pieces).reshape(frames, rows, width, model)


def solution(mesh):
    split = Mesh(
        mesh.devices.reshape(mesh.shape["tm"] // MATES, MATES // CORES, CORES, mesh.shape["height"]),
        ("rest", "pair", "core", "height"),
    )
    along = ("rest", "pair", "core")
    in_specs = (
        P(along, "height", None, None),
        P(),
        P(),
        P((*along, "height"), None),
        P(),
        P(),
        P(),
        P(),
    )
    out_specs = P(along, "height", None, None)
    return jax.shard_map(
        per_device, mesh=split, in_specs=in_specs, out_specs=out_specs, check_vma=False
    )
```
